128 devices in a mesh: brick: 32 (over y, x, core), pool: 4 (over z).
Axes of the slice: x: 4, y: 4, z: 4, core: 2. Of those that a mesh axis runs over, the one named last changes fastest.
Arguments:
- displacement: float32 [3, 1179648], P(None, ('brick', 'pool')), may hold values from -6 to 6
- node_map: int32 [8, 1048576], P(None, ('brick', 'pool')), may hold values from 0 to 9215
- shape_grads: float32 [3, 8, 1048576], P(None, None, ('brick', 'pool')), may hold values from -2 to 2
- volumes: float32 [1048576], P(('brick', 'pool')), may hold values from 0.5 to 2
- elastic_moduli: float32 [2, 1048576], P(None, ('brick', 'pool')), may hold values from 1 to 10
- external_force: float32 [3, 1179648], P(None, ('brick', 'pool')), may hold values from -64 to 64
- nodal_mass: float32 [1179648], P(('brick', 'pool')), may hold values from 10 to 40
- shared_nodes: int32 [128, 4, 1024], P(('brick', 'pool')), may hold values from 0 to 9215, as said below
- band_count: int32 [128], P(('brick', 'pool')), may hold values from 1 to 4, as said below
- band_owner: int32 [128, 4], P(('brick', 'pool')), may hold values from -1 to 127, as said below
- band_element: int32 [128, 4], P(('brick', 'pool')), may hold values from 0 to 8191, as said below
- micro_fields: float32 [512, 8, 4096], P(('brick', 'pool')), may hold values from -5 to 10, as said below
Outputs:
- acceleration: float32 [3, 1179648], P(None, ('brick', 'pool'))
- band_stress: float32 [6, 512], P(None, ('brick', 'pool'))
- owned_fields: float32 [256, 8, 4096], P(('brick', 'pool'))
The draws below stay inside these ranges and needn't reach their ends.
Inputs may be any that keep to these rules, and one draw needn't show every extreme that they name: `band_count`: they sum to 256. `band_owner`: -1 exactly on slots k >= band_count[d]. The live slots of all blocks, block by block in order, take consecutive ordinals m = t, t + 1, ... for some start t; the slot with ordinal m is owned by device pi((m // 4) % 32) * 4 + m % 4 for a permutation pi of the brick indices. So every device owns exactly 2 live slots and no two live slots of one block share an owner. `band_element`: the entries of one block's row are different. `shared_nodes`: the 4096 entries of one block are different. `micro_fields`: channels 6 and 7 lie between 1 and 10, channels 0 to 5 between -5 and 5.
All inputs are finite; a program needn't handle non-finite values.
Results may differ from the reference program's by a relative error of at most 0.0001.
Values sent between devices are 32-bit elements; how exact they have to be, the bound alone decides.
No kernel may reach another device: no remote copies, remote signals or barrier semaphores. Data moves between devices by JAX's collectives and lax.ppermute only.
A program may use at most 192 MiB of HBM per device.

```python
import math
import jax
import jax.numpy as jnp
from jax import lax

E_DEV = 8192
NODES_DEV = 9216
FACE = 1024
P_DEV = 2
C_OLD = 4
G = 16
NV = 4096
ITERS = 2
NDEV = 128
N_BRICK = 32
N_POOL = 4


def band_layout(key):
    base_key = jax.random.fold_in(key, 17)
    key_order, key_shift, key_score, key_turn, key_perm = jax.random.split(base_key, 5)
    heavy_count = max(1, NDEV // 8)
    light_count = NDEV - heavy_count
    remain = NDEV * P_DEV - heavy_count * C_OLD
    share_each = remain // light_count
    extra_ones = remain - share_each * light_count
    position = jnp.arange(NDEV, dtype=jnp.int32)
    offset = position - heavy_count
    pair_moves = jax.random.randint(key_shift, (NDEV,), 0, share_each)
    moved_amount = pair_moves[jnp.maximum(offset, 0) // 2]
    has_partner = offset // 2 * 2 + 1 < light_count
    signed_move = jnp.where(offset % 2 == 0, moved_amount, -moved_amount)
    signed_move = jnp.where(has_partner, signed_move, 0)
    light_load = share_each + jnp.where(offset < extra_ones, 1, 0) + signed_move
    by_position = jnp.where(position < heavy_count, C_OLD, light_load).astype(jnp.int32)
    device_order = jax.random.permutation(key_order, NDEV)
    counts = jnp.zeros((NDEV,), jnp.int32).at[device_order].set(by_position)
    starts = jnp.cumsum(counts) - counts
    slot_index = jnp.arange(C_OLD, dtype=jnp.int32)
    alive = slot_index[None, :] < counts[:, None]
    scores = jax.random.randint(key_score, (NDEV, C_OLD), 0, 1 << 20) * C_OLD + slot_index[None, :]
    scores = jnp.where(alive, scores, (1 << 30) + slot_index[None, :])
    ranks = jnp.argsort(jnp.argsort(scores, axis=1), axis=1).astype(jnp.int32)
    turn_shift = jax.random.randint(key_turn, (), 0, NDEV)
    ordinal = starts[:, None] + ranks + turn_shift
    brick_order = jax.random.permutation(key_perm, N_BRICK).astype(jnp.int32)
    owner_brick = brick_order[ordinal // N_POOL % N_BRICK]
    owner_value = owner_brick * N_POOL + ordinal % N_POOL
    owners = jnp.where(alive, owner_value, -1)
    return (counts, owners.astype(jnp.int32))


def draw_band_count(key, part):
    return band_layout(key)[0]


def draw_band_owner(key, part):
    return band_layout(key)[1]


def draw_band_element(key, part):
    device_keys = jax.random.split(jax.random.fold_in(key, 5), NDEV)
    chosen = jax.vmap(lambda device_key: jax.random.permutation(device_key, E_DEV)[:C_OLD])(device_keys)
    return chosen.astype(jnp.int32)


def draw_shared_nodes(key, part):
    device_keys = jax.random.split(jax.random.fold_in(key, 9), NDEV)
    chosen = jax.vmap(lambda device_key: jax.random.permutation(device_key, NODES_DEV)[:4 * FACE])(device_keys)
    return chosen.reshape(NDEV, 4, FACE).astype(jnp.int32)


def draw_micro_fields(key, part):
    key_strain, key_moduli = jax.random.split(jax.random.fold_in(key, 29))
    row_total = NDEV * C_OLD
    strain = jnp.clip(jax.random.normal(key_strain, (row_total, 6, NV), jnp.float32), -5.0, 5.0)
    moduli = jnp.exp(jax.random.uniform(key_moduli, (row_total, 2, NV), jnp.float32, 0.0, math.log(10.0)))
    moduli = jnp.clip(moduli, 1.0, 10.0)
    return jnp.concatenate([strain, moduli], axis=1)


def place_ends(entries, own_key, low, largest):
    place = [jax.random.randint(jax.random.fold_in(own_key, axis), (), 0, length) for axis, length in enumerate(entries.shape)]
    longest = entries.shape.index(max(entries.shape))
    beside = place[:longest] + [(place[longest] + 1) % entries.shape[longest]] + place[longest + 1:]
    return entries.at[tuple(place)].set(low).at[tuple(beside)].set(largest)


def level_of(own_key, shape, pieces, smallest, high):
    level, own = 1.0, jax.random.fold_in(own_key, 6)
    for axis_at, shards_of in pieces:
        draws = jnp.exp(jax.random.uniform(jax.random.fold_in(own, axis_at), (shards_of,), jnp.float32, smallest / len(pieces), high / len(pieces)))
        level = level * jnp.repeat(draws, shape[axis_at] // shards_of).reshape([-1 if axis == axis_at else 1 for axis in range(len(shape))])
    return level


def scatter_about(own_key, shape, scale, limit, shards=(), kind=jnp.bfloat16):
    loudness = level_of(own_key, shape, shards, -0.22, 0.18) if shards else 1.0
    array = jax.random.normal(own_key, shape, jnp.float32) * scale * loudness
    return jnp.minimum(jnp.maximum(array, -limit), limit).astype(kind)


def setup_inputs(seed: int = 0) -> dict:
    arg_keys = jax.random.split(jax.random.key(seed), 13)
    displacement = scatter_about(arg_keys[0], (3, NDEV * NODES_DEV), 1.0, 6.0, ((1, 128),), jnp.float32)
    node_map = place_ends(jax.random.randint(arg_keys[1], (8, NDEV * E_DEV), 0, NODES_DEV), jax.random.fold_in(arg_keys[1], 1), 0, NODES_DEV - 1).astype(jnp.int32)
    shape_grads = scatter_about(arg_keys[2], (3, 8, NDEV * E_DEV), 8 ** -0.5, 2.0, ((2, 128),), jnp.float32)
    volumes = jnp.clip(jnp.exp(math.log(2.0) - 1.3862944 * jax.random.uniform(arg_keys[3], (NDEV * E_DEV,), jnp.float32) ** level_of(arg_keys[3], (NDEV * E_DEV,), ((0, 128),), -0.2, 0.2)), 0.5, 2.0)
    elastic_moduli = jnp.clip(jnp.exp(math.log(10.0) - 2.3025851 * jax.random.uniform(arg_keys[4], (2, NDEV * E_DEV), jnp.float32) ** level_of(arg_keys[4], (2, NDEV * E_DEV), ((1, 128),), -0.2, 0.2)), 1.0, 10.0)
    external_force = scatter_about(arg_keys[5], (3, NDEV * NODES_DEV), 10.0, 64.0, ((1, 128),), jnp.float32)
    nodal_mass = jnp.clip(jnp.exp(math.log(40.0) - 1.3862944 * jax.random.uniform(arg_keys[6], (NDEV * NODES_DEV,), jnp.float32) ** level_of(arg_keys[6], (NDEV * NODES_DEV,), ((0, 128),), -0.2, 0.2)), 10.0, 40.0)
    shared_nodes = draw_shared_nodes(jax.random.fold_in(arg_keys[12], 71), 0)
    band_count = draw_band_count(jax.random.fold_in(arg_keys[12], 71), 0)
    band_owner = draw_band_owner(jax.random.fold_in(arg_keys[12], 71), 0)
    band_element = draw_band_element(jax.random.fold_in(arg_keys[12], 71), 0)
    micro_fields = draw_micro_fields(jax.random.fold_in(arg_keys[12], 71), 0)
    return {"displacement": displacement, "node_map": node_map, "shape_grads": shape_grads, "volumes": volumes, "elastic_moduli": elastic_moduli, "external_force": external_force, "nodal_mass": nodal_mass, "shared_nodes": shared_nodes, "band_count": band_count, "band_owner": band_owner, "band_element": band_element, "micro_fields": micro_fields}


ref_lambda = 5.5
ref_shear = 5.5
highest = lax.Precision.HIGHEST


def wave_of(positions, length_cells):
    return jnp.where(positions * 2 < length_cells, positions, positions - length_cells).astype(jnp.float32)


def green_apply(tensor_parts, wave_x, wave_y, wave_z):
    tau_xx, tau_yy, tau_zz, tau_yz, tau_xz, tau_xy = tensor_parts
    along_x = tau_xx * wave_x + tau_xy * wave_y + tau_xz * wave_z
    along_y = tau_xy * wave_x + tau_yy * wave_y + tau_yz * wave_z
    along_z = tau_xz * wave_x + tau_yz * wave_y + tau_zz * wave_z
    squared = wave_x * wave_x + wave_y * wave_y + wave_z * wave_z
    nonzero = squared > 0.0
    safe_square = jnp.where(nonzero, squared, 1.0)
    first_term = jnp.where(nonzero, 1.0 / (2.0 * ref_shear * safe_square), 0.0)
    coupling = (ref_lambda + ref_shear) / (ref_shear * (ref_lambda + 2.0 * ref_shear))
    second = jnp.where(nonzero, coupling / (safe_square * safe_square), 0.0)
    normal_part = (along_x * wave_x + along_y * wave_y + along_z * wave_z) * second
    return [
        first_term * (2.0 * wave_x * along_x) - normal_part * wave_x * wave_x,
        first_term * (2.0 * wave_y * along_y) - normal_part * wave_y * wave_y,
        first_term * (2.0 * wave_z * along_z) - normal_part * wave_z * wave_z,
        first_term * (wave_y * along_z + wave_z * along_y) - normal_part * wave_y * wave_z,
        first_term * (wave_x * along_z + wave_z * along_x) - normal_part * wave_x * wave_z,
        first_term * (wave_x * along_y + wave_y * along_x) - normal_part * wave_x * wave_y,
    ]


def cell_stress(strain, lame_first, shear_mod):
    trace_sum = strain[:, 0] + strain[:, 1] + strain[:, 2]
    normal = [lame_first * trace_sum + 2.0 * shear_mod * strain[:, channel] for channel in range(3)]
    shears = [2.0 * shear_mod * strain[:, channel] for channel in range(3, 6)]
    return jnp.stack(normal + shears, axis=1)


def element_strain(displacement, node_map, shape_grads):
    corners = displacement[:, node_map]
    tensor = jnp.einsum("iae,jae->ije", corners, shape_grads, precision=highest)
    return jnp.stack([tensor[0, 0], tensor[1, 1], tensor[2, 2],
                      0.5 * (tensor[1, 2] + tensor[2, 1]),
                      0.5 * (tensor[0, 2] + tensor[2, 0]),
                      0.5 * (tensor[0, 1] + tensor[1, 0])], axis=0)


def macro_stress(strain, moduli):
    trace_sum = strain[0] + strain[1] + strain[2]
    normal = [moduli[0] * trace_sum + 2.0 * moduli[1] * strain[channel] for channel in range(3)]
    shears = [2.0 * moduli[1] * strain[channel] for channel in range(3, 6)]
    return jnp.stack(normal + shears, axis=0)


def element_forces(stress, shape_grads, volumes):
    full = jnp.stack([jnp.stack([stress[0], stress[5], stress[4]]),
                      jnp.stack([stress[5], stress[1], stress[3]]),
                      jnp.stack([stress[4], stress[3], stress[2]])])
    return jnp.einsum("ije,jae->iae", full, shape_grads, precision=highest) * volumes[None, None, :]


def cell_block(fields, macro):
    members = fields.shape[0]
    strain = fields[:, :6].reshape(members, 6, G, G, G)
    lame_first = fields[:, 6].reshape(members, G, G, G)
    shear_mod = fields[:, 7].reshape(members, G, G, G)
    waves = wave_of(jnp.arange(G, dtype=jnp.int32), G)
    wave_x = waves[:, None, None]
    wave_y = waves[None, :, None]
    wave_z = waves[None, None, :]
    target = macro[:, :, None, None, None]
    for iteration in range(ITERS):
        spectrum = jnp.fft.fftn(cell_stress(strain, lame_first, shear_mod), axes=(2, 3, 4))
        real_out = green_apply([spectrum.real[:, channel] for channel in range(6)], wave_x, wave_y, wave_z)
        imag_out = green_apply([spectrum.imag[:, channel] for channel in range(6)], wave_x, wave_y, wave_z)
        combined = lax.complex(jnp.stack(real_out, axis=1), jnp.stack(imag_out, axis=1))
        update = jnp.fft.ifftn(combined, axes=(2, 3, 4)).real
        average = jnp.mean(strain, axis=(2, 3, 4), keepdims=True)
        strain = strain - update + (target - average)
    final = cell_stress(strain, lame_first, shear_mod)
    homogenized = jnp.mean(final, axis=(2, 3, 4))
    return jnp.concatenate([strain.reshape(members, 6, NV), fields[:, 6:]], axis=1), homogenized


def reference(displacement, node_map, shape_grads, volumes, elastic_moduli, external_force, nodal_mass,
              shared_nodes, band_count, band_owner, band_element, micro_fields):
    moved = displacement.reshape(3, NDEV, NODES_DEV).transpose(1, 0, 2)
    corner_map = node_map.reshape(8, NDEV, E_DEV).transpose(1, 0, 2)
    gradients = shape_grads.reshape(3, 8, NDEV, E_DEV).transpose(2, 0, 1, 3)
    block_volumes = volumes.reshape(NDEV, E_DEV)
    moduli = elastic_moduli.reshape(2, NDEV, E_DEV).transpose(1, 0, 2)
    strain = jax.vmap(element_strain)(moved, corner_map, gradients)
    slot_index = jnp.arange(C_OLD, dtype=jnp.int32)
    device_index = jnp.arange(NDEV, dtype=jnp.int32)
    live = slot_index[None, :] < band_count[:, None]
    band_strain = jax.vmap(lambda values, picks: values[:, picks].T)(strain, band_element)
    sends = jnp.sum(((band_owner[:, :, None] == device_index[None, None, :]) & live[:, :, None]).astype(jnp.int32), axis=1)
    ranks = jnp.cumsum(sends, axis=0) - sends
    safe_owner = jnp.where(live, band_owner, 0).astype(jnp.int32)
    new_slot = safe_owner * P_DEV + jnp.take_along_axis(ranks, safe_owner, axis=1)
    flat_slot = (device_index[:, None] * C_OLD + slot_index[None, :]).astype(jnp.int32)
    total_cells = NDEV * P_DEV
    target = jnp.where(live, new_slot, total_cells).astype(jnp.int32).reshape(-1)
    sources = jnp.zeros((total_cells,), jnp.int32).at[target].set(flat_slot.reshape(-1), mode="drop")
    strain_rows = band_strain.reshape(NDEV * C_OLD, 6)

    def run_owner(picks):
        return cell_block(micro_fields[picks], strain_rows[picks])

    owned, homogenized = lax.map(run_owner, sources.reshape(NDEV, P_DEV))
    owned_fields = owned.reshape(total_cells, 8, NV)
    stress_rows = jnp.zeros((NDEV * C_OLD, 6), jnp.float32).at[sources].set(homogenized.reshape(total_cells, 6))
    band_stress = stress_rows.T
    replace_rows = stress_rows.reshape(NDEV, C_OLD, 6)

    def device_force(strain_block, moduli_block, picks, alive, replace, grads_block, volume_block, map_block):
        stress = macro_stress(strain_block, moduli_block)
        stress = stress.at[:, jnp.where(alive, picks, E_DEV)].set(replace.T, mode="drop")
        forces = element_forces(stress, grads_block, volume_block)
        return jnp.zeros((3, NODES_DEV), jnp.float32).at[:, map_block].add(forces)

    own_force = jax.vmap(device_force)(strain, moduli, band_element, live, replace_rows, gradients, block_volumes, corner_map)
    picked = jax.vmap(lambda force_block, face_block: force_block[:, face_block])(own_force, shared_nodes)
    grid = picked.reshape(N_BRICK, N_POOL, 3, 4, FACE)
    empty_brick = jnp.zeros_like(grid[:1])
    from_lower_brick = jnp.concatenate([empty_brick, grid[:-1]], axis=0)[:, :, :, 1]
    from_upper_brick = jnp.concatenate([grid[1:], empty_brick], axis=0)[:, :, :, 0]
    empty_pool = jnp.zeros_like(grid[:, :1])
    from_lower_pool = jnp.concatenate([empty_pool, grid[:, :-1]], axis=1)[:, :, :, 3]
    from_upper_pool = jnp.concatenate([grid[:, 1:], empty_pool], axis=1)[:, :, :, 2]
    incoming = jnp.stack([from_lower_brick, from_upper_brick, from_lower_pool, from_upper_pool], axis=3)
    incoming = incoming.reshape(NDEV, 3, 4, FACE)

    def add_faces(force_block, face_block, arriving):
        result = force_block.at[:, face_block[0]].add(arriving[:, 0])
        result = result.at[:, face_block[1]].add(arriving[:, 1])
        result = result.at[:, face_block[2]].add(arriving[:, 2])
        return result.at[:, face_block[3]].add(arriving[:, 3])

    assembled = jax.vmap(add_faces)(own_force, shared_nodes, incoming)
    forces_flat = assembled.transpose(1, 0, 2).reshape(3, NDEV * NODES_DEV)
    acceleration = (external_force - forces_flat) / nodal_mass[None, :]
    return acceleration, band_stress, owned_fields
```

```python
import math

import jax
import jax.numpy as jnp
import numpy as np
from jax import lax
from jax.experimental import pallas as pl
from jax.experimental.pallas import tpu as pltpu
from jax.sharding import PartitionSpec as P

G = 16
NV = 4096
ITERS = 2
LANES = 128
TILES = 32
HI = 40
LO = 256
VMEM = pltpu.VMEM
SMEM = pltpu.SMEM
f32 = jnp.float32
bf16 = jnp.bfloat16

ref_lambda = 5.5
ref_shear = 5.5


def green_table():
    index = np.arange(G)

    def operator(ix, iy, iz):
        wave = [np.where(2 * m < G, m, m - G).astype(np.float64) for m in (ix, iy, iz)]
        kx, ky, kz = np.broadcast_arrays(wave[0], wave[1], wave[2])
        square = kx * kx + ky * ky + kz * kz
        safe = np.where(square > 0, square, 1.0)
        first = np.where(square > 0, 1.0 / (2.0 * ref_shear * safe), 0.0)
        factor = (ref_lambda + ref_shear) / (ref_shear * (ref_lambda + 2.0 * ref_shear))
        second = np.where(square > 0, factor / (safe * safe), 0.0)
        zero, one = np.zeros_like(kx), np.ones_like(kx)
        columns = []
        for j in range(6):
            xx, yy, zz, yz, xz, xy = [one if j == c else zero for c in range(6)]
            wx = xx * kx + xy * ky + xz * kz
            wy = xy * kx + yy * ky + yz * kz
            wz = xz * kx + yz * ky + zz * kz
            s = (wx * kx + wy * ky + wz * kz) * second
            columns.append(
                np.stack(
                    [
                        first * 2 * kx * wx - s * kx * kx,
                        first * 2 * ky * wy - s * ky * ky,
                        first * 2 * kz * wz - s * kz * kz,
                        first * (ky * wz + kz * wy) - s * ky * kz,
                        first * (kx * wz + kz * wx) - s * kx * kz,
                        first * (kx * wy + ky * wx) - s * kx * ky,
                        zero,
                        zero,
                    ]
                )
            )
        return np.stack(columns)

    ix, iy, iz = index[:, None, None], index[None, :, None], index[None, None, :]
    table = 0.5 * (operator(ix, iy, iz) + operator((-ix) % G, (-iy) % G, (-iz) % G)) / NV
    return table.reshape(6, 8, G, G * G).transpose(2, 0, 1, 3).astype(np.float32)


def plane_tables():
    plane = np.arange(G * G)
    phase = (plane[:, None] // G * (plane[None, :] // G) + plane[:, None] % G * (plane[None, :] % G)) % G
    parts = []
    for table in (np.cos(phase * (2 * np.pi / G)), np.sin(phase * (2 * np.pi / G))):
        table = table.astype(np.float32)
        high = table.astype(bf16)
        parts += [high, (table - high.astype(np.float32)).astype(bf16)]
    return np.stack(parts)


def twiddle(value, power, sign):
    re, im = value
    power %= 16
    if power == 0:
        return re, im
    if power == 4:
        return (-im, re) if sign > 0 else (im, -re)
    if power == 8:
        return -re, -im
    if power == 12:
        return (im, -re) if sign > 0 else (-im, re)
    angle = sign * 2 * math.pi * power / 16
    c, s = math.cos(angle), math.sin(angle)
    if power % 4 == 2:
        h = abs(c)
        a = re if c > 0 else -re
        b = im if c > 0 else -im
        if c * s > 0:
            return (a - b) * h, (a + b) * h
        return (a + b) * h, (b - a) * h
    return re * c - im * s, re * s + im * c


def dft4(v, sign):
    (ar, ai), (br, bi), (cr, ci), (dr, di) = v
    pr, pi_ = ar + cr, ai + ci
    mr, mi = ar - cr, ai - ci
    qr, qi = br + dr, bi + di
    nr, ni = br - dr, bi - di
    if sign < 0:
        jr, ji = ni, -nr
    else:
        jr, ji = -ni, nr
    return [(pr + qr, pi_ + qi), (mr + jr, mi + ji), (pr - qr, pi_ - qi), (mr - jr, mi - ji)]


def dft16(values, sign):
    inner = []
    for n2 in range(4):
        inner.append(dft4([values[n2 + 4 * n1] for n1 in range(4)], sign))
    out = [None] * 16
    for k1 in range(4):
        column = dft4([twiddle(inner[n2][k1], n2 * k1, sign) for n2 in range(4)], sign)
        for k2 in range(4):
            out[k1 + 4 * k2] = column[k2]
    return out


def slab_stress(d, first_rows):
    wide = d.shape
    trace = d[0:1] + d[1:2] + d[2:3]
    lam_trace = jnp.broadcast_to(d[6:7] * trace, wide)
    twice = jnp.broadcast_to(2.0 * d[7:8], wide)
    return twice * d + jnp.where(first_rows, lam_trace, 0.0)


def plane_products(sr, si, cmat):
    x = jnp.concatenate([sr[...], si[...]], axis=0)
    high = x.astype(bf16)
    low = (x - high.astype(f32)).astype(bf16)

    def times(at):
        a, b = cmat[at], cmat[at + 1]
        return (
            jnp.dot(high, a, preferred_element_type=f32)
            + jnp.dot(low, a, preferred_element_type=f32)
            + jnp.dot(high, b, preferred_element_type=f32)
        )

    return times(0), times(2)


def cells_kernel(
    count, owner, element, disp, nm, grads, micro, green, cmat, send, band_stress, st, sr, si
):
    half_rows = 8 * G
    lane = lax.broadcasted_iota(jnp.int32, (8, LANES), 1)
    row = lax.broadcasted_iota(jnp.int32, (8, LANES), 0)
    row_wide = lax.broadcasted_iota(jnp.int32, (8, 2 * LANES), 0)
    first_rows = row_wide < 3

    targets = []
    for k in range(4):
        e = element[0, k]
        base = pl.multiple_of(e // LANES * LANES, LANES)
        at = lane == e % LANES

        def pick(tile):
            return jnp.sum(jnp.where(at, tile, 0.0), axis=1, keepdims=True)

        node = pick(nm[:, pl.ds(base, LANES)].astype(f32)).astype(jnp.int32)
        shape = [jnp.broadcast_to(pick(grads[j, :, pl.ds(base, LANES)]), (8, LANES)) for j in range(3)]
        node = jnp.broadcast_to(node, (8, LANES)) - lane
        found = [jnp.zeros((8, LANES), f32) for _ in range(3)]
        for r in range(72):
            hit = node == r * LANES
            for c in range(3):
                values = jnp.broadcast_to(disp[c : c + 1, r * LANES : (r + 1) * LANES], (8, LANES))
                found[c] = jnp.where(hit, values, found[c])
        u = [jnp.sum(found[c], axis=1, keepdims=True) for c in range(3)]

        def total(value):
            return jnp.sum(value, axis=0, keepdims=True)

        parts = [
            total(u[0] * shape[0]),
            total(u[1] * shape[1]),
            total(u[2] * shape[2]),
            0.5 * total(u[1] * shape[2] + u[2] * shape[1]),
            0.5 * total(u[0] * shape[2] + u[2] * shape[0]),
            0.5 * total(u[0] * shape[1] + u[1] * shape[0]),
        ]
        target = jnp.zeros((8, LANES), f32)
        for c in range(6):
            target = jnp.where(row == c, jnp.broadcast_to(parts[c], (8, LANES)), target)
        targets.append(target)

    def slab(k, x, iteration):
        if iteration == 0:
            return micro[k, :, 2 * LANES * x : 2 * LANES * (x + 1)]
        return st[k, 8 * x : 8 * x + 8, :]

    shifts = []
    for k in range(4):
        total = jnp.zeros((8, 2 * LANES), f32)
        for x in range(G):
            total = total + slab(k, x, 0)
        mean = jnp.sum(total, axis=1, keepdims=True) * (1.0 / NV)
        shift = jnp.where(row < 6, targets[k] - mean, 0.0)
        shifts.append(jnp.concatenate([shift, shift], axis=1))

    for iteration in range(ITERS):
        for pair in range(2):
            for x in range(G):
                at = pair * half_rows + 8 * x
                sr[at : at + 8, :] = slab_stress(slab(2 * pair, x, iteration), first_rows)
                si[at : at + 8, :] = slab_stress(slab(2 * pair + 1, x, iteration), first_rows)
        by_cos, by_sin = plane_products(sr, si, cmat)
        rows = 2 * half_rows
        sr[...] = by_cos[:rows] + by_sin[rows:]
        si[...] = by_cos[rows:] - by_sin[:rows]
        for pair in range(2):
            for part in range(2):
                cols = slice(part * LANES, (part + 1) * LANES)
                at = [pair * half_rows + 8 * x for x in range(G)]
                values = dft16([(sr[a : a + 8, cols], si[a : a + 8, cols]) for a in at], -1)
                for x in range(G):
                    sr[at[x] : at[x] + 8, cols] = values[x][0]
                    si[at[x] : at[x] + 8, cols] = values[x][1]
                updates = []
                for x in range(G):
                    re = im = None
                    for j in range(6):
                        weight = green[x, j, :, cols]
                        tr = weight * jnp.broadcast_to(sr[at[x] + j : at[x] + j + 1, cols], (8, LANES))
                        ti = weight * jnp.broadcast_to(si[at[x] + j : at[x] + j + 1, cols], (8, LANES))
                        re = tr if re is None else re + tr
                        im = ti if im is None else im + ti
                    updates.append((re, im))
                values = dft16(updates, 1)
                for x in range(G):
                    sr[at[x] : at[x] + 8, cols] = values[x][0]
                    si[at[x] : at[x] + 8, cols] = values[x][1]
        by_cos, by_sin = plane_products(sr, si, cmat)
        sr[...] = by_cos[:rows] - by_sin[rows:]
        si[...] = by_cos[rows:] + by_sin[:rows]
        for k in range(4):
            source = (sr, si)[k % 2]
            for x in range(G):
                at = k // 2 * half_rows + 8 * x
                value = slab(k, x, iteration) - source[at : at + 8, :]
                if iteration == 0:
                    value = value + shifts[k]
                st[k, 8 * x : 8 * x + 8, :] = value

    result = jnp.zeros((8, LANES), f32)
    for k in range(4):
        live = k < count[0]
        total = jnp.zeros((8, 2 * LANES), f32)
        for x in range(G):
            total = total + slab_stress(st[k, 8 * x : 8 * x + 8, :], first_rows)
        mean = jnp.sum(total, axis=1, keepdims=True) * (1.0 / NV)
        result = jnp.where((lane == k) & live, jnp.broadcast_to(mean, (8, LANES)), result)
        pool = owner[0, k] & 3

        @pl.when(live)
        def _():
            for i in range(TILES):
                x, part = i // 2, i % 2
                send[i * 4 + pool] = st[k, 8 * x : 8 * x + 8, part * LANES : (part + 1) * LANES]

    band_stress[...] = result[0:6, 0:4]


def solve_cells(count, owner, element, disp, nm, grads, micro, green, cmat):
    rows = 16 * G
    return pl.pallas_call(
        cells_kernel,
        out_shape=(
            jax.ShapeDtypeStruct((4 * TILES, 8, LANES), f32),
            jax.ShapeDtypeStruct((6, 4), f32),
        ),
        in_specs=[pl.BlockSpec(memory_space=SMEM)] * 3 + [pl.BlockSpec(memory_space=VMEM)] * 6,
        out_specs=(pl.BlockSpec(memory_space=VMEM), pl.BlockSpec(memory_space=VMEM)),
        scratch_shapes=[
            VMEM((4, 8 * G, 2 * LANES), f32),
            VMEM((rows, 2 * LANES), f32),
            VMEM((rows, 2 * LANES), f32),
        ],
        compiler_params=pltpu.CompilerParams(vmem_limit_bytes=32 << 20),
        name="cells",
    )(count, owner, element, disp, nm, grads, micro, green, cmat)


def one_hot_sum(node, values, width):
    hi = jnp.broadcast_to(node >> 8, (HI, width))
    lo = jnp.broadcast_to(node & 255, (LO, width))
    coarse = lax.broadcasted_iota(jnp.int32, (HI, width), 0) == hi
    fine = lax.broadcasted_iota(jnp.int32, (LO, width), 0) == lo
    left = jnp.concatenate(
        [jnp.where(coarse, jnp.broadcast_to(v, (HI, width)), 0.0) for v in values], axis=0
    ).astype(bf16)
    right = jnp.where(fine, 1.0, 0.0).astype(bf16)
    return left, right


def halves(value):
    high = value.astype(bf16).astype(f32)
    return high, value - high


def macro_kernel(count, element, replace, disp, nm, grads, volumes, moduli, shared, own, f0, f1, f2, f3, sums):
    sums[...] = jnp.zeros_like(sums)
    lane = lax.broadcasted_iota(jnp.int32, (1, LANES), 1)
    live = [k < count[0] for k in range(4)]

    def scatter(node, forces):
        values = []
        for force in forces:
            values += list(halves(force))
        total = None
        for s in range(0, 8, 2):
            lefts, rights = [], []
            for q in (s, s + 1):
                left, right = one_hot_sum(node[q : q + 1], [v[q : q + 1] for v in values], LANES)
                lefts.append(left)
                rights.append(right)
            product = lax.dot_general(
                jnp.concatenate(lefts, axis=1),
                jnp.concatenate(rights, axis=1),
                (((1,), (1,)), ((), ())),
                preferred_element_type=f32,
            )
            total = product if total is None else total + product
        sums[...] += total

    def body(step, carry):
        scatter(carry[0], carry[1:])
        t = jnp.minimum(step, 63)
        cols = pl.ds(pl.multiple_of(t * LANES, LANES), LANES)
        node = nm[:, cols]
        hi, lo = node >> 7, node & 127
        u = [jnp.zeros((8, LANES), f32) for _ in range(3)]
        for r in range(72):
            hit = hi == r
            for c in range(3):
                values = jnp.broadcast_to(disp[c : c + 1, r * LANES : (r + 1) * LANES], (8, LANES))
                found = jnp.take_along_axis(values, lo, axis=1, mode="promise_in_bounds")
                u[c] = jnp.where(hit, found, u[c])
        g = [grads[j, :, cols] for j in range(3)]

        def total(value):
            return jnp.sum(value, axis=0, keepdims=True)

        strain = [
            total(u[0] * g[0]),
            total(u[1] * g[1]),
            total(u[2] * g[2]),
            0.5 * total(u[1] * g[2] + u[2] * g[1]),
            0.5 * total(u[0] * g[2] + u[2] * g[0]),
            0.5 * total(u[0] * g[1] + u[1] * g[0]),
        ]
        lam = moduli[0:1, cols]
        mu = moduli[1:2, cols]
        volume = volumes[pl.ds(t, 1), :]
        spherical = lam * (strain[0] + strain[1] + strain[2])
        stress = [spherical + 2.0 * mu * strain[c] for c in range(3)]
        stress += [2.0 * mu * strain[c] for c in range(3, 6)]
        for k in range(4):
            hit = (lane + t * LANES == element[0, k]) & live[k]
            stress = [jnp.where(hit, replace[c, k], stress[c]) for c in range(6)]
        xx, yy, zz, yz, xz, xy = [
            jnp.broadcast_to(component * volume, (8, LANES)) for component in stress
        ]
        fx = xx * g[0] + xy * g[1] + xz * g[2]
        fy = xy * g[0] + yy * g[1] + yz * g[2]
        fz = xz * g[0] + yz * g[1] + zz * g[2]
        return node, fx, fy, fz

    zero = jnp.zeros((8, LANES), f32)
    lax.fori_loop(0, 65, body, (jnp.zeros((8, LANES), jnp.int32), zero, zero, zero))

    for c in range(3):
        at = 2 * c * HI
        own[c * HI : (c + 1) * HI, :] = sums[at : at + HI, :] + sums[at + HI : at + 2 * HI, :]

    faces = (f0, f1, f2, f3)
    for pair in range(4):
        first, second = 2 * pair, 2 * pair + 1
        node = jnp.concatenate(
            [
                shared[0, :, first * LANES : (first + 1) * LANES],
                shared[0, :, second * LANES : (second + 1) * LANES],
            ],
            axis=0,
        )
        hi, lo = node >> 7, node & 127
        picked = [jnp.zeros((8, LANES), f32) for _ in range(3)]
        for r in range(72):
            hit = hi == r
            for c in range(3):
                at = c * HI + r // 2
                cols = slice(r % 2 * LANES, (r % 2 + 1) * LANES)
                values = jnp.broadcast_to(own[at : at + 1, cols], (8, LANES))
                found = jnp.take_along_axis(values, lo, axis=1, mode="promise_in_bounds")
                picked[c] = jnp.where(hit, found, picked[c])
        for c in range(3):
            for face in range(4):
                faces[face][c : c + 1, first * LANES : (first + 1) * LANES] = picked[c][face : face + 1]
                faces[face][c : c + 1, second * LANES : (second + 1) * LANES] = picked[c][
                    4 + face : 5 + face
                ]


def macro_forces(count, element, replace, disp, nm, grads, volumes, moduli, shared):
    vmem = pl.BlockSpec(memory_space=VMEM)
    return pl.pallas_call(
        macro_kernel,
        out_shape=(jax.ShapeDtypeStruct((3 * HI, LO), f32),)
        + (jax.ShapeDtypeStruct((3, 1024), f32),) * 4,
        in_specs=[pl.BlockSpec(memory_space=SMEM)] * 3 + [vmem] * 6,
        out_specs=(vmem,) * 5,
        scratch_shapes=[VMEM((6 * HI, LO), f32)],
        compiler_params=pltpu.CompilerParams(vmem_limit_bytes=32 << 20),
        name="macro",
    )(count, element, replace, disp, nm, grads, volumes, moduli, shared)


def assemble_kernel(own, shared, r0, r1, r2, r3, external, mass, out):
    total = None
    for face, arrived in enumerate((r0, r1, r2, r3)):
        for part in range(4):
            cols = slice(part * LO, (part + 1) * LO)
            values = []
            for c in range(3):
                values += list(halves(arrived[c : c + 1, cols]))
            left, right = one_hot_sum(shared[0, face : face + 1, cols], values, LO)
            product = lax.dot_general(
                left, right, (((1,), (1,)), ((), ())), preferred_element_type=f32
            )
            total = product if total is None else total + product
    for c in range(3):
        at = 2 * c * HI
        whole = own[c * HI : (c + 1) * HI, :] + total[at : at + HI] + total[at + HI : at + 2 * HI]
        for r in range(36):
            out[c : c + 1, r * LO : (r + 1) * LO] = whole[r : r + 1]
    out[...] = (external[...] - out[...]) / mass[...]


def assemble(own, shared, arrived, external, mass):
    vmem = pl.BlockSpec(memory_space=VMEM)
    return pl.pallas_call(
        assemble_kernel,
        out_shape=jax.ShapeDtypeStruct(external.shape, f32),
        in_specs=[vmem] * 8,
        out_specs=vmem,
        compiler_params=pltpu.CompilerParams(vmem_limit_bytes=32 << 20),
        name="assemble",
    )(own, shared, *arrived, external, mass)


def sort_kernel(pool, owners, pieces, out, order, places, sem):
    blocks = owners.shape[0]
    lane = lax.broadcasted_iota(jnp.int32, (blocks, LANES), 1)
    block = lax.broadcasted_iota(jnp.int32, (blocks, LANES), 0)
    wanted = lane * 4 + pool[0]
    hit = jnp.zeros((blocks, LANES), jnp.bool_)
    for k in range(4):
        hit = hit | (jnp.broadcast_to(owners[:, k : k + 1], (blocks, LANES)) == wanted)
    first = jnp.min(jnp.where(hit, block, blocks - 1), axis=0, keepdims=True)
    last = jnp.max(jnp.where(hit, block, 0), axis=0, keepdims=True)
    order[0:1, :] = first
    order[1:2, :] = last
    copy = pltpu.make_async_copy(order, places, sem)
    copy.start()
    copy.wait()
    for b in range(out.shape[0]):
        for s in range(2):
            out[b, s] = pieces[places[s, b]]


def sort_pieces(pool, owners, pieces, bricks):
    vmem = pl.BlockSpec(memory_space=VMEM)
    return pl.pallas_call(
        sort_kernel,
        out_shape=jax.ShapeDtypeStruct((bricks, 2, 8, LANES), f32),
        in_specs=[pl.BlockSpec(memory_space=SMEM), vmem, vmem],
        out_specs=vmem,
        scratch_shapes=[VMEM((8, LANES), jnp.int32), SMEM((8, LANES), jnp.int32), pltpu.SemaphoreType.DMA],
        compiler_params=pltpu.CompilerParams(vmem_limit_bytes=32 << 20),
        name="sort_pieces",
    )(pool, owners, pieces)


def join_kernel(pieces, out):
    for i in range(TILES):
        for s in range(2):
            out[s, :, i * LANES : (i + 1) * LANES] = pieces[i, s]


def join_pieces(pieces):
    vmem = pl.BlockSpec(memory_space=VMEM)
    return pl.pallas_call(
        join_kernel,
        out_shape=jax.ShapeDtypeStruct((2, 8, NV), f32),
        in_specs=[vmem],
        out_specs=vmem,
        name="join_pieces",
    )(pieces)


def shards(
    displacement,
    node_map,
    shape_grads,
    volumes,
    elastic_moduli,
    external_force,
    nodal_mass,
    shared_nodes,
    band_count,
    band_owner,
    band_element,
    micro_fields,
):
    both = ("brick", "pool")
    bricks, pools = lax.axis_size("brick"), lax.axis_size("pool")
    owners = lax.all_gather(band_owner, both, axis=0, tiled=True)
    send, band_stress = solve_cells(
        band_count,
        band_owner,
        band_element,
        displacement,
        node_map,
        shape_grads,
        micro_fields,
        jnp.asarray(green_table()),
        jnp.asarray(plane_tables()),
    )
    pieces = lax.all_to_all(send, both, split_axis=0, concat_axis=0, tiled=True)
    own, f0, f1, f2, f3 = macro_forces(
        band_count,
        band_element,
        band_stress,
        displacement,
        node_map,
        shape_grads,
        volumes.reshape(64, LANES),
        elastic_moduli,
        shared_nodes,
    )
    up_b = [(i, i + 1) for i in range(bricks - 1)]
    down_b = [(i + 1, i) for i in range(bricks - 1)]
    up_p = [(i, i + 1) for i in range(pools - 1)]
    down_p = [(i + 1, i) for i in range(pools - 1)]
    arrived = (
        lax.ppermute(f1, "brick", up_b),
        lax.ppermute(f0, "brick", down_b),
        lax.ppermute(f3, "pool", up_p),
        lax.ppermute(f2, "pool", down_p),
    )
    pool = lax.axis_index("pool").astype(jnp.int32).reshape(1)
    sorted_pieces = sort_pieces(pool, owners, pieces, bricks)
    mine = lax.all_to_all(sorted_pieces, "brick", split_axis=0, concat_axis=0, tiled=True)
    acceleration = assemble(own, shared_nodes, arrived, external_force, nodal_mass.reshape(1, -1))
    owned_fields = join_pieces(mine)
    return (acceleration, band_stress, owned_fields)


def solution(mesh):
    both = ("brick", "pool")
    placed = (
        P(None, both),
        P(None, both),
        P(None, None, both),
        P(both),
        P(None, both),
        P(None, both),
        P(both),
        P(both, None, None),
        P(both),
        P(both, None),
        P(both, None),
        P(both, None, None),
    )
    return jax.shard_map(
        shards,
        mesh=mesh,
        in_specs=placed,
        out_specs=(P(None, both), P(None, both), P(both, None, None)),
        check_vma=False,
    )
```

```python
import functools
import math

import jax
import jax.numpy as jnp
import numpy as np
from jax import lax
from jax.experimental import pallas as pl
from jax.experimental.pallas import tpu as pltpu
from jax.sharding import PartitionSpec as P

G = 16
NV = 4096
ITERS = 2
LANES = 128
TILES = 32
HI = 40
LO = 256
UNROLL = 2
SPLIT = 32
VMEM = pltpu.VMEM
SMEM = pltpu.SMEM
f32 = jnp.float32
bf16 = jnp.bfloat16

ref_lambda = 5.5
ref_shear = 5.5


def green_table():
    index = np.arange(G)

    def operator(ix, iy, iz):
        wave = [np.where(2 * m < G, m, m - G).astype(np.float64) for m in (ix, iy, iz)]
        kx, ky, kz = np.broadcast_arrays(wave[0], wave[1], wave[2])
        square = kx * kx + ky * ky + kz * kz
        safe = np.where(square > 0, square, 1.0)
        first = np.where(square > 0, 1.0 / (2.0 * ref_shear * safe), 0.0)
        factor = (ref_lambda + ref_shear) / (ref_shear * (ref_lambda + 2.0 * ref_shear))
        second = np.where(square > 0, factor / (safe * safe), 0.0)
        zero, one = np.zeros_like(kx), np.ones_like(kx)
        columns = []
        for j in range(6):
            xx, yy, zz, yz, xz, xy = [one if j == c else zero for c in range(6)]
            wx = xx * kx + xy * ky + xz * kz
            wy = xy * kx + yy * ky + yz * kz
            wz = xz * kx + yz * ky + zz * kz
            s = (wx * kx + wy * ky + wz * kz) * second
            columns.append(
                np.stack(
                    [
                        first * 2 * kx * wx - s * kx * kx,
                        first * 2 * ky * wy - s * ky * ky,
                        first * 2 * kz * wz - s * kz * kz,
                        first * (ky * wz + kz * wy) - s * ky * kz,
                        first * (kx * wz + kz * wx) - s * kx * kz,
                        first * (kx * wy + ky * wx) - s * kx * ky,
                        zero,
                        zero,
                    ]
                )
            )
        return np.stack(columns)

    ix, iy, iz = index[:, None, None], index[None, :, None], index[None, None, :]
    table = 0.5 * (operator(ix, iy, iz) + operator((-ix) % G, (-iy) % G, (-iz) % G)) / NV
    return table.reshape(6, 8, G, G * G).transpose(2, 0, 1, 3).astype(np.float32)


def plane_tables():
    plane = np.arange(G * G)
    phase = (plane[:, None] // G * (plane[None, :] // G) + plane[:, None] % G * (plane[None, :] % G)) % G
    parts = []
    for table in (np.cos(phase * (2 * np.pi / G)), np.sin(phase * (2 * np.pi / G))):
        table = table.astype(np.float32)
        high = table.astype(bf16)
        parts += [high, (table - high.astype(np.float32)).astype(bf16)]
    return np.stack(parts)


def twiddle(value, power, sign):
    re, im = value
    power %= 16
    if power == 0:
        return re, im
    if power == 4:
        return (-im, re) if sign > 0 else (im, -re)
    if power == 8:
        return -re, -im
    if power == 12:
        return (im, -re) if sign > 0 else (-im, re)
    angle = sign * 2 * math.pi * power / 16
    c, s = math.cos(angle), math.sin(angle)
    if power % 4 == 2:
        h = abs(c)
        a = re if c > 0 else -re
        b = im if c > 0 else -im
        if c * s > 0:
            return (a - b) * h, (a + b) * h
        return (a + b) * h, (b - a) * h
    return re * c - im * s, re * s + im * c


def dft4(v, sign):
    (ar, ai), (br, bi), (cr, ci), (dr, di) = v
    pr, pi_ = ar + cr, ai + ci
    mr, mi = ar - cr, ai - ci
    qr, qi = br + dr, bi + di
    nr, ni = br - dr, bi - di
    if sign < 0:
        jr, ji = ni, -nr
    else:
        jr, ji = -ni, nr
    return [(pr + qr, pi_ + qi), (mr + jr, mi + ji), (pr - qr, pi_ - qi), (mr - jr, mi - ji)]


def dft16(values, sign):
    inner = []
    for n2 in range(4):
        inner.append(dft4([values[n2 + 4 * n1] for n1 in range(4)], sign))
    out = [None] * 16
    for k1 in range(4):
        column = dft4([twiddle(inner[n2][k1], n2 * k1, sign) for n2 in range(4)], sign)
        for k2 in range(4):
            out[k1 + 4 * k2] = column[k2]
    return out


def slab_stress(d, first_rows):
    wide = d.shape
    trace = d[0:1] + d[1:2] + d[2:3]
    lam_trace = jnp.broadcast_to(d[6:7] * trace, wide)
    twice = jnp.broadcast_to(2.0 * d[7:8], wide)
    return twice * d + jnp.where(first_rows, lam_trace, 0.0)


def plane_products(sr, si, cmat):
    x = jnp.concatenate([sr[...], si[...]], axis=0)
    high = x.astype(bf16)
    low = (x - high.astype(f32)).astype(bf16)

    def times(at):
        a, b = cmat[at], cmat[at + 1]
        return (
            jnp.dot(high, a, preferred_element_type=f32)
            + jnp.dot(low, a, preferred_element_type=f32)
            + jnp.dot(high, b, preferred_element_type=f32)
        )

    return times(0), times(2)


def cells_kernel(
    count, owner, element, disp, nm, grads, micro, green, cmat, send, band_stress, st, sr, si
):
    half_rows = 8 * G
    lane = lax.broadcasted_iota(jnp.int32, (8, LANES), 1)
    row = lax.broadcasted_iota(jnp.int32, (8, LANES), 0)
    row_wide = lax.broadcasted_iota(jnp.int32, (8, 2 * LANES), 0)
    first_rows = row_wide < 3

    targets = []
    for k in range(4):
        e = element[0, k]
        base = pl.multiple_of(e // LANES * LANES, LANES)
        at = lane == e % LANES

        def pick(tile):
            return jnp.sum(jnp.where(at, tile, 0.0), axis=1, keepdims=True)

        node = pick(nm[:, pl.ds(base, LANES)].astype(f32)).astype(jnp.int32)
        shape = [jnp.broadcast_to(pick(grads[j, :, pl.ds(base, LANES)]), (8, LANES)) for j in range(3)]
        node = jnp.broadcast_to(node, (8, LANES)) - lane
        found = [jnp.zeros((8, LANES), f32) for _ in range(3)]
        for r in range(72):
            hit = node == r * LANES
            for c in range(3):
                values = jnp.broadcast_to(disp[c : c + 1, r * LANES : (r + 1) * LANES], (8, LANES))
                found[c] = jnp.where(hit, values, found[c])
        u = [jnp.sum(found[c], axis=1, keepdims=True) for c in range(3)]

        def total(value):
            return jnp.sum(value, axis=0, keepdims=True)

        parts = [
            total(u[0] * shape[0]),
            total(u[1] * shape[1]),
            total(u[2] * shape[2]),
            0.5 * total(u[1] * shape[2] + u[2] * shape[1]),
            0.5 * total(u[0] * shape[2] + u[2] * shape[0]),
            0.5 * total(u[0] * shape[1] + u[1] * shape[0]),
        ]
        target = jnp.zeros((8, LANES), f32)
        for c in range(6):
            target = jnp.where(row == c, jnp.broadcast_to(parts[c], (8, LANES)), target)
        targets.append(target)

    def slab(k, x, iteration):
        if iteration == 0:
            return micro[k, :, 2 * LANES * x : 2 * LANES * (x + 1)]
        return st[k, 8 * x : 8 * x + 8, :]

    shifts = []
    for k in range(4):
        total = jnp.zeros((8, 2 * LANES), f32)
        for x in range(G):
            total = total + slab(k, x, 0)
        mean = jnp.sum(total, axis=1, keepdims=True) * (1.0 / NV)
        shift = jnp.where(row < 6, targets[k] - mean, 0.0)
        shifts.append(jnp.concatenate([shift, shift], axis=1))

    for iteration in range(ITERS):
        for pair in range(2):
            for x in range(G):
                at = pair * half_rows + 8 * x
                sr[at : at + 8, :] = slab_stress(slab(2 * pair, x, iteration), first_rows)
                si[at : at + 8, :] = slab_stress(slab(2 * pair + 1, x, iteration), first_rows)
        by_cos, by_sin = plane_products(sr, si, cmat)
        rows = 2 * half_rows
        sr[...] = by_cos[:rows] + by_sin[rows:]
        si[...] = by_cos[rows:] - by_sin[:rows]
        for pair in range(2):
            for part in range(2):
                cols = slice(part * LANES, (part + 1) * LANES)
                at = [pair * half_rows + 8 * x for x in range(G)]
                values = dft16([(sr[a : a + 8, cols], si[a : a + 8, cols]) for a in at], -1)
                for x in range(G):
                    sr[at[x] : at[x] + 8, cols] = values[x][0]
                    si[at[x] : at[x] + 8, cols] = values[x][1]
                updates = []
                for x in range(G):
                    re = im = None
                    for j in range(6):
                        weight = green[x, j, :, cols]
                        tr = weight * jnp.broadcast_to(sr[at[x] + j : at[x] + j + 1, cols], (8, LANES))
                        ti = weight * jnp.broadcast_to(si[at[x] + j : at[x] + j + 1, cols], (8, LANES))
                        re = tr if re is None else re + tr
                        im = ti if im is None else im + ti
                    updates.append((re, im))
                values = dft16(updates, 1)
                for x in range(G):
                    sr[at[x] : at[x] + 8, cols] = values[x][0]
                    si[at[x] : at[x] + 8, cols] = values[x][1]
        by_cos, by_sin = plane_products(sr, si, cmat)
        sr[...] = by_cos[:rows] - by_sin[rows:]
        si[...] = by_cos[rows:] + by_sin[:rows]
        for k in range(4):
            source = (sr, si)[k % 2]
            for x in range(G):
                at = k // 2 * half_rows + 8 * x
                value = slab(k, x, iteration) - source[at : at + 8, :]
                if iteration == 0:
                    value = value + shifts[k]
                st[k, 8 * x : 8 * x + 8, :] = value

    send[pl.ds(8, 4 * TILES, stride=9), :] = jnp.full((4 * TILES, LANES), -1.0, f32)
    result = jnp.zeros((8, LANES), f32)
    for k in range(4):
        live = k < count[0]
        total = jnp.zeros((8, 2 * LANES), f32)
        for x in range(G):
            total = total + slab_stress(st[k, 8 * x : 8 * x + 8, :], first_rows)
        mean = jnp.sum(total, axis=1, keepdims=True) * (1.0 / NV)
        result = jnp.where((lane == k) & live, jnp.broadcast_to(mean, (8, LANES)), result)
        pool = owner[0, k] & 3

        @pl.when(live)
        def _():
            for i in range(TILES):
                x, part = i // 2, i % 2
                send[pl.ds(9 * (4 * i + pool), 8), :] = st[
                    k, 8 * x : 8 * x + 8, part * LANES : (part + 1) * LANES
                ]
            brick = (owner[0, k] >> 2).astype(f32)
            send[pl.ds(9 * pool + 8, TILES, stride=36), :] = jnp.full((TILES, LANES), brick, f32)

    band_stress[...] = result[0:6, 0:4]


def solve_cells(count, owner, element, disp, nm, grads, micro, green, cmat):
    rows = 16 * G
    return pl.pallas_call(
        cells_kernel,
        out_shape=(
            jax.ShapeDtypeStruct((36 * TILES, LANES), f32),
            jax.ShapeDtypeStruct((6, 4), f32),
        ),
        in_specs=[pl.BlockSpec(memory_space=SMEM)] * 3 + [pl.BlockSpec(memory_space=VMEM)] * 6,
        out_specs=(pl.BlockSpec(memory_space=VMEM), pl.BlockSpec(memory_space=VMEM)),
        scratch_shapes=[
            VMEM((4, 8 * G, 2 * LANES), f32),
            VMEM((rows, 2 * LANES), f32),
            VMEM((rows, 2 * LANES), f32),
        ],
        compiler_params=pltpu.CompilerParams(vmem_limit_bytes=56 << 20),
        name="cells",
    )(count, owner, element, disp, nm, grads, micro, green, cmat)


def one_hot_sum(node, values, width):
    hi = jnp.broadcast_to(node >> 8, (HI, width))
    lo = jnp.broadcast_to(node & 255, (LO, width))
    coarse = lax.broadcasted_iota(jnp.int32, (HI, width), 0) == hi
    fine = lax.broadcasted_iota(jnp.int32, (LO, width), 0) == lo
    left = jnp.concatenate(
        [jnp.where(coarse, jnp.broadcast_to(v, (HI, width)), 0.0) for v in values], axis=0
    ).astype(bf16)
    right = jnp.where(fine, 1.0, 0.0).astype(bf16)
    return left, right


def halves(value):
    high = value.astype(bf16).astype(f32)
    return high, value - high


def macro_tiles(begin, end, unroll, count, element, replace, disp, nm, grads, volumes, moduli, sums):
    lane = lax.broadcasted_iota(jnp.int32, (1, LANES), 1)
    live = [k < count[0] for k in range(4)]

    def scatter(node, forces):
        values = []
        for force in forces:
            values += list(halves(force))
        total = None
        for s in range(0, 8, 2):
            lefts, rights = [], []
            for q in (s, s + 1):
                left, right = one_hot_sum(node[q : q + 1], [v[q : q + 1] for v in values], LANES)
                lefts.append(left)
                rights.append(right)
            product = lax.dot_general(
                jnp.concatenate(lefts, axis=1),
                jnp.concatenate(rights, axis=1),
                (((1,), (1,)), ((), ())),
                preferred_element_type=f32,
            )
            total = product if total is None else total + product
        return total

    def forces_of(t):
        cols = pl.ds(pl.multiple_of(t * LANES, LANES), LANES)
        node = nm[:, cols]
        hi, lo = node >> 7, node & 127
        u = [jnp.zeros((8, LANES), f32) for _ in range(3)]
        for r in range(72):
            hit = hi == r
            for c in range(3):
                values = jnp.broadcast_to(disp[c : c + 1, r * LANES : (r + 1) * LANES], (8, LANES))
                found = jnp.take_along_axis(values, lo, axis=1, mode="promise_in_bounds")
                u[c] = jnp.where(hit, found, u[c])
        g = [grads[j, :, cols] for j in range(3)]

        def total(value):
            return jnp.sum(value, axis=0, keepdims=True)

        strain = [
            total(u[0] * g[0]),
            total(u[1] * g[1]),
            total(u[2] * g[2]),
            0.5 * total(u[1] * g[2] + u[2] * g[1]),
            0.5 * total(u[0] * g[2] + u[2] * g[0]),
            0.5 * total(u[0] * g[1] + u[1] * g[0]),
        ]
        lam = moduli[0:1, cols]
        mu = moduli[1:2, cols]
        volume = volumes[pl.ds(t, 1), :]
        spherical = lam * (strain[0] + strain[1] + strain[2])
        stress = [spherical + 2.0 * mu * strain[c] for c in range(3)]
        stress += [2.0 * mu * strain[c] for c in range(3, 6)]
        for k in range(4):
            hit = (lane + t * LANES == element[0, k]) & live[k]
            stress = [jnp.where(hit, replace[c, k], stress[c]) for c in range(6)]
        xx, yy, zz, yz, xz, xy = [
            jnp.broadcast_to(component * volume, (8, LANES)) for component in stress
        ]
        fx = xx * g[0] + xy * g[1] + xz * g[2]
        fy = xy * g[0] + yy * g[1] + yz * g[2]
        fz = xz * g[0] + yz * g[1] + zz * g[2]
        return node, fx, fy, fz

    def group(step):
        return tuple(forces_of(begin + step * unroll + i) for i in range(unroll))

    def add(carry):
        total = None
        for node, *forces in carry:
            part = scatter(node, forces)
            total = part if total is None else total + part
        sums[...] += total

    def body(step, carry):
        add(carry)
        return group(step)

    add(lax.fori_loop(1, (end - begin) // unroll, body, group(0)))


def macro_first_kernel(unroll, count, element, replace, disp, nm, grads, volumes, moduli, sums):
    sums[...] = jnp.zeros_like(sums)
    macro_tiles(0, SPLIT, unroll, count, element, replace, disp, nm, grads, volumes, moduli, sums)


def macro_last_kernel(
    unroll, count, element, replace, disp, nm, grads, volumes, moduli, so_far, shared, own, f0, f1, f2, f3, sums
):
    sums[...] = so_far[...]
    macro_tiles(SPLIT, 64, unroll, count, element, replace, disp, nm, grads, volumes, moduli, sums)

    for c in range(3):
        at = 2 * c * HI
        own[c * HI : (c + 1) * HI, :] = sums[at : at + HI, :] + sums[at + HI : at + 2 * HI, :]

    faces = (f0, f1, f2, f3)
    for pair in range(4):
        first, second = 2 * pair, 2 * pair + 1
        node = jnp.concatenate(
            [
                shared[0, :, first * LANES : (first + 1) * LANES],
                shared[0, :, second * LANES : (second + 1) * LANES],
            ],
            axis=0,
        )
        hi, lo = node >> 7, node & 127
        picked = [jnp.zeros((8, LANES), f32) for _ in range(3)]
        for r in range(72):
            hit = hi == r
            for c in range(3):
                at = c * HI + r // 2
                cols = slice(r % 2 * LANES, (r % 2 + 1) * LANES)
                values = jnp.broadcast_to(own[at : at + 1, cols], (8, LANES))
                found = jnp.take_along_axis(values, lo, axis=1, mode="promise_in_bounds")
                picked[c] = jnp.where(hit, found, picked[c])
        for c in range(3):
            for face in range(4):
                faces[face][c : c + 1, first * LANES : (first + 1) * LANES] = picked[c][face : face + 1]
                faces[face][c : c + 1, second * LANES : (second + 1) * LANES] = picked[c][
                    4 + face : 5 + face
                ]


def macro_first(*arguments):
    vmem = pl.BlockSpec(memory_space=VMEM)
    return pl.pallas_call(
        functools.partial(macro_first_kernel, UNROLL),
        out_shape=jax.ShapeDtypeStruct((6 * HI, LO), f32),
        in_specs=[pl.BlockSpec(memory_space=SMEM)] * 3 + [vmem] * 5,
        out_specs=vmem,
        compiler_params=pltpu.CompilerParams(vmem_limit_bytes=32 << 20),
        name="macro_first",
    )(*arguments)


def macro_last(*arguments):
    vmem = pl.BlockSpec(memory_space=VMEM)
    return pl.pallas_call(
        functools.partial(macro_last_kernel, UNROLL),
        out_shape=(jax.ShapeDtypeStruct((3 * HI, LO), f32),)
        + (jax.ShapeDtypeStruct((3, 1024), f32),) * 4,
        in_specs=[pl.BlockSpec(memory_space=SMEM)] * 3 + [vmem] * 7,
        out_specs=(vmem,) * 5,
        scratch_shapes=[VMEM((6 * HI, LO), f32)],
        compiler_params=pltpu.CompilerParams(vmem_limit_bytes=32 << 20),
        name="macro_last",
    )(*arguments)


def assemble_kernel(own, shared, r0, r1, r2, r3, external, mass, out):
    total = None
    for face, arrived in enumerate((r0, r1, r2, r3)):
        for part in range(4):
            cols = slice(part * LO, (part + 1) * LO)
            values = []
            for c in range(3):
                values += list(halves(arrived[c : c + 1, cols]))
            left, right = one_hot_sum(shared[0, face : face + 1, cols], values, LO)
            product = lax.dot_general(
                left, right, (((1,), (1,)), ((), ())), preferred_element_type=f32
            )
            total = product if total is None else total + product
    for c in range(3):
        at = 2 * c * HI
        whole = own[c * HI : (c + 1) * HI, :] + total[at : at + HI] + total[at + HI : at + 2 * HI]
        for r in range(36):
            out[c : c + 1, r * LO : (r + 1) * LO] = whole[r : r + 1]
    out[...] = (external[...] - out[...]) / mass[...]


def assemble(own, shared, arrived, external, mass):
    vmem = pl.BlockSpec(memory_space=VMEM)
    return pl.pallas_call(
        assemble_kernel,
        out_shape=jax.ShapeDtypeStruct(external.shape, f32),
        in_specs=[vmem] * 8,
        out_specs=vmem,
        compiler_params=pltpu.CompilerParams(vmem_limit_bytes=32 << 20),
        name="assemble",
    )(own, shared, *arrived, external, mass)


def sort_kernel(pieces, out, order, places, sem):
    blocks = pieces.shape[0] // 9
    lane = lax.broadcasted_iota(jnp.int32, (blocks, LANES), 1)
    block = lax.broadcasted_iota(jnp.int32, (blocks, LANES), 0)
    hit = pieces[pl.ds(8, blocks, stride=9), :] == lane.astype(f32)
    order[0:1, :] = jnp.min(jnp.where(hit, block, blocks - 1), axis=0, keepdims=True)
    order[1:2, :] = jnp.max(jnp.where(hit, block, 0), axis=0, keepdims=True)
    copy = pltpu.make_async_copy(order, places, sem)
    copy.start()
    copy.wait()
    for b in range(out.shape[0]):
        for s in range(2):
            out[b, s] = pieces[pl.ds(9 * places[s, b], 8), :]


def sort_pieces(pieces, bricks):
    vmem = pl.BlockSpec(memory_space=VMEM)
    return pl.pallas_call(
        sort_kernel,
        out_shape=jax.ShapeDtypeStruct((bricks, 2, 8, LANES), f32),
        in_specs=[vmem],
        out_specs=vmem,
        scratch_shapes=[VMEM((8, LANES), jnp.int32), SMEM((8, LANES), jnp.int32), pltpu.SemaphoreType.DMA],
        compiler_params=pltpu.CompilerParams(vmem_limit_bytes=32 << 20),
        name="sort_pieces",
    )(pieces)


def join_kernel(pieces, out):
    for i in range(TILES):
        for s in range(2):
            out[s, :, i * LANES : (i + 1) * LANES] = pieces[i, s]


def join_pieces(pieces):
    vmem = pl.BlockSpec(memory_space=VMEM)
    return pl.pallas_call(
        join_kernel,
        out_shape=jax.ShapeDtypeStruct((2, 8, NV), f32),
        in_specs=[vmem],
        out_specs=vmem,
        name="join_pieces",
    )(pieces)


def shards(
    displacement,
    node_map,
    shape_grads,
    volumes,
    elastic_moduli,
    external_force,
    nodal_mass,
    shared_nodes,
    band_count,
    band_owner,
    band_element,
    micro_fields,
):
    both = ("brick", "pool")
    bricks, pools = lax.axis_size("brick"), lax.axis_size("pool")
    send, band_stress = solve_cells(
        band_count,
        band_owner,
        band_element,
        displacement,
        node_map,
        shape_grads,
        micro_fields,
        jnp.asarray(green_table()),
        jnp.asarray(plane_tables()),
    )
    pieces = lax.all_to_all(
        send.reshape(bricks * pools, 1, 9 * LANES), both, split_axis=0, concat_axis=0, tiled=True
    )
    macro = (
        band_count,
        band_element,
        band_stress,
        displacement,
        node_map,
        shape_grads,
        volumes.reshape(64, LANES),
        elastic_moduli,
    )
    so_far = macro_first(*macro)
    pieces, so_far = lax.optimization_barrier((pieces, so_far))
    sorted_pieces = sort_pieces(pieces.reshape(9 * bricks * pools, LANES), bricks)
    mine = lax.all_to_all(sorted_pieces, "brick", split_axis=0, concat_axis=0, tiled=True)
    own, f0, f1, f2, f3 = macro_last(*macro, so_far, shared_nodes)
    up_b = [(i, i + 1) for i in range(bricks - 1)]
    down_b = [(i + 1, i) for i in range(bricks - 1)]
    up_p = [(i, i + 1) for i in range(pools - 1)]
    down_p = [(i + 1, i) for i in range(pools - 1)]
    arrived = (
        lax.ppermute(f1, "brick", up_b),
        lax.ppermute(f0, "brick", down_b),
        lax.ppermute(f3, "pool", up_p),
        lax.ppermute(f2, "pool", down_p),
    )
    acceleration = assemble(own, shared_nodes, arrived, external_force, nodal_mass.reshape(1, -1))
    owned_fields = join_pieces(mine)
    return (acceleration, band_stress, owned_fields)


def solution(mesh):
    both = ("brick", "pool")
    placed = (
        P(None, both),
        P(None, both),
        P(None, None, both),
        P(both),
        P(None, both),
        P(None, both),
        P(both),
        P(both, None, None),
        P(both),
        P(both, None),
        P(both, None),
        P(both, None, None),
    )
    return jax.shard_map(
        shards,
        mesh=mesh,
        in_specs=placed,
        out_specs=(P(None, both), P(None, both), P(both, None, None)),
        check_vma=False,
    )
```

```python
import functools
import math

import jax
import jax.numpy as jnp
import numpy as np
from jax import lax
from jax.experimental import pallas as pl
from jax.experimental.pallas import tpu as pltpu
from jax.sharding import PartitionSpec as P

G = 16
NV = 4096
ITERS = 2
LANES = 128
TILES = 32
HI = 40
LO = 256
UNROLL = 2
SPLIT = 40
BRICK = ("row", "pair", "core")
BOTH = BRICK + ("pool",)
VMEM = pltpu.VMEM
SMEM = pltpu.SMEM
f32 = jnp.float32
bf16 = jnp.bfloat16

ref_lambda = 5.5
ref_shear = 5.5


def green_table():
    index = np.arange(G)

    def operator(ix, iy, iz):
        wave = [np.where(2 * m < G, m, m - G).astype(np.float64) for m in (ix, iy, iz)]
        kx, ky, kz = np.broadcast_arrays(wave[0], wave[1], wave[2])
        square = kx * kx + ky * ky + kz * kz
        safe = np.where(square > 0, square, 1.0)
        first = np.where(square > 0, 1.0 / (2.0 * ref_shear * safe), 0.0)
        factor = (ref_lambda + ref_shear) / (ref_shear * (ref_lambda + 2.0 * ref_shear))
        second = np.where(square > 0, factor / (safe * safe), 0.0)
        zero, one = np.zeros_like(kx), np.ones_like(kx)
        columns = []
        for j in range(6):
            xx, yy, zz, yz, xz, xy = [one if j == c else zero for c in range(6)]
            wx = xx * kx + xy * ky + xz * kz
            wy = xy * kx + yy * ky + yz * kz
            wz = xz * kx + yz * ky + zz * kz
            s = (wx * kx + wy * ky + wz * kz) * second
            columns.append(
                np.stack(
                    [
                        first * 2 * kx * wx - s * kx * kx,
                        first * 2 * ky * wy - s * ky * ky,
                        first * 2 * kz * wz - s * kz * kz,
                        first * (ky * wz + kz * wy) - s * ky * kz,
                        first * (kx * wz + kz * wx) - s * kx * kz,
                        first * (kx * wy + ky * wx) - s * kx * ky,
                        zero,
                        zero,
                    ]
                )
            )
        return np.stack(columns)

    ix, iy, iz = index[:, None, None], index[None, :, None], index[None, None, :]
    table = 0.5 * (operator(ix, iy, iz) + operator((-ix) % G, (-iy) % G, (-iz) % G)) / NV
    return table.reshape(6, 8, G, G * G).transpose(2, 0, 1, 3).astype(np.float32)


def plane_tables():
    plane = np.arange(G * G)
    phase = (plane[:, None] // G * (plane[None, :] // G) + plane[:, None] % G * (plane[None, :] % G)) % G
    parts = []
    for table in (np.cos(phase * (2 * np.pi / G)), np.sin(phase * (2 * np.pi / G))):
        table = table.astype(np.float32)
        high = table.astype(bf16)
        parts += [high, (table - high.astype(np.float32)).astype(bf16)]
    return np.stack(parts)


def twiddle(value, power, sign):
    re, im = value
    power %= 16
    if power == 0:
        return re, im
    if power == 4:
        return (-im, re) if sign > 0 else (im, -re)
    if power == 8:
        return -re, -im
    if power == 12:
        return (im, -re) if sign > 0 else (-im, re)
    angle = sign * 2 * math.pi * power / 16
    c, s = math.cos(angle), math.sin(angle)
    if power % 4 == 2:
        h = abs(c)
        a = re if c > 0 else -re
        b = im if c > 0 else -im
        if c * s > 0:
            return (a - b) * h, (a + b) * h
        return (a + b) * h, (b - a) * h
    return re * c - im * s, re * s + im * c


def dft4(v, sign):
    (ar, ai), (br, bi), (cr, ci), (dr, di) = v
    pr, pi_ = ar + cr, ai + ci
    mr, mi = ar - cr, ai - ci
    qr, qi = br + dr, bi + di
    nr, ni = br - dr, bi - di
    if sign < 0:
        jr, ji = ni, -nr
    else:
        jr, ji = -ni, nr
    return [(pr + qr, pi_ + qi), (mr + jr, mi + ji), (pr - qr, pi_ - qi), (mr - jr, mi - ji)]


def dft16(values, sign):
    inner = []
    for n2 in range(4):
        inner.append(dft4([values[n2 + 4 * n1] for n1 in range(4)], sign))
    out = [None] * 16
    for k1 in range(4):
        column = dft4([twiddle(inner[n2][k1], n2 * k1, sign) for n2 in range(4)], sign)
        for k2 in range(4):
            out[k1 + 4 * k2] = column[k2]
    return out


def slab_stress(d, first_rows):
    wide = d.shape
    trace = d[0:1] + d[1:2] + d[2:3]
    lam_trace = jnp.broadcast_to(d[6:7] * trace, wide)
    twice = jnp.broadcast_to(2.0 * d[7:8], wide)
    return twice * d + jnp.where(first_rows, lam_trace, 0.0)


def plane_products(sr, si, cmat):
    x = jnp.concatenate([sr[...], si[...]], axis=0)
    high = x.astype(bf16)
    low = (x - high.astype(f32)).astype(bf16)

    def times(at):
        a, b = cmat[at], cmat[at + 1]
        return (
            jnp.dot(high, a, preferred_element_type=f32)
            + jnp.dot(low, a, preferred_element_type=f32)
            + jnp.dot(high, b, preferred_element_type=f32)
        )

    return times(0), times(2)


def cells_kernel(
    count, owner, element, disp, nm, grads, micro, green, cmat, send, band_stress, st, sr, si
):
    half_rows = 8 * G
    lane = lax.broadcasted_iota(jnp.int32, (8, LANES), 1)
    row = lax.broadcasted_iota(jnp.int32, (8, LANES), 0)
    row_wide = lax.broadcasted_iota(jnp.int32, (8, 2 * LANES), 0)
    first_rows = row_wide < 3

    targets = []
    for k in range(4):
        e = element[0, k]
        base = pl.multiple_of(e // LANES * LANES, LANES)
        at = lane == e % LANES

        def pick(tile):
            return jnp.sum(jnp.where(at, tile, 0.0), axis=1, keepdims=True)

        node = pick(nm[:, pl.ds(base, LANES)].astype(f32)).astype(jnp.int32)
        shape = [jnp.broadcast_to(pick(grads[j, :, pl.ds(base, LANES)]), (8, LANES)) for j in range(3)]
        node = jnp.broadcast_to(node, (8, LANES)) - lane
        found = [jnp.zeros((8, LANES), f32) for _ in range(3)]
        for r in range(72):
            hit = node == r * LANES
            for c in range(3):
                values = jnp.broadcast_to(disp[c : c + 1, r * LANES : (r + 1) * LANES], (8, LANES))
                found[c] = jnp.where(hit, values, found[c])
        u = [jnp.sum(found[c], axis=1, keepdims=True) for c in range(3)]

        def total(value):
            return jnp.sum(value, axis=0, keepdims=True)

        parts = [
            total(u[0] * shape[0]),
            total(u[1] * shape[1]),
            total(u[2] * shape[2]),
            0.5 * total(u[1] * shape[2] + u[2] * shape[1]),
            0.5 * total(u[0] * shape[2] + u[2] * shape[0]),
            0.5 * total(u[0] * shape[1] + u[1] * shape[0]),
        ]
        target = jnp.zeros((8, LANES), f32)
        for c in range(6):
            target = jnp.where(row == c, jnp.broadcast_to(parts[c], (8, LANES)), target)
        targets.append(target)

    def slab(k, x, iteration):
        if iteration == 0:
            return micro[k, :, 2 * LANES * x : 2 * LANES * (x + 1)]
        return st[k, 8 * x : 8 * x + 8, :]

    shifts = []
    for k in range(4):
        total = jnp.zeros((8, 2 * LANES), f32)
        for x in range(G):
            total = total + slab(k, x, 0)
        mean = jnp.sum(total, axis=1, keepdims=True) * (1.0 / NV)
        shift = jnp.where(row < 6, targets[k] - mean, 0.0)
        shifts.append(jnp.concatenate([shift, shift], axis=1))

    for iteration in range(ITERS):
        for pair in range(2):
            for x in range(G):
                at = pair * half_rows + 8 * x
                sr[at : at + 8, :] = slab_stress(slab(2 * pair, x, iteration), first_rows)
                si[at : at + 8, :] = slab_stress(slab(2 * pair + 1, x, iteration), first_rows)
        by_cos, by_sin = plane_products(sr, si, cmat)
        rows = 2 * half_rows
        sr[...] = by_cos[:rows] + by_sin[rows:]
        si[...] = by_cos[rows:] - by_sin[:rows]
        for pair in range(2):
            for part in range(2):
                cols = slice(part * LANES, (part + 1) * LANES)
                at = [pair * half_rows + 8 * x for x in range(G)]
                values = dft16([(sr[a : a + 8, cols], si[a : a + 8, cols]) for a in at], -1)
                for x in range(G):
                    sr[at[x] : at[x] + 8, cols] = values[x][0]
                    si[at[x] : at[x] + 8, cols] = values[x][1]
                updates = []
                for x in range(G):
                    re = im = None
                    for j in range(6):
                        weight = green[x, j, :, cols]
                        tr = weight * jnp.broadcast_to(sr[at[x] + j : at[x] + j + 1, cols], (8, LANES))
                        ti = weight * jnp.broadcast_to(si[at[x] + j : at[x] + j + 1, cols], (8, LANES))
                        re = tr if re is None else re + tr
                        im = ti if im is None else im + ti
                    updates.append((re, im))
                values = dft16(updates, 1)
                for x in range(G):
                    sr[at[x] : at[x] + 8, cols] = values[x][0]
                    si[at[x] : at[x] + 8, cols] = values[x][1]
        by_cos, by_sin = plane_products(sr, si, cmat)
        sr[...] = by_cos[:rows] - by_sin[rows:]
        si[...] = by_cos[rows:] + by_sin[:rows]
        for k in range(4):
            source = (sr, si)[k % 2]
            for x in range(G):
                at = k // 2 * half_rows + 8 * x
                value = slab(k, x, iteration) - source[at : at + 8, :]
                if iteration == 0:
                    value = value + shifts[k]
                st[k, 8 * x : 8 * x + 8, :] = value

    send[pl.ds(8, 4 * TILES, stride=9), :] = jnp.full((4 * TILES, LANES), -1.0, f32)
    result = jnp.zeros((8, LANES), f32)
    for k in range(4):
        live = k < count[0]
        total = jnp.zeros((8, 2 * LANES), f32)
        for x in range(G):
            total = total + slab_stress(st[k, 8 * x : 8 * x + 8, :], first_rows)
        mean = jnp.sum(total, axis=1, keepdims=True) * (1.0 / NV)
        result = jnp.where((lane == k) & live, jnp.broadcast_to(mean, (8, LANES)), result)
        pool = owner[0, k] & 3

        @pl.when(live)
        def _():
            for i in range(TILES):
                x, part = i // 2, i % 2
                send[pl.ds(9 * (4 * i + pool), 8), :] = st[
                    k, 8 * x : 8 * x + 8, part * LANES : (part + 1) * LANES
                ]
            brick = (owner[0, k] >> 2).astype(f32)
            send[pl.ds(9 * pool + 8, TILES, stride=36), :] = jnp.full((TILES, LANES), brick, f32)

    band_stress[...] = result[0:6, 0:4]


def solve_cells(count, owner, element, disp, nm, grads, micro, green, cmat):
    rows = 16 * G
    return pl.pallas_call(
        cells_kernel,
        out_shape=(
            jax.ShapeDtypeStruct((36 * TILES, LANES), f32),
            jax.ShapeDtypeStruct((6, 4), f32),
        ),
        in_specs=[pl.BlockSpec(memory_space=SMEM)] * 3 + [pl.BlockSpec(memory_space=VMEM)] * 6,
        out_specs=(pl.BlockSpec(memory_space=VMEM), pl.BlockSpec(memory_space=VMEM)),
        scratch_shapes=[
            VMEM((4, 8 * G, 2 * LANES), f32),
            VMEM((rows, 2 * LANES), f32),
            VMEM((rows, 2 * LANES), f32),
        ],
        compiler_params=pltpu.CompilerParams(vmem_limit_bytes=56 << 20),
        name="cells",
    )(count, owner, element, disp, nm, grads, micro, green, cmat)


def one_hot_sum(node, values, width):
    hi = jnp.broadcast_to(node >> 8, (HI, width))
    lo = jnp.broadcast_to(node & 255, (LO, width))
    coarse = lax.broadcasted_iota(jnp.int32, (HI, width), 0) == hi
    fine = lax.broadcasted_iota(jnp.int32, (LO, width), 0) == lo
    left = jnp.concatenate(
        [jnp.where(coarse, jnp.broadcast_to(v, (HI, width)), 0.0) for v in values], axis=0
    ).astype(bf16)
    right = jnp.where(fine, 1.0, 0.0).astype(bf16)
    return left, right


def halves(value):
    high = value.astype(bf16).astype(f32)
    return high, value - high


def macro_tiles(begin, end, unroll, count, element, replace, disp, nm, grads, volumes, moduli, sums):
    lane = lax.broadcasted_iota(jnp.int32, (1, LANES), 1)
    live = [k < count[0] for k in range(4)]

    def scatter(node, forces):
        values = []
        for force in forces:
            values += list(halves(force))
        total = None
        for s in range(0, 8, 2):
            lefts, rights = [], []
            for q in (s, s + 1):
                left, right = one_hot_sum(node[q : q + 1], [v[q : q + 1] for v in values], LANES)
                lefts.append(left)
                rights.append(right)
            product = lax.dot_general(
                jnp.concatenate(lefts, axis=1),
                jnp.concatenate(rights, axis=1),
                (((1,), (1,)), ((), ())),
                preferred_element_type=f32,
            )
            total = product if total is None else total + product
        return total

    def forces_of(t):
        cols = pl.ds(pl.multiple_of(t * LANES, LANES), LANES)
        node = nm[:, cols]
        hi, lo = node >> 7, node & 127
        u = [jnp.zeros((8, LANES), f32) for _ in range(3)]
        for r in range(72):
            hit = hi == r
            for c in range(3):
                values = jnp.broadcast_to(disp[c : c + 1, r * LANES : (r + 1) * LANES], (8, LANES))
                found = jnp.take_along_axis(values, lo, axis=1, mode="promise_in_bounds")
                u[c] = jnp.where(hit, found, u[c])
        g = [grads[j, :, cols] for j in range(3)]

        def total(value):
            return jnp.sum(value, axis=0, keepdims=True)

        strain = [
            total(u[0] * g[0]),
            total(u[1] * g[1]),
            total(u[2] * g[2]),
            0.5 * total(u[1] * g[2] + u[2] * g[1]),
            0.5 * total(u[0] * g[2] + u[2] * g[0]),
            0.5 * total(u[0] * g[1] + u[1] * g[0]),
        ]
        lam = moduli[0:1, cols]
        mu = moduli[1:2, cols]
        volume = volumes[pl.ds(t, 1), :]
        spherical = lam * (strain[0] + strain[1] + strain[2])
        stress = [spherical + 2.0 * mu * strain[c] for c in range(3)]
        stress += [2.0 * mu * strain[c] for c in range(3, 6)]
        for k in range(4):
            hit = (lane + t * LANES == element[0, k]) & live[k]
            stress = [jnp.where(hit, replace[c, k], stress[c]) for c in range(6)]
        xx, yy, zz, yz, xz, xy = [
            jnp.broadcast_to(component * volume, (8, LANES)) for component in stress
        ]
        fx = xx * g[0] + xy * g[1] + xz * g[2]
        fy = xy * g[0] + yy * g[1] + yz * g[2]
        fz = xz * g[0] + yz * g[1] + zz * g[2]
        return node, fx, fy, fz

    def group(step):
        return tuple(forces_of(begin + step * unroll + i) for i in range(unroll))

    def add(carry):
        total = None
        for node, *forces in carry:
            part = scatter(node, forces)
            total = part if total is None else total + part
        sums[...] += total

    def body(step, carry):
        add(carry)
        return group(step)

    add(lax.fori_loop(1, (end - begin) // unroll, body, group(0)))


def macro_first_kernel(unroll, count, element, replace, disp, nm, grads, volumes, moduli, sums):
    sums[...] = jnp.zeros_like(sums)
    macro_tiles(0, SPLIT, unroll, count, element, replace, disp, nm, grads, volumes, moduli, sums)


def macro_last_kernel(
    unroll,
    count,
    element,
    replace,
    core_index,
    pool_index,
    disp,
    nm,
    grads,
    volumes,
    moduli,
    so_far,
    shared,
    own,
    inner,
    outer,
    sums,
    faces,
):
    sums[...] = so_far[...]
    macro_tiles(SPLIT, 64, unroll, count, element, replace, disp, nm, grads, volumes, moduli, sums)

    for c in range(3):
        at = 2 * c * HI
        own[c * HI : (c + 1) * HI, :] = sums[at : at + HI, :] + sums[at + HI : at + 2 * HI, :]

    for pair in range(4):
        first, second = 2 * pair, 2 * pair + 1
        node = jnp.concatenate(
            [
                shared[0, :, first * LANES : (first + 1) * LANES],
                shared[0, :, second * LANES : (second + 1) * LANES],
            ],
            axis=0,
        )
        hi, lo = node >> 7, node & 127
        picked = [jnp.zeros((8, LANES), f32) for _ in range(3)]
        for r in range(72):
            hit = hi == r
            for c in range(3):
                at = c * HI + r // 2
                cols = slice(r % 2 * LANES, (r % 2 + 1) * LANES)
                values = jnp.broadcast_to(own[at : at + 1, cols], (8, LANES))
                found = jnp.take_along_axis(values, lo, axis=1, mode="promise_in_bounds")
                picked[c] = jnp.where(hit, found, picked[c])
        for c in range(3):
            for face in range(4):
                faces[face, c : c + 1, first * LANES : (first + 1) * LANES] = picked[c][face : face + 1]
                faces[face, c : c + 1, second * LANES : (second + 1) * LANES] = picked[c][
                    4 + face : 5 + face
                ]
    core, pool = core_index[0], pool_index[0]
    pools = inner.shape[0] // 2
    inner[...] = jnp.zeros_like(inner)
    inner[(1 - core) * pools + pool] = faces[1 - core]
    outer[...] = faces[core]

    @pl.when(pool > 0)
    def _():
        inner[core * pools + pool - 1] = faces[2]

    @pl.when(pool < pools - 1)
    def _():
        inner[core * pools + pool + 1] = faces[3]


def macro_first(*arguments):
    vmem = pl.BlockSpec(memory_space=VMEM)
    return pl.pallas_call(
        functools.partial(macro_first_kernel, UNROLL),
        out_shape=jax.ShapeDtypeStruct((6 * HI, LO), f32),
        in_specs=[pl.BlockSpec(memory_space=SMEM)] * 3 + [vmem] * 5,
        out_specs=vmem,
        compiler_params=pltpu.CompilerParams(vmem_limit_bytes=32 << 20),
        name="macro_first",
    )(*arguments)


def macro_last(pools, *arguments):
    vmem = pl.BlockSpec(memory_space=VMEM)
    return pl.pallas_call(
        functools.partial(macro_last_kernel, UNROLL),
        out_shape=(
            jax.ShapeDtypeStruct((3 * HI, LO), f32),
            jax.ShapeDtypeStruct((2 * pools, 3, 1024), f32),
            jax.ShapeDtypeStruct((3, 1024), f32),
        ),
        in_specs=[pl.BlockSpec(memory_space=SMEM)] * 5 + [vmem] * 7,
        out_specs=(vmem,) * 3,
        scratch_shapes=[VMEM((6 * HI, LO), f32), VMEM((4, 3, 1024), f32)],
        compiler_params=pltpu.CompilerParams(vmem_limit_bytes=32 << 20),
        name="macro_last",
    )(*arguments)


def assemble_kernel(core_index, pool_index, own, shared, inner, outer, external, mass, out):
    core, pool = core_index[0], pool_index[0]
    pools = inner.shape[0] // 2
    below, above = jnp.maximum(pool - 1, 0), jnp.minimum(pool + 1, pools - 1)
    arrivals = (
        (1 - core, True, lambda c, cols: inner[(1 - core) * pools + pool, c : c + 1, cols]),
        (core, True, lambda c, cols: outer[c : c + 1, cols]),
        (2, pool > 0, lambda c, cols: inner[core * pools + below, c : c + 1, cols]),
        (3, pool < pools - 1, lambda c, cols: inner[core * pools + above, c : c + 1, cols]),
    )
    total = None
    for face, there, arrived in arrivals:
        for part in range(4):
            cols = slice(part * LO, (part + 1) * LO)
            values = []
            for c in range(3):
                value = arrived(c, cols)
                if there is not True:
                    value = jnp.where(there, value, 0.0)
                values += list(halves(value))
            left, right = one_hot_sum(shared[0, pl.ds(face, 1), cols], values, LO)
            product = lax.dot_general(
                left, right, (((1,), (1,)), ((), ())), preferred_element_type=f32
            )
            total = product if total is None else total + product
    for c in range(3):
        at = 2 * c * HI
        whole = own[c * HI : (c + 1) * HI, :] + total[at : at + HI] + total[at + HI : at + 2 * HI]
        for r in range(36):
            out[c : c + 1, r * LO : (r + 1) * LO] = whole[r : r + 1]
    out[...] = (external[...] - out[...]) / mass[...]


def assemble(place, own, shared, inner, outer, external, mass):
    vmem = pl.BlockSpec(memory_space=VMEM)
    return pl.pallas_call(
        assemble_kernel,
        out_shape=jax.ShapeDtypeStruct(external.shape, f32),
        in_specs=[pl.BlockSpec(memory_space=SMEM)] * 2 + [vmem] * 6,
        out_specs=vmem,
        compiler_params=pltpu.CompilerParams(vmem_limit_bytes=32 << 20),
        name="assemble",
    )(*place, own, shared, inner, outer, external, mass)


def sort_kernel(pieces, out, order, places, sem):
    blocks = pieces.shape[0] // 9
    lane = lax.broadcasted_iota(jnp.int32, (blocks, LANES), 1)
    block = lax.broadcasted_iota(jnp.int32, (blocks, LANES), 0)
    hit = pieces[pl.ds(8, blocks, stride=9), :] == lane.astype(f32)
    order[0:1, :] = jnp.min(jnp.where(hit, block, blocks - 1), axis=0, keepdims=True)
    order[1:2, :] = jnp.max(jnp.where(hit, block, 0), axis=0, keepdims=True)
    copy = pltpu.make_async_copy(order, places, sem)
    copy.start()
    copy.wait()
    for b in range(out.shape[0]):
        for s in range(2):
            out[b, s] = pieces[pl.ds(9 * places[s, b], 8), :]


def sort_pieces(pieces, bricks):
    vmem = pl.BlockSpec(memory_space=VMEM)
    return pl.pallas_call(
        sort_kernel,
        out_shape=jax.ShapeDtypeStruct((bricks, 2, 8, LANES), f32),
        in_specs=[vmem],
        out_specs=vmem,
        scratch_shapes=[VMEM((8, LANES), jnp.int32), SMEM((8, LANES), jnp.int32), pltpu.SemaphoreType.DMA],
        compiler_params=pltpu.CompilerParams(vmem_limit_bytes=32 << 20),
        name="sort_pieces",
    )(pieces)


def join_kernel(pieces, out):
    for i in range(TILES):
        for s in range(2):
            out[s, :, i * LANES : (i + 1) * LANES] = pieces[i, s]


def join_pieces(pieces):
    vmem = pl.BlockSpec(memory_space=VMEM)
    return pl.pallas_call(
        join_kernel,
        out_shape=jax.ShapeDtypeStruct((2, 8, NV), f32),
        in_specs=[vmem],
        out_specs=vmem,
        name="join_pieces",
    )(pieces)


def shards(
    displacement,
    node_map,
    shape_grads,
    volumes,
    elastic_moduli,
    external_force,
    nodal_mass,
    shared_nodes,
    band_count,
    band_owner,
    band_element,
    micro_fields,
):
    bricks, pools = lax.axis_size(BRICK), lax.axis_size("pool")
    place = tuple(lax.axis_index(axis).astype(jnp.int32).reshape(1) for axis in ("core", "pool"))
    send, band_stress = solve_cells(
        band_count,
        band_owner,
        band_element,
        displacement,
        node_map,
        shape_grads,
        micro_fields,
        jnp.asarray(green_table()),
        jnp.asarray(plane_tables()),
    )
    pieces = lax.all_to_all(
        send.reshape(bricks * pools, 1, 9 * LANES), BOTH, split_axis=0, concat_axis=0, tiled=True
    )
    sparse = (band_count, band_element, band_stress)
    dense = (displacement, node_map, shape_grads, volumes.reshape(64, LANES), elastic_moduli)
    so_far = macro_first(*sparse, *dense)
    pieces, so_far = lax.optimization_barrier((pieces, so_far))
    sorted_pieces = sort_pieces(pieces.reshape(9 * bricks * pools, LANES), bricks)
    sorted_pieces, so_far = lax.optimization_barrier((sorted_pieces, so_far))
    mine = lax.all_to_all(sorted_pieces, BRICK, split_axis=0, concat_axis=0, tiled=True)
    own, inner, outer = macro_last(pools, *sparse, *place, *dense, so_far, shared_nodes)
    inner = lax.all_to_all(inner, ("core", "pool"), split_axis=0, concat_axis=0, tiled=True)
    steps = [(i, i + 1) for i in range(1, bricks - 1, 2)]
    outer = lax.ppermute(outer, BRICK, steps + [(j, i) for i, j in steps])
    owned_fields = join_pieces(mine)
    inner, outer, owned_fields = lax.optimization_barrier((inner, outer, owned_fields))
    acceleration = assemble(
        place, own, shared_nodes, inner, outer, external_force, nodal_mass.reshape(1, -1)
    )
    return (acceleration, band_stress, owned_fields)


def solution(mesh):
    bricks, pools = mesh.devices.shape
    split = jax.sharding.Mesh(
        mesh.devices.reshape(4, bricks // 8, 2, pools), ("row", "pair", "core", "pool")
    )
    placed = (
        P(None, BOTH),
        P(None, BOTH),
        P(None, None, BOTH),
        P(BOTH),
        P(None, BOTH),
        P(None, BOTH),
        P(BOTH),
        P(BOTH, None, None),
        P(BOTH),
        P(BOTH, None),
        P(BOTH, None),
        P(BOTH, None, None),
    )
    return jax.shard_map(
        shards,
        mesh=split,
        in_specs=placed,
        out_specs=(P(None, BOTH), P(None, BOTH), P(BOTH, None, None)),
        check_vma=False,
    )
```

```python
import functools
import math

import jax
import jax.numpy as jnp
import numpy as np
from jax import lax
from jax.experimental import pallas as pl
from jax.experimental.pallas import tpu as pltpu
from jax.sharding import PartitionSpec as P

G = 16
NV = 4096
ITERS = 2
LANES = 128
TILES = 32
HI = 40
LO = 256
UNROLL = 2
SPLIT = 40
BRICK = ("row", "pair", "core")
BOTH = BRICK + ("pool",)
VMEM = pltpu.VMEM
SMEM = pltpu.SMEM
f32 = jnp.float32
bf16 = jnp.bfloat16

ref_lambda = 5.5
ref_shear = 5.5


def green_table():
    index = np.arange(G)

    def operator(ix, iy, iz):
        wave = [np.where(2 * m < G, m, m - G).astype(np.float64) for m in (ix, iy, iz)]
        kx, ky, kz = np.broadcast_arrays(wave[0], wave[1], wave[2])
        square = kx * kx + ky * ky + kz * kz
        safe = np.where(square > 0, square, 1.0)
        first = np.where(square > 0, 1.0 / (2.0 * ref_shear * safe), 0.0)
        factor = (ref_lambda + ref_shear) / (ref_shear * (ref_lambda + 2.0 * ref_shear))
        second = np.where(square > 0, factor / (safe * safe), 0.0)
        zero, one = np.zeros_like(kx), np.ones_like(kx)
        columns = []
        for j in range(6):
            xx, yy, zz, yz, xz, xy = [one if j == c else zero for c in range(6)]
            wx = xx * kx + xy * ky + xz * kz
            wy = xy * kx + yy * ky + yz * kz
            wz = xz * kx + yz * ky + zz * kz
            s = (wx * kx + wy * ky + wz * kz) * second
            columns.append(
                np.stack(
                    [
                        first * 2 * kx * wx - s * kx * kx,
                        first * 2 * ky * wy - s * ky * ky,
                        first * 2 * kz * wz - s * kz * kz,
                        first * (ky * wz + kz * wy) - s * ky * kz,
                        first * (kx * wz + kz * wx) - s * kx * kz,
                        first * (kx * wy + ky * wx) - s * kx * ky,
                        zero,
                        zero,
                    ]
                )
            )
        return np.stack(columns)

    ix, iy, iz = index[:, None, None], index[None, :, None], index[None, None, :]
    table = 0.5 * (operator(ix, iy, iz) + operator((-ix) % G, (-iy) % G, (-iz) % G)) / NV
    table = table.reshape(6, 8, G, G * G).transpose(2, 0, 1, 3)
    pairs, alone = half_plane()
    even, odd = np.concatenate([pairs, alone[:2]]), np.concatenate([pairs, alone[2:]])
    return np.stack([table[..., even], table[..., odd]]).astype(np.float32)


def half_plane():
    index = np.arange(G * G)
    mirror = (-(index // G)) % G * G + (-(index % G)) % G
    return index[index < mirror], index[index == mirror]


def plane_tables():
    pairs, alone = half_plane()
    plane = np.arange(G * G)

    def angle(k):
        turns = (plane[:, None] // G * (k // G)[None, :] + plane[:, None] % G * (k % G)[None, :]) % G
        return turns * (2 * np.pi / G)

    there = np.concatenate(
        [
            np.cos(angle(pairs)),
            np.cos(angle(alone[:2])),
            -np.sin(angle(pairs)),
            np.cos(angle(alone[2:])),
        ],
        axis=1,
    )
    weight = np.full((G * G, 1), 2.0)
    weight[[126, 127, 254, 255]] = 1.0
    parts = []
    for table in (there, weight * there.T):
        high = table.astype(np.float32).astype(bf16)
        parts += [high, (table - high.astype(np.float64)).astype(np.float32).astype(bf16)]
    return np.stack(parts)


def twiddle(value, power, sign):
    re, im = value
    power %= 16
    if power == 0:
        return re, im
    if power == 4:
        return (-im, re) if sign > 0 else (im, -re)
    if power == 8:
        return -re, -im
    if power == 12:
        return (im, -re) if sign > 0 else (-im, re)
    angle = sign * 2 * math.pi * power / 16
    c, s = math.cos(angle), math.sin(angle)
    if power % 4 == 2:
        h = abs(c)
        a = re if c > 0 else -re
        b = im if c > 0 else -im
        if c * s > 0:
            return (a - b) * h, (a + b) * h
        return (a + b) * h, (b - a) * h
    return re * c - im * s, re * s + im * c


def dft4(v, sign):
    (ar, ai), (br, bi), (cr, ci), (dr, di) = v
    pr, pi_ = ar + cr, ai + ci
    mr, mi = ar - cr, ai - ci
    qr, qi = br + dr, bi + di
    nr, ni = br - dr, bi - di
    if sign < 0:
        jr, ji = ni, -nr
    else:
        jr, ji = -ni, nr
    return [(pr + qr, pi_ + qi), (mr + jr, mi + ji), (pr - qr, pi_ - qi), (mr - jr, mi - ji)]


def dft16(values, sign):
    inner = []
    for n2 in range(4):
        inner.append(dft4([values[n2 + 4 * n1] for n1 in range(4)], sign))
    out = [None] * 16
    for k1 in range(4):
        column = dft4([twiddle(inner[n2][k1], n2 * k1, sign) for n2 in range(4)], sign)
        for k2 in range(4):
            out[k1 + 4 * k2] = column[k2]
    return out


def slab_stress(d, first_rows):
    wide = d.shape
    trace = d[0:1] + d[1:2] + d[2:3]
    lam_trace = jnp.broadcast_to(d[6:7] * trace, wide)
    twice = jnp.broadcast_to(2.0 * d[7:8], wide)
    return twice * d + jnp.where(first_rows, lam_trace, 0.0)


def plane_product(x, cmat, at):
    high = x.astype(bf16)
    low = (x - high.astype(f32)).astype(bf16)
    rows = x.shape[0]
    both = jnp.dot(jnp.concatenate([high, low], axis=0), cmat[at], preferred_element_type=f32)
    return both[:rows] + both[rows:] + jnp.dot(high, cmat[at + 1], preferred_element_type=f32)


def cells_kernel(
    count, owner, element, disp, nm, grads, micro, green, cmat, send, band_stress, st, *work
):
    half_rows = 8 * G
    lane = lax.broadcasted_iota(jnp.int32, (8, LANES), 1)
    row = lax.broadcasted_iota(jnp.int32, (8, LANES), 0)
    row_wide = lax.broadcasted_iota(jnp.int32, (8, 2 * LANES), 0)
    first_rows = row_wide < 3

    targets = []
    for k in range(4):
        e = element[0, k]
        base = pl.multiple_of(e // LANES * LANES, LANES)
        at = lane == e % LANES

        def pick(tile):
            return jnp.sum(jnp.where(at, tile, 0.0), axis=1, keepdims=True)

        node = pick(nm[:, pl.ds(base, LANES)].astype(f32)).astype(jnp.int32)
        shape = [jnp.broadcast_to(pick(grads[j, :, pl.ds(base, LANES)]), (8, LANES)) for j in range(3)]
        node = jnp.broadcast_to(node, (8, LANES)) - lane
        found = [jnp.zeros((8, LANES), f32) for _ in range(3)]
        for r in range(72):
            hit = node == r * LANES
            for c in range(3):
                values = jnp.broadcast_to(disp[c : c + 1, r * LANES : (r + 1) * LANES], (8, LANES))
                found[c] = jnp.where(hit, values, found[c])
        u = [jnp.sum(found[c], axis=1, keepdims=True) for c in range(3)]

        def total(value):
            return jnp.sum(value, axis=0, keepdims=True)

        parts = [
            total(u[0] * shape[0]),
            total(u[1] * shape[1]),
            total(u[2] * shape[2]),
            0.5 * total(u[1] * shape[2] + u[2] * shape[1]),
            0.5 * total(u[0] * shape[2] + u[2] * shape[0]),
            0.5 * total(u[0] * shape[1] + u[1] * shape[0]),
        ]
        target = jnp.zeros((8, LANES), f32)
        for c in range(6):
            target = jnp.where(row == c, jnp.broadcast_to(parts[c], (8, LANES)), target)
        targets.append(target)

    def slab(k, x, iteration):
        if iteration == 0:
            return micro[k, :, 2 * LANES * x : 2 * LANES * (x + 1)]
        return st[k, 8 * x : 8 * x + 8, :]

    shifts = []
    for k in range(4):
        total = jnp.zeros((8, 2 * LANES), f32)
        for x in range(G):
            total = total + slab(k, x, 0)
        mean = jnp.sum(total, axis=1, keepdims=True) * (1.0 / NV)
        shift = jnp.where(row < 6, targets[k] - mean, 0.0)
        shifts.append(jnp.concatenate([shift, shift], axis=1))

    re_cols, im_cols = slice(0, LANES), slice(LANES, 2 * LANES)
    own_mirror = lane >= 126
    whole_mirror = lax.broadcasted_iota(jnp.int32, (half_rows, LANES), 1) >= 126
    for iteration in range(ITERS):
        for pair in range(2):
            plane, spectrum = work[2 * pair], work[2 * pair + 1]
            at = [[cell * half_rows + 8 * x for x in range(G)] for cell in range(2)]
            for cell in range(2):
                for x in range(G):
                    a = at[cell][x]
                    plane[a : a + 8, :] = slab_stress(slab(2 * pair + cell, x, iteration), first_rows)
            plane[...] = plane_product(plane[...], cmat, 0)
            for cell in range(2):
                values = []
                for x in range(G):
                    a = at[cell][x]
                    re, im = plane[a : a + 8, re_cols], plane[a : a + 8, im_cols]
                    if cell == 0:
                        other = at[1][x]
                        im = jnp.where(own_mirror, plane[other : other + 8, re_cols], im)
                    else:
                        other = at[0][x]
                        re = jnp.where(own_mirror, plane[other : other + 8, im_cols], re)
                    values.append((re, im))
                values = dft16(values, -1)
                for x in range(G):
                    a = at[cell][x]
                    spectrum[a : a + 8, re_cols] = values[x][0]
                    spectrum[a : a + 8, im_cols] = values[x][1]
            for cell in range(2):
                updates = []
                for x in range(G):
                    re = im = None
                    for j in range(6):
                        weight = green[cell, x, j]
                        a = at[cell][x] + j
                        tr = weight * jnp.broadcast_to(spectrum[a : a + 1, re_cols], (8, LANES))
                        ti = weight * jnp.broadcast_to(spectrum[a : a + 1, im_cols], (8, LANES))
                        re = tr if re is None else re + tr
                        im = ti if im is None else im + ti
                    updates.append((re, im))
                values = dft16(updates, 1)
                for x in range(G):
                    a = at[cell][x]
                    plane[a : a + 8, re_cols] = values[x][0]
                    plane[a : a + 8, im_cols] = values[x][1]
            first_im = plane[:half_rows, im_cols]
            second_re = plane[half_rows:, re_cols]
            plane[:half_rows, im_cols] = jnp.where(whole_mirror, second_re, first_im)
            plane[half_rows:, re_cols] = jnp.where(whole_mirror, first_im, second_re)
            update = plane_product(plane[...], cmat, 2)
            for cell in range(2):
                k = 2 * pair + cell
                for x in range(G):
                    a = at[cell][x]
                    value = slab(k, x, iteration) - update[a : a + 8, :]
                    if iteration == 0:
                        value = value + shifts[k]
                    st[k, 8 * x : 8 * x + 8, :] = value

    send[pl.ds(8, 4 * TILES, stride=9), :] = jnp.full((4 * TILES, LANES), -1.0, f32)
    result = jnp.zeros((8, LANES), f32)
    for k in range(4):
        live = k < count[0]
        total = jnp.zeros((8, 2 * LANES), f32)
        for x in range(G):
            total = total + slab_stress(st[k, 8 * x : 8 * x + 8, :], first_rows)
        mean = jnp.sum(total, axis=1, keepdims=True) * (1.0 / NV)
        result = jnp.where((lane == k) & live, jnp.broadcast_to(mean, (8, LANES)), result)
        pool = owner[0, k] & 3

        @pl.when(live)
        def _():
            for i in range(TILES):
                x, part = i // 2, i % 2
                send[pl.ds(9 * (4 * i + pool), 8), :] = st[
                    k, 8 * x : 8 * x + 8, part * LANES : (part + 1) * LANES
                ]
            brick = (owner[0, k] >> 2).astype(f32)
            send[pl.ds(9 * pool + 8, TILES, stride=36), :] = jnp.full((TILES, LANES), brick, f32)

    band_stress[...] = result[0:6, 0:4]


def solve_cells(count, owner, element, disp, nm, grads, micro, green, cmat):
    return pl.pallas_call(
        cells_kernel,
        out_shape=(
            jax.ShapeDtypeStruct((36 * TILES, LANES), f32),
            jax.ShapeDtypeStruct((6, 4), f32),
        ),
        in_specs=[pl.BlockSpec(memory_space=SMEM)] * 3 + [pl.BlockSpec(memory_space=VMEM)] * 6,
        out_specs=(pl.BlockSpec(memory_space=VMEM), pl.BlockSpec(memory_space=VMEM)),
        scratch_shapes=[
            VMEM((4, 8 * G, 2 * LANES), f32),
        ]
        + [VMEM((16 * G, 2 * LANES), f32)] * 4,
        compiler_params=pltpu.CompilerParams(vmem_limit_bytes=56 << 20),
        name="cells",
    )(count, owner, element, disp, nm, grads, micro, green, cmat)


def one_hot_sum(node, values, width):
    hi = jnp.broadcast_to(node >> 8, (HI, width))
    lo = jnp.broadcast_to(node & 255, (LO, width))
    coarse = lax.broadcasted_iota(jnp.int32, (HI, width), 0) == hi
    fine = lax.broadcasted_iota(jnp.int32, (LO, width), 0) == lo
    left = jnp.concatenate(
        [jnp.where(coarse, jnp.broadcast_to(v, (HI, width)), 0.0) for v in values], axis=0
    ).astype(bf16)
    right = jnp.where(fine, 1.0, 0.0).astype(bf16)
    return left, right


def halves(value):
    high = value.astype(bf16).astype(f32)
    return high, value - high


def macro_tiles(begin, end, unroll, count, element, replace, disp, nm, grads, volumes, moduli, sums):
    lane = lax.broadcasted_iota(jnp.int32, (1, LANES), 1)
    live = [k < count[0] for k in range(4)]

    def scatter(node, forces):
        values = []
        for force in forces:
            values += list(halves(force))
        total = None
        for s in range(0, 8, 2):
            lefts, rights = [], []
            for q in (s, s + 1):
                left, right = one_hot_sum(node[q : q + 1], [v[q : q + 1] for v in values], LANES)
                lefts.append(left)
                rights.append(right)
            product = lax.dot_general(
                jnp.concatenate(lefts, axis=1),
                jnp.concatenate(rights, axis=1),
                (((1,), (1,)), ((), ())),
                preferred_element_type=f32,
            )
            total = product if total is None else total + product
        return total

    def forces_of(t):
        cols = pl.ds(pl.multiple_of(t * LANES, LANES), LANES)
        node = nm[:, cols]
        hi, lo = node >> 7, node & 127
        u = [jnp.zeros((8, LANES), f32) for _ in range(3)]
        for r in range(72):
            hit = hi == r
            for c in range(3):
                values = jnp.broadcast_to(disp[c : c + 1, r * LANES : (r + 1) * LANES], (8, LANES))
                found = jnp.take_along_axis(values, lo, axis=1, mode="promise_in_bounds")
                u[c] = jnp.where(hit, found, u[c])
        g = [grads[j, :, cols] for j in range(3)]

        def total(value):
            return jnp.sum(value, axis=0, keepdims=True)

        strain = [
            total(u[0] * g[0]),
            total(u[1] * g[1]),
            total(u[2] * g[2]),
            0.5 * total(u[1] * g[2] + u[2] * g[1]),
            0.5 * total(u[0] * g[2] + u[2] * g[0]),
            0.5 * total(u[0] * g[1] + u[1] * g[0]),
        ]
        lam = moduli[0:1, cols]
        mu = moduli[1:2, cols]
        volume = volumes[pl.ds(t, 1), :]
        spherical = lam * (strain[0] + strain[1] + strain[2])
        stress = [spherical + 2.0 * mu * strain[c] for c in range(3)]
        stress += [2.0 * mu * strain[c] for c in range(3, 6)]
        for k in range(4):
            hit = (lane + t * LANES == element[0, k]) & live[k]
            stress = [jnp.where(hit, replace[c, k], stress[c]) for c in range(6)]
        xx, yy, zz, yz, xz, xy = [
            jnp.broadcast_to(component * volume, (8, LANES)) for component in stress
        ]
        fx = xx * g[0] + xy * g[1] + xz * g[2]
        fy = xy * g[0] + yy * g[1] + yz * g[2]
        fz = xz * g[0] + yz * g[1] + zz * g[2]
        return node, fx, fy, fz

    def group(step):
        return tuple(forces_of(begin + step * unroll + i) for i in range(unroll))

    def add(carry):
        total = None
        for node, *forces in carry:
            part = scatter(node, forces)
            total = part if total is None else total + part
        sums[...] += total

    def body(step, carry):
        add(carry)
        return group(step)

    add(lax.fori_loop(1, (end - begin) // unroll, body, group(0)))


def macro_first_kernel(unroll, count, element, replace, disp, nm, grads, volumes, moduli, sums):
    sums[...] = jnp.zeros_like(sums)
    macro_tiles(0, SPLIT, unroll, count, element, replace, disp, nm, grads, volumes, moduli, sums)


def macro_last_kernel(
    unroll,
    count,
    element,
    replace,
    core_index,
    pool_index,
    disp,
    nm,
    grads,
    volumes,
    moduli,
    so_far,
    shared,
    own,
    inner,
    outer,
    sums,
    faces,
):
    sums[...] = so_far[...]
    macro_tiles(SPLIT, 64, unroll, count, element, replace, disp, nm, grads, volumes, moduli, sums)

    for c in range(3):
        at = 2 * c * HI
        own[c * HI : (c + 1) * HI, :] = sums[at : at + HI, :] + sums[at + HI : at + 2 * HI, :]

    for pair in range(4):
        first, second = 2 * pair, 2 * pair + 1
        node = jnp.concatenate(
            [
                shared[0, :, first * LANES : (first + 1) * LANES],
                shared[0, :, second * LANES : (second + 1) * LANES],
            ],
            axis=0,
        )
        hi, lo = node >> 7, node & 127
        picked = [jnp.zeros((8, LANES), f32) for _ in range(3)]
        for r in range(72):
            hit = hi == r
            for c in range(3):
                at = c * HI + r // 2
                cols = slice(r % 2 * LANES, (r % 2 + 1) * LANES)
                values = jnp.broadcast_to(own[at : at + 1, cols], (8, LANES))
                found = jnp.take_along_axis(values, lo, axis=1, mode="promise_in_bounds")
                picked[c] = jnp.where(hit, found, picked[c])
        for c in range(3):
            for face in range(4):
                faces[face, c : c + 1, first * LANES : (first + 1) * LANES] = picked[c][face : face + 1]
                faces[face, c : c + 1, second * LANES : (second + 1) * LANES] = picked[c][
                    4 + face : 5 + face
                ]
    core, pool = core_index[0], pool_index[0]
    pools = inner.shape[0] // 2
    inner[...] = jnp.zeros_like(inner)
    inner[(1 - core) * pools + pool] = faces[1 - core]
    outer[...] = faces[core]

    @pl.when(pool > 0)
    def _():
        inner[core * pools + pool - 1] = faces[2]

    @pl.when(pool < pools - 1)
    def _():
        inner[core * pools + pool + 1] = faces[3]


def macro_first(*arguments):
    vmem = pl.BlockSpec(memory_space=VMEM)
    return pl.pallas_call(
        functools.partial(macro_first_kernel, UNROLL),
        out_shape=jax.ShapeDtypeStruct((6 * HI, LO), f32),
        in_specs=[pl.BlockSpec(memory_space=SMEM)] * 3 + [vmem] * 5,
        out_specs=vmem,
        compiler_params=pltpu.CompilerParams(vmem_limit_bytes=32 << 20),
        name="macro_first",
    )(*arguments)


def macro_last(pools, *arguments):
    vmem = pl.BlockSpec(memory_space=VMEM)
    return pl.pallas_call(
        functools.partial(macro_last_kernel, UNROLL),
        out_shape=(
            jax.ShapeDtypeStruct((3 * HI, LO), f32),
            jax.ShapeDtypeStruct((2 * pools, 3, 1024), f32),
            jax.ShapeDtypeStruct((3, 1024), f32),
        ),
        in_specs=[pl.BlockSpec(memory_space=SMEM)] * 5 + [vmem] * 7,
        out_specs=(vmem,) * 3,
        scratch_shapes=[VMEM((6 * HI, LO), f32), VMEM((4, 3, 1024), f32)],
        compiler_params=pltpu.CompilerParams(vmem_limit_bytes=32 << 20),
        name="macro_last",
    )(*arguments)


def assemble_kernel(core_index, pool_index, own, shared, inner, outer, external, mass, out):
    core, pool = core_index[0], pool_index[0]
    pools = inner.shape[0] // 2
    below, above = jnp.maximum(pool - 1, 0), jnp.minimum(pool + 1, pools - 1)
    arrivals = (
        (1 - core, True, lambda c, cols: inner[(1 - core) * pools + pool, c : c + 1, cols]),
        (core, True, lambda c, cols: outer[c : c + 1, cols]),
        (2, pool > 0, lambda c, cols: inner[core * pools + below, c : c + 1, cols]),
        (3, pool < pools - 1, lambda c, cols: inner[core * pools + above, c : c + 1, cols]),
    )
    total = None
    for face, there, arrived in arrivals:
        for part in range(4):
            cols = slice(part * LO, (part + 1) * LO)
            values = []
            for c in range(3):
                value = arrived(c, cols)
                if there is not True:
                    value = jnp.where(there, value, 0.0)
                values += list(halves(value))
            left, right = one_hot_sum(shared[0, pl.ds(face, 1), cols], values, LO)
            product = lax.dot_general(
                left, right, (((1,), (1,)), ((), ())), preferred_element_type=f32
            )
            total = product if total is None else total + product
    for c in range(3):
        at = 2 * c * HI
        whole = own[c * HI : (c + 1) * HI, :] + total[at : at + HI] + total[at + HI : at + 2 * HI]
        for r in range(36):
            out[c : c + 1, r * LO : (r + 1) * LO] = whole[r : r + 1]
    out[...] = (external[...] - out[...]) / mass[...]


def assemble(place, own, shared, inner, outer, external, mass):
    vmem = pl.BlockSpec(memory_space=VMEM)
    return pl.pallas_call(
        assemble_kernel,
        out_shape=jax.ShapeDtypeStruct(external.shape, f32),
        in_specs=[pl.BlockSpec(memory_space=SMEM)] * 2 + [vmem] * 6,
        out_specs=vmem,
        compiler_params=pltpu.CompilerParams(vmem_limit_bytes=32 << 20),
        name="assemble",
    )(*place, own, shared, inner, outer, external, mass)


def sort_kernel(pieces, out, order, places, sem):
    blocks = pieces.shape[0] // 9
    lane = lax.broadcasted_iota(jnp.int32, (blocks, LANES), 1)
    block = lax.broadcasted_iota(jnp.int32, (blocks, LANES), 0)
    hit = pieces[pl.ds(8, blocks, stride=9), :] == lane.astype(f32)
    order[0:1, :] = jnp.min(jnp.where(hit, block, blocks - 1), axis=0, keepdims=True)
    order[1:2, :] = jnp.max(jnp.where(hit, block, 0), axis=0, keepdims=True)
    copy = pltpu.make_async_copy(order, places, sem)
    copy.start()
    copy.wait()
    for b in range(out.shape[0]):
        for s in range(2):
            out[b, s] = pieces[pl.ds(9 * places[s, b], 8), :]


def sort_pieces(pieces, bricks):
    vmem = pl.BlockSpec(memory_space=VMEM)
    return pl.pallas_call(
        sort_kernel,
        out_shape=jax.ShapeDtypeStruct((bricks, 2, 8, LANES), f32),
        in_specs=[vmem],
        out_specs=vmem,
        scratch_shapes=[VMEM((8, LANES), jnp.int32), SMEM((8, LANES), jnp.int32), pltpu.SemaphoreType.DMA],
        compiler_params=pltpu.CompilerParams(vmem_limit_bytes=32 << 20),
        name="sort_pieces",
    )(pieces)


def join_kernel(pieces, out):
    for i in range(TILES):
        for s in range(2):
            out[s, :, i * LANES : (i + 1) * LANES] = pieces[i, s]


def join_pieces(pieces):
    vmem = pl.BlockSpec(memory_space=VMEM)
    return pl.pallas_call(
        join_kernel,
        out_shape=jax.ShapeDtypeStruct((2, 8, NV), f32),
        in_specs=[vmem],
        out_specs=vmem,
        name="join_pieces",
    )(pieces)


def shards(
    displacement,
    node_map,
    shape_grads,
    volumes,
    elastic_moduli,
    external_force,
    nodal_mass,
    shared_nodes,
    band_count,
    band_owner,
    band_element,
    micro_fields,
):
    bricks, pools = lax.axis_size(BRICK), lax.axis_size("pool")
    place = tuple(lax.axis_index(axis).astype(jnp.int32).reshape(1) for axis in ("core", "pool"))
    send, band_stress = solve_cells(
        band_count,
        band_owner,
        band_element,
        displacement,
        node_map,
        shape_grads,
        micro_fields,
        jnp.asarray(green_table()),
        jnp.asarray(plane_tables()),
    )
    pieces = lax.all_to_all(
        send.reshape(bricks * pools, 1, 9 * LANES), BOTH, split_axis=0, concat_axis=0, tiled=True
    )
    sparse = (band_count, band_element, band_stress)
    dense = (displacement, node_map, shape_grads, volumes.reshape(64, LANES), elastic_moduli)
    so_far = macro_first(*sparse, *dense)
    pieces, so_far = lax.optimization_barrier((pieces, so_far))
    sorted_pieces = sort_pieces(pieces.reshape(9 * bricks * pools, LANES), bricks)
    sorted_pieces, so_far = lax.optimization_barrier((sorted_pieces, so_far))
    mine = lax.all_to_all(sorted_pieces, BRICK, split_axis=0, concat_axis=0, tiled=True)
    own, inner, outer = macro_last(pools, *sparse, *place, *dense, so_far, shared_nodes)
    inner = lax.all_to_all(inner, ("core", "pool"), split_axis=0, concat_axis=0, tiled=True)
    steps = [(i, i + 1) for i in range(1, bricks - 1, 2)]
    outer = lax.ppermute(outer, BRICK, steps + [(j, i) for i, j in steps])
    owned_fields = join_pieces(mine)
    inner, outer, owned_fields = lax.optimization_barrier((inner, outer, owned_fields))
    acceleration = assemble(
        place, own, shared_nodes, inner, outer, external_force, nodal_mass.reshape(1, -1)
    )
    return (acceleration, band_stress, owned_fields)


def solution(mesh):
    bricks, pools = mesh.devices.shape
    split = jax.sharding.Mesh(
        mesh.devices.reshape(4, bricks // 8, 2, pools), ("row", "pair", "core", "pool")
    )
    placed = (
        P(None, BOTH),
        P(None, BOTH),
        P(None, None, BOTH),
        P(BOTH),
        P(None, BOTH),
        P(None, BOTH),
        P(BOTH),
        P(BOTH, None, None),
        P(BOTH),
        P(BOTH, None),
        P(BOTH, None),
        P(BOTH, None, None),
    )
    return jax.shard_map(
        shards,
        mesh=split,
        in_specs=placed,
        out_specs=(P(None, BOTH), P(None, BOTH), P(BOTH, None, None)),
        check_vma=False,
    )
```

```python
import functools
import math

import jax
import jax.numpy as jnp
import numpy as np
from jax import lax
from jax.experimental import pallas as pl
from jax.experimental.pallas import tpu as pltpu
from jax.sharding import PartitionSpec as P

G = 16
NV = 4096
ITERS = 2
LANES = 128
TILES = 32
HI = 40
LO = 256
STEPS = float((1 << 20) - 2)
OFFSET = 1 << 20
UNROLL = 4
SPLIT = 48
BRICK = ("row", "pair", "core")
BOTH = BRICK + ("pool",)
VMEM = pltpu.VMEM
SMEM = pltpu.SMEM
f32 = jnp.float32
bf16 = jnp.bfloat16

ref_lambda = 5.5
ref_shear = 5.5


def green_table():
    index = np.arange(G)

    def operator(ix, iy, iz):
        wave = [np.where(2 * m < G, m, m - G).astype(np.float64) for m in (ix, iy, iz)]
        kx, ky, kz = np.broadcast_arrays(wave[0], wave[1], wave[2])
        square = kx * kx + ky * ky + kz * kz
        safe = np.where(square > 0, square, 1.0)
        first = np.where(square > 0, 1.0 / (2.0 * ref_shear * safe), 0.0)
        factor = (ref_lambda + ref_shear) / (ref_shear * (ref_lambda + 2.0 * ref_shear))
        second = np.where(square > 0, factor / (safe * safe), 0.0)
        zero, one = np.zeros_like(kx), np.ones_like(kx)
        columns = []
        for j in range(6):
            xx, yy, zz, yz, xz, xy = [one if j == c else zero for c in range(6)]
            wx = xx * kx + xy * ky + xz * kz
            wy = xy * kx + yy * ky + yz * kz
            wz = xz * kx + yz * ky + zz * kz
            s = (wx * kx + wy * ky + wz * kz) * second
            columns.append(
                np.stack(
                    [
                        first * 2 * kx * wx - s * kx * kx,
                        first * 2 * ky * wy - s * ky * ky,
                        first * 2 * kz * wz - s * kz * kz,
                        first * (ky * wz + kz * wy) - s * ky * kz,
                        first * (kx * wz + kz * wx) - s * kx * kz,
                        first * (kx * wy + ky * wx) - s * kx * ky,
                        zero,
                        zero,
                    ]
                )
            )
        return np.stack(columns)

    ix, iy, iz = index[:, None, None], index[None, :, None], index[None, None, :]
    table = 0.5 * (operator(ix, iy, iz) + operator((-ix) % G, (-iy) % G, (-iz) % G)) / NV
    table = table.reshape(6, 8, G, G * G).transpose(2, 0, 1, 3)
    pairs, alone = half_plane()
    even, odd = np.concatenate([pairs, alone[:2]]), np.concatenate([pairs, alone[2:]])
    return np.stack([table[..., even], table[..., odd]]).astype(np.float32)


def half_plane():
    index = np.arange(G * G)
    mirror = (-(index // G)) % G * G + (-(index % G)) % G
    return index[index < mirror], index[index == mirror]


def plane_tables():
    pairs, alone = half_plane()
    plane = np.arange(G * G)

    def angle(k):
        turns = (plane[:, None] // G * (k // G)[None, :] + plane[:, None] % G * (k % G)[None, :]) % G
        return turns * (2 * np.pi / G)

    there = np.concatenate(
        [
            np.cos(angle(pairs)),
            np.cos(angle(alone[:2])),
            -np.sin(angle(pairs)),
            np.cos(angle(alone[2:])),
        ],
        axis=1,
    )
    weight = np.full((G * G, 1), 2.0)
    weight[[126, 127, 254, 255]] = 1.0
    parts = []
    for table in (there, weight * there.T):
        high = table.astype(np.float32).astype(bf16)
        parts += [high, (table - high.astype(np.float64)).astype(np.float32).astype(bf16)]
    return np.stack(parts)


def twiddle(value, power, sign):
    re, im = value
    power %= 16
    if power == 0:
        return re, im
    if power == 4:
        return (-im, re) if sign > 0 else (im, -re)
    if power == 8:
        return -re, -im
    if power == 12:
        return (im, -re) if sign > 0 else (-im, re)
    angle = sign * 2 * math.pi * power / 16
    c, s = math.cos(angle), math.sin(angle)
    if power % 4 == 2:
        h = abs(c)
        a = re if c > 0 else -re
        b = im if c > 0 else -im
        if c * s > 0:
            return (a - b) * h, (a + b) * h
        return (a + b) * h, (b - a) * h
    return re * c - im * s, re * s + im * c


def dft4(v, sign):
    (ar, ai), (br, bi), (cr, ci), (dr, di) = v
    pr, pi_ = ar + cr, ai + ci
    mr, mi = ar - cr, ai - ci
    qr, qi = br + dr, bi + di
    nr, ni = br - dr, bi - di
    if sign < 0:
        jr, ji = ni, -nr
    else:
        jr, ji = -ni, nr
    return [(pr + qr, pi_ + qi), (mr + jr, mi + ji), (pr - qr, pi_ - qi), (mr - jr, mi - ji)]


def dft16(values, sign):
    inner = []
    for n2 in range(4):
        inner.append(dft4([values[n2 + 4 * n1] for n1 in range(4)], sign))
    out = [None] * 16
    for k1 in range(4):
        column = dft4([twiddle(inner[n2][k1], n2 * k1, sign) for n2 in range(4)], sign)
        for k2 in range(4):
            out[k1 + 4 * k2] = column[k2]
    return out


def slab_stress(d, first_rows):
    wide = d.shape
    trace = d[0:1] + d[1:2] + d[2:3]
    lam_trace = jnp.broadcast_to(d[6:7] * trace, wide)
    twice = jnp.broadcast_to(2.0 * d[7:8], wide)
    return twice * d + jnp.where(first_rows, lam_trace, 0.0)


def plane_product(x, cmat, at):
    high = x.astype(bf16)
    low = (x - high.astype(f32)).astype(bf16)
    rows = x.shape[0]
    both = jnp.dot(jnp.concatenate([high, low], axis=0), cmat[at], preferred_element_type=f32)
    return both[:rows] + both[rows:] + jnp.dot(high, cmat[at + 1], preferred_element_type=f32)


def cells_kernel(
    count, owner, element, disp, nm, grads, micro, green, cmat, send, band_stress, replace, st, *work
):
    half_rows = 8 * G
    lane = lax.broadcasted_iota(jnp.int32, (8, LANES), 1)
    row = lax.broadcasted_iota(jnp.int32, (8, LANES), 0)
    row_wide = lax.broadcasted_iota(jnp.int32, (8, 2 * LANES), 0)
    first_rows = row_wide < 3

    targets = []
    for k in range(4):
        e = element[0, k]
        base = pl.multiple_of(e // LANES * LANES, LANES)
        at = lane == e % LANES

        def pick(tile):
            return jnp.sum(jnp.where(at, tile, 0.0), axis=1, keepdims=True)

        node = pick(nm[:, pl.ds(base, LANES)].astype(f32)).astype(jnp.int32)
        shape = [jnp.broadcast_to(pick(grads[j, :, pl.ds(base, LANES)]), (8, LANES)) for j in range(3)]
        node = jnp.broadcast_to(node, (8, LANES)) - lane
        found = [jnp.zeros((8, LANES), f32) for _ in range(3)]
        for r in range(72):
            hit = node == r * LANES
            for c in range(3):
                values = jnp.broadcast_to(disp[c : c + 1, r * LANES : (r + 1) * LANES], (8, LANES))
                found[c] = jnp.where(hit, values, found[c])
        u = [jnp.sum(found[c], axis=1, keepdims=True) for c in range(3)]

        def total(value):
            return jnp.sum(value, axis=0, keepdims=True)

        parts = [
            total(u[0] * shape[0]),
            total(u[1] * shape[1]),
            total(u[2] * shape[2]),
            0.5 * total(u[1] * shape[2] + u[2] * shape[1]),
            0.5 * total(u[0] * shape[2] + u[2] * shape[0]),
            0.5 * total(u[0] * shape[1] + u[1] * shape[0]),
        ]
        target = jnp.zeros((8, LANES), f32)
        for c in range(6):
            target = jnp.where(row == c, jnp.broadcast_to(parts[c], (8, LANES)), target)
        targets.append(target)

    def slab(k, x, iteration):
        if iteration == 0:
            return micro[k, :, 2 * LANES * x : 2 * LANES * (x + 1)]
        return st[k, 8 * x : 8 * x + 8, :]

    shifts = []
    for k in range(4):
        total = jnp.zeros((8, 2 * LANES), f32)
        for x in range(G):
            total = total + slab(k, x, 0)
        mean = jnp.sum(total, axis=1, keepdims=True) * (1.0 / NV)
        shift = jnp.where(row < 6, targets[k] - mean, 0.0)
        shifts.append(jnp.concatenate([shift, shift], axis=1))

    re_cols, im_cols = slice(0, LANES), slice(LANES, 2 * LANES)
    own_mirror = lane >= 126
    whole_mirror = lax.broadcasted_iota(jnp.int32, (half_rows, LANES), 1) >= 126
    for iteration in range(ITERS):
        for pair in range(2):
            plane, spectrum = work[2 * pair], work[2 * pair + 1]
            at = [[cell * half_rows + 8 * x for x in range(G)] for cell in range(2)]
            for cell in range(2):
                for x in range(G):
                    a = at[cell][x]
                    plane[a : a + 8, :] = slab_stress(slab(2 * pair + cell, x, iteration), first_rows)
            plane[...] = plane_product(plane[...], cmat, 0)
            for cell in range(2):
                values = []
                for x in range(G):
                    a = at[cell][x]
                    re, im = plane[a : a + 8, re_cols], plane[a : a + 8, im_cols]
                    if cell == 0:
                        other = at[1][x]
                        im = jnp.where(own_mirror, plane[other : other + 8, re_cols], im)
                    else:
                        other = at[0][x]
                        re = jnp.where(own_mirror, plane[other : other + 8, im_cols], re)
                    values.append((re, im))
                values = dft16(values, -1)
                for x in range(G):
                    a = at[cell][x]
                    spectrum[a : a + 8, re_cols] = values[x][0]
                    spectrum[a : a + 8, im_cols] = values[x][1]
            for cell in range(2):
                updates = []
                for x in range(G):
                    re = im = None
                    for j in range(6):
                        weight = green[cell, x, j]
                        a = at[cell][x] + j
                        tr = weight * jnp.broadcast_to(spectrum[a : a + 1, re_cols], (8, LANES))
                        ti = weight * jnp.broadcast_to(spectrum[a : a + 1, im_cols], (8, LANES))
                        re = tr if re is None else re + tr
                        im = ti if im is None else im + ti
                    updates.append((re, im))
                values = dft16(updates, 1)
                for x in range(G):
                    a = at[cell][x]
                    plane[a : a + 8, re_cols] = values[x][0]
                    plane[a : a + 8, im_cols] = values[x][1]
            first_im = plane[:half_rows, im_cols]
            second_re = plane[half_rows:, re_cols]
            plane[:half_rows, im_cols] = jnp.where(whole_mirror, second_re, first_im)
            plane[half_rows:, re_cols] = jnp.where(whole_mirror, first_im, second_re)
            update = plane_product(plane[...], cmat, 2)
            for cell in range(2):
                k = 2 * pair + cell
                for x in range(G):
                    a = at[cell][x]
                    value = slab(k, x, iteration) - update[a : a + 8, :]
                    if iteration == 0:
                        value = value + shifts[k]
                    st[k, 8 * x : 8 * x + 8, :] = value

    send[pl.ds(8, 4 * TILES, stride=9), :] = jnp.full((4 * TILES, LANES), -1.0, f32)
    result = jnp.zeros((8, LANES), f32)
    for k in range(4):
        live = k < count[0]
        total = jnp.zeros((8, 2 * LANES), f32)
        for x in range(G):
            total = total + slab_stress(st[k, 8 * x : 8 * x + 8, :], first_rows)
        mean = jnp.sum(total, axis=1, keepdims=True) * (1.0 / NV)
        result = jnp.where((lane == k) & live, jnp.broadcast_to(mean, (8, LANES)), result)
        pool = owner[0, k] & 3

        @pl.when(live)
        def _():
            for i in range(TILES):
                x, part = i // 2, i % 2
                send[pl.ds(9 * (4 * i + pool), 8), :] = st[
                    k, 8 * x : 8 * x + 8, part * LANES : (part + 1) * LANES
                ]
            brick = (owner[0, k] >> 2).astype(f32)
            send[pl.ds(9 * pool + 8, TILES, stride=36), :] = jnp.full((TILES, LANES), brick, f32)

    band_stress[...] = result[0:6, 0:4]
    for k in range(4):
        live_element = jnp.where(k < count[0], element[0, k], -1).astype(f32)
        result = jnp.where((lane == k) & (row == 6), live_element, result)
    replace[...] = result[:, 0:4]


def solve_cells(count, owner, element, disp, nm, grads, micro, green, cmat):
    return pl.pallas_call(
        cells_kernel,
        out_shape=(
            jax.ShapeDtypeStruct((36 * TILES, LANES), f32),
            jax.ShapeDtypeStruct((6, 4), f32),
            jax.ShapeDtypeStruct((8, 4), f32),
        ),
        in_specs=[pl.BlockSpec(memory_space=SMEM)] * 3 + [pl.BlockSpec(memory_space=VMEM)] * 6,
        out_specs=(pl.BlockSpec(memory_space=VMEM),) * 3,
        scratch_shapes=[
            VMEM((4, 8 * G, 2 * LANES), f32),
        ]
        + [VMEM((16 * G, 2 * LANES), f32)] * 4,
        compiler_params=pltpu.CompilerParams(vmem_limit_bytes=56 << 20),
        name="cells",
    )(count, owner, element, disp, nm, grads, micro, green, cmat)


def one_hot_sum(node, values, width):
    hi = jnp.broadcast_to(node >> 8, (HI, width))
    lo = jnp.broadcast_to(node & 255, (LO, width))
    coarse = lax.broadcasted_iota(jnp.int32, (HI, width), 0) == hi
    fine = lax.broadcasted_iota(jnp.int32, (LO, width), 0) == lo
    left = jnp.concatenate(
        [jnp.where(coarse, jnp.broadcast_to(v, (HI, width)), 0.0) for v in values], axis=0
    ).astype(bf16)
    right = jnp.where(fine, 1.0, 0.0).astype(bf16)
    return left, right


def halves(value):
    high = value.astype(bf16).astype(f32)
    return high, value - high


def pack_table(disp, table, step):
    largest = jnp.zeros((3, LANES), f32)
    for r in range(72):
        largest = jnp.maximum(largest, jnp.abs(disp[:, r * LANES : (r + 1) * LANES]))
    largest = jnp.maximum(jnp.max(largest, axis=0, keepdims=True), 1e-30)
    step[...] = largest * (1.0 / STEPS)
    scale = jnp.broadcast_to(STEPS / largest, (3, LANES))
    for r in range(72):
        cols = slice(r * LANES, (r + 1) * LANES)
        level = jnp.floor(disp[:, cols] * scale + (OFFSET + 0.5)).astype(jnp.int32)
        last = level[2:3]
        parts = jnp.concatenate([(last & 0x7FF) << 21, (last >> 11) << 21], axis=0)
        table[:, cols] = level[0:2] | parts


def unpack(first, second, step):
    mask = (1 << 21) - 1
    last = lax.shift_right_logical(first, 21) | (lax.shift_right_logical(second, 21) << 11)
    return [(level - OFFSET).astype(f32) * step for level in (first & mask, second & mask, last)]


def macro_tiles(begin, end, unroll, replace, table, step_of, nm, grads, volumes, moduli, sums):
    lane = lax.broadcasted_iota(jnp.int32, (1, LANES), 1).astype(f32)
    steps = jnp.broadcast_to(step_of[...], (8, LANES))

    def scatter(node, forces):
        values = []
        for force in forces:
            values += list(halves(force))
        total = None
        for s in range(0, 8, 2):
            lefts, rights = [], []
            for q in (s, s + 1):
                left, right = one_hot_sum(node[q : q + 1], [v[q : q + 1] for v in values], LANES)
                lefts.append(left)
                rights.append(right)
            product = lax.dot_general(
                jnp.concatenate(lefts, axis=1),
                jnp.concatenate(rights, axis=1),
                (((1,), (1,)), ((), ())),
                preferred_element_type=f32,
            )
            total = product if total is None else total + product
        return total

    def forces_of(t):
        cols = pl.ds(pl.multiple_of(t * LANES, LANES), LANES)
        node = nm[:, cols]
        hi, lo = node >> 7, node & 127
        words = [jnp.zeros((8, LANES), jnp.int32) for _ in range(2)]
        for r in range(72):
            hit = hi == r
            for w in range(2):
                values = jnp.broadcast_to(table[w : w + 1, r * LANES : (r + 1) * LANES], (8, LANES))
                found = jnp.take_along_axis(values, lo, axis=1, mode="promise_in_bounds")
                words[w] = jnp.where(hit, found, words[w])
        u = unpack(*words, jnp.take_along_axis(steps, lo, axis=1, mode="promise_in_bounds"))
        g = [grads[j, :, cols] for j in range(3)]

        def total(value):
            return jnp.sum(value, axis=0, keepdims=True)

        strain = [
            total(u[0] * g[0]),
            total(u[1] * g[1]),
            total(u[2] * g[2]),
            0.5 * total(u[1] * g[2] + u[2] * g[1]),
            0.5 * total(u[0] * g[2] + u[2] * g[0]),
            0.5 * total(u[0] * g[1] + u[1] * g[0]),
        ]
        lam = moduli[0:1, cols]
        mu = moduli[1:2, cols]
        volume = volumes[pl.ds(t, 1), :]
        spherical = lam * (strain[0] + strain[1] + strain[2])
        stress = [spherical + 2.0 * mu * strain[c] for c in range(3)]
        stress += [2.0 * mu * strain[c] for c in range(3, 6)]
        for k in range(4):
            hit = lane == replace[6, k] - lax.convert_element_type(t * LANES, f32)
            stress = [jnp.where(hit, replace[c, k], stress[c]) for c in range(6)]
        xx, yy, zz, yz, xz, xy = [
            jnp.broadcast_to(component * volume, (8, LANES)) for component in stress
        ]
        fx = xx * g[0] + xy * g[1] + xz * g[2]
        fy = xy * g[0] + yy * g[1] + yz * g[2]
        fz = xz * g[0] + yz * g[1] + zz * g[2]
        return node, fx, fy, fz

    def group(step):
        return tuple(forces_of(begin + step * unroll + i) for i in range(unroll))

    def add(carry):
        total = None
        for node, *forces in carry:
            part = scatter(node, forces)
            total = part if total is None else total + part
        sums[...] += total

    def body(step, carry):
        add(carry)
        return group(step)

    add(lax.fori_loop(1, (end - begin) // unroll, body, group(0)))


def macro_first_kernel(unroll, replace, disp, nm, grads, volumes, moduli, sums, table, step):
    pack_table(disp, table, step)
    sums[...] = jnp.zeros_like(sums)
    macro_tiles(0, SPLIT, unroll, replace, table, step, nm, grads, volumes, moduli, sums)


def macro_last_kernel(
    unroll,
    replace,
    core_index,
    pool_index,
    table,
    step,
    nm,
    grads,
    volumes,
    moduli,
    so_far,
    shared,
    own,
    inner,
    outer,
    sums,
    faces,
):
    sums[...] = so_far[...]
    macro_tiles(SPLIT, 64, unroll, replace, table, step, nm, grads, volumes, moduli, sums)

    for c in range(3):
        at = 2 * c * HI
        own[c * HI : (c + 1) * HI, :] = sums[at : at + HI, :] + sums[at + HI : at + 2 * HI, :]

    for pair in range(4):
        first, second = 2 * pair, 2 * pair + 1
        node = jnp.concatenate(
            [
                shared[0, :, first * LANES : (first + 1) * LANES],
                shared[0, :, second * LANES : (second + 1) * LANES],
            ],
            axis=0,
        )
        hi, lo = node >> 7, node & 127
        picked = [jnp.zeros((8, LANES), f32) for _ in range(3)]
        for r in range(72):
            hit = hi == r
            for c in range(3):
                at = c * HI + r // 2
                cols = slice(r % 2 * LANES, (r % 2 + 1) * LANES)
                values = jnp.broadcast_to(own[at : at + 1, cols], (8, LANES))
                found = jnp.take_along_axis(values, lo, axis=1, mode="promise_in_bounds")
                picked[c] = jnp.where(hit, found, picked[c])
        for c in range(3):
            for face in range(4):
                faces[face, c : c + 1, first * LANES : (first + 1) * LANES] = picked[c][face : face + 1]
                faces[face, c : c + 1, second * LANES : (second + 1) * LANES] = picked[c][
                    4 + face : 5 + face
                ]
    core, pool = core_index[0], pool_index[0]
    pools = inner.shape[0] // 2
    inner[...] = jnp.zeros_like(inner)
    inner[(1 - core) * pools + pool] = faces[1 - core]
    outer[...] = faces[core]

    @pl.when(pool > 0)
    def _():
        inner[core * pools + pool - 1] = faces[2]

    @pl.when(pool < pools - 1)
    def _():
        inner[core * pools + pool + 1] = faces[3]


def macro_first(*arguments):
    vmem = pl.BlockSpec(memory_space=VMEM)
    return pl.pallas_call(
        functools.partial(macro_first_kernel, UNROLL),
        out_shape=(
            jax.ShapeDtypeStruct((6 * HI, LO), f32),
            jax.ShapeDtypeStruct((2, 72 * LANES), jnp.int32),
            jax.ShapeDtypeStruct((1, LANES), f32),
        ),
        in_specs=[pl.BlockSpec(memory_space=SMEM)] + [vmem] * 5,
        out_specs=(vmem,) * 3,
        compiler_params=pltpu.CompilerParams(vmem_limit_bytes=32 << 20),
        name="macro_first",
    )(*arguments)


def macro_last(pools, *arguments):
    vmem = pl.BlockSpec(memory_space=VMEM)
    return pl.pallas_call(
        functools.partial(macro_last_kernel, UNROLL),
        out_shape=(
            jax.ShapeDtypeStruct((3 * HI, LO), f32),
            jax.ShapeDtypeStruct((2 * pools, 3, 1024), f32),
            jax.ShapeDtypeStruct((3, 1024), f32),
        ),
        in_specs=[pl.BlockSpec(memory_space=SMEM)] * 3 + [vmem] * 8,
        out_specs=(vmem,) * 3,
        scratch_shapes=[VMEM((6 * HI, LO), f32), VMEM((4, 3, 1024), f32)],
        compiler_params=pltpu.CompilerParams(vmem_limit_bytes=32 << 20),
        name="macro_last",
    )(*arguments)


def assemble_kernel(core_index, pool_index, own, shared, inner, outer, external, mass, out):
    core, pool = core_index[0], pool_index[0]
    pools = inner.shape[0] // 2
    below, above = jnp.maximum(pool - 1, 0), jnp.minimum(pool + 1, pools - 1)
    arrivals = (
        (1 - core, True, lambda c, cols: inner[(1 - core) * pools + pool, c : c + 1, cols]),
        (core, True, lambda c, cols: outer[c : c + 1, cols]),
        (2, pool > 0, lambda c, cols: inner[core * pools + below, c : c + 1, cols]),
        (3, pool < pools - 1, lambda c, cols: inner[core * pools + above, c : c + 1, cols]),
    )
    total = None
    for face, there, arrived in arrivals:
        for part in range(4):
            cols = slice(part * LO, (part + 1) * LO)
            values = []
            for c in range(3):
                value = arrived(c, cols)
                if there is not True:
                    value = jnp.where(there, value, 0.0)
                values += list(halves(value))
            left, right = one_hot_sum(shared[0, pl.ds(face, 1), cols], values, LO)
            product = lax.dot_general(
                left, right, (((1,), (1,)), ((), ())), preferred_element_type=f32
            )
            total = product if total is None else total + product
    for c in range(3):
        at = 2 * c * HI
        whole = own[c * HI : (c + 1) * HI, :] + total[at : at + HI] + total[at + HI : at + 2 * HI]
        for r in range(36):
            out[c : c + 1, r * LO : (r + 1) * LO] = whole[r : r + 1]
    out[...] = (external[...] - out[...]) / mass[...]


def assemble(place, own, shared, inner, outer, external, mass):
    vmem = pl.BlockSpec(memory_space=VMEM)
    return pl.pallas_call(
        assemble_kernel,
        out_shape=jax.ShapeDtypeStruct(external.shape, f32),
        in_specs=[pl.BlockSpec(memory_space=SMEM)] * 2 + [vmem] * 6,
        out_specs=vmem,
        compiler_params=pltpu.CompilerParams(vmem_limit_bytes=32 << 20),
        name="assemble",
    )(*place, own, shared, inner, outer, external, mass)


def sort_kernel(pieces, out, order, places, sem):
    blocks = pieces.shape[0] // 9
    lane = lax.broadcasted_iota(jnp.int32, (blocks, LANES), 1)
    block = lax.broadcasted_iota(jnp.int32, (blocks, LANES), 0)
    hit = pieces[pl.ds(8, blocks, stride=9), :] == lane.astype(f32)
    order[0:1, :] = jnp.min(jnp.where(hit, block, blocks - 1), axis=0, keepdims=True)
    order[1:2, :] = jnp.max(jnp.where(hit, block, 0), axis=0, keepdims=True)
    copy = pltpu.make_async_copy(order, places, sem)
    copy.start()
    copy.wait()
    for b in range(out.shape[0]):
        for s in range(2):
            out[b, s] = pieces[pl.ds(9 * places[s, b], 8), :]


def sort_pieces(pieces, bricks):
    vmem = pl.BlockSpec(memory_space=VMEM)
    return pl.pallas_call(
        sort_kernel,
        out_shape=jax.ShapeDtypeStruct((bricks, 2, 8, LANES), f32),
        in_specs=[vmem],
        out_specs=vmem,
        scratch_shapes=[VMEM((8, LANES), jnp.int32), SMEM((8, LANES), jnp.int32), pltpu.SemaphoreType.DMA],
        compiler_params=pltpu.CompilerParams(vmem_limit_bytes=32 << 20),
        name="sort_pieces",
    )(pieces)


def join_kernel(pieces, out):
    for i in range(TILES):
        for s in range(2):
            out[s, :, i * LANES : (i + 1) * LANES] = pieces[i, s]


def join_pieces(pieces):
    vmem = pl.BlockSpec(memory_space=VMEM)
    return pl.pallas_call(
        join_kernel,
        out_shape=jax.ShapeDtypeStruct((2, 8, NV), f32),
        in_specs=[vmem],
        out_specs=vmem,
        name="join_pieces",
    )(pieces)


def shards(
    displacement,
    node_map,
    shape_grads,
    volumes,
    elastic_moduli,
    external_force,
    nodal_mass,
    shared_nodes,
    band_count,
    band_owner,
    band_element,
    micro_fields,
):
    bricks, pools = lax.axis_size(BRICK), lax.axis_size("pool")
    place = tuple(lax.axis_index(axis).astype(jnp.int32).reshape(1) for axis in ("core", "pool"))
    send, band_stress, replace = solve_cells(
        band_count,
        band_owner,
        band_element,
        displacement,
        node_map,
        shape_grads,
        micro_fields,
        jnp.asarray(green_table()),
        jnp.asarray(plane_tables()),
    )
    pieces = lax.all_to_all(
        send.reshape(bricks * pools, 1, 9 * LANES), BOTH, split_axis=0, concat_axis=0, tiled=True
    )
    dense = (node_map, shape_grads, volumes.reshape(64, LANES), elastic_moduli)
    so_far, table, step = macro_first(replace, displacement, *dense)
    pieces, so_far = lax.optimization_barrier((pieces, so_far))
    sorted_pieces = sort_pieces(pieces.reshape(9 * bricks * pools, LANES), bricks)
    sorted_pieces, so_far = lax.optimization_barrier((sorted_pieces, so_far))
    mine = lax.all_to_all(sorted_pieces, BRICK, split_axis=0, concat_axis=0, tiled=True)
    own, inner, outer = macro_last(pools, replace, *place, table, step, *dense, so_far, shared_nodes)
    inner = lax.all_to_all(inner, ("core", "pool"), split_axis=0, concat_axis=0, tiled=True)
    steps = [(i, i + 1) for i in range(1, bricks - 1, 2)]
    outer = lax.ppermute(outer, BRICK, steps + [(j, i) for i, j in steps])
    owned_fields = join_pieces(mine)
    inner, outer, owned_fields = lax.optimization_barrier((inner, outer, owned_fields))
    acceleration = assemble(
        place, own, shared_nodes, inner, outer, external_force, nodal_mass.reshape(1, -1)
    )
    return (acceleration, band_stress, owned_fields)


def solution(mesh):
    bricks, pools = mesh.devices.shape
    split = jax.sharding.Mesh(
        mesh.devices.reshape(4, bricks // 8, 2, pools), ("row", "pair", "core", "pool")
    )
    placed = (
        P(None, BOTH),
        P(None, BOTH),
        P(None, None, BOTH),
        P(BOTH),
        P(None, BOTH),
        P(None, BOTH),
        P(BOTH),
        P(BOTH, None, None),
        P(BOTH),
        P(BOTH, None),
        P(BOTH, None),
        P(BOTH, None, None),
    )
    return jax.shard_map(
        shards,
        mesh=split,
        in_specs=placed,
        out_specs=(P(None, BOTH), P(None, BOTH), P(BOTH, None, None)),
        check_vma=False,
    )
```

```python
import functools
import math

import jax
import jax.numpy as jnp
import numpy as np
from jax import lax
from jax.experimental import pallas as pl
from jax.experimental.pallas import tpu as pltpu
from jax.sharding import PartitionSpec as P

G = 16
NV = 4096
ITERS = 2
LANES = 128
TILES = 32
HI = 48
LO = 256
STEPS = float((1 << 20) - 2)
OFFSET = 1 << 20
UNROLL = 4
SPLIT = 48
BRICK = ("row", "pair", "core")
BOTH = BRICK + ("pool",)
VMEM = pltpu.VMEM
SMEM = pltpu.SMEM
f32 = jnp.float32
bf16 = jnp.bfloat16

ref_lambda = 5.5
ref_shear = 5.5


def green_table():
    index = np.arange(G)

    def operator(ix, iy, iz):
        wave = [np.where(2 * m < G, m, m - G).astype(np.float64) for m in (ix, iy, iz)]
        kx, ky, kz = np.broadcast_arrays(wave[0], wave[1], wave[2])
        square = kx * kx + ky * ky + kz * kz
        safe = np.where(square > 0, square, 1.0)
        first = np.where(square > 0, 1.0 / (2.0 * ref_shear * safe), 0.0)
        factor = (ref_lambda + ref_shear) / (ref_shear * (ref_lambda + 2.0 * ref_shear))
        second = np.where(square > 0, factor / (safe * safe), 0.0)
        zero, one = np.zeros_like(kx), np.ones_like(kx)
        columns = []
        for j in range(6):
            xx, yy, zz, yz, xz, xy = [one if j == c else zero for c in range(6)]
            wx = xx * kx + xy * ky + xz * kz
            wy = xy * kx + yy * ky + yz * kz
            wz = xz * kx + yz * ky + zz * kz
            s = (wx * kx + wy * ky + wz * kz) * second
            columns.append(
                np.stack(
                    [
                        first * 2 * kx * wx - s * kx * kx,
                        first * 2 * ky * wy - s * ky * ky,
                        first * 2 * kz * wz - s * kz * kz,
                        first * (ky * wz + kz * wy) - s * ky * kz,
                        first * (kx * wz + kz * wx) - s * kx * kz,
                        first * (kx * wy + ky * wx) - s * kx * ky,
                        zero,
                        zero,
                    ]
                )
            )
        return np.stack(columns)

    ix, iy, iz = index[:, None, None], index[None, :, None], index[None, None, :]
    table = 0.5 * (operator(ix, iy, iz) + operator((-ix) % G, (-iy) % G, (-iz) % G)) / NV
    table = table.reshape(6, 8, G, G * G).transpose(2, 0, 1, 3)
    pairs, alone = half_plane()
    even, odd = np.concatenate([pairs, alone[:2]]), np.concatenate([pairs, alone[2:]])
    return np.stack([table[..., even], table[..., odd]]).astype(np.float32)


def half_plane():
    index = np.arange(G * G)
    mirror = (-(index // G)) % G * G + (-(index % G)) % G
    return index[index < mirror], index[index == mirror]


def plane_tables():
    pairs, alone = half_plane()
    plane = np.arange(G * G)

    def angle(k):
        turns = (plane[:, None] // G * (k // G)[None, :] + plane[:, None] % G * (k % G)[None, :]) % G
        return turns * (2 * np.pi / G)

    there = np.concatenate(
        [
            np.cos(angle(pairs)),
            np.cos(angle(alone[:2])),
            -np.sin(angle(pairs)),
            np.cos(angle(alone[2:])),
        ],
        axis=1,
    )
    weight = np.full((G * G, 1), 2.0)
    weight[[126, 127, 254, 255]] = 1.0
    parts = []
    for table in (there, weight * there.T):
        high = table.astype(np.float32).astype(bf16)
        parts += [high, (table - high.astype(np.float64)).astype(np.float32).astype(bf16)]
    return np.stack(parts)


def twiddle(value, power, sign):
    re, im = value
    power %= 16
    if power == 0:
        return re, im
    if power == 4:
        return (-im, re) if sign > 0 else (im, -re)
    if power == 8:
        return -re, -im
    if power == 12:
        return (im, -re) if sign > 0 else (-im, re)
    angle = sign * 2 * math.pi * power / 16
    c, s = math.cos(angle), math.sin(angle)
    if power % 4 == 2:
        h = abs(c)
        a = re if c > 0 else -re
        b = im if c > 0 else -im
        if c * s > 0:
            return (a - b) * h, (a + b) * h
        return (a + b) * h, (b - a) * h
    return re * c - im * s, re * s + im * c


def dft4(v, sign):
    (ar, ai), (br, bi), (cr, ci), (dr, di) = v
    pr, pi_ = ar + cr, ai + ci
    mr, mi = ar - cr, ai - ci
    qr, qi = br + dr, bi + di
    nr, ni = br - dr, bi - di
    if sign < 0:
        jr, ji = ni, -nr
    else:
        jr, ji = -ni, nr
    return [(pr + qr, pi_ + qi), (mr + jr, mi + ji), (pr - qr, pi_ - qi), (mr - jr, mi - ji)]


def dft16(values, sign):
    inner = []
    for n2 in range(4):
        inner.append(dft4([values[n2 + 4 * n1] for n1 in range(4)], sign))
    out = [None] * 16
    for k1 in range(4):
        column = dft4([twiddle(inner[n2][k1], n2 * k1, sign) for n2 in range(4)], sign)
        for k2 in range(4):
            out[k1 + 4 * k2] = column[k2]
    return out


def slab_stress(d, first_rows):
    wide = d.shape
    trace = d[0:1] + d[1:2] + d[2:3]
    lam_trace = jnp.broadcast_to(d[6:7] * trace, wide)
    twice = jnp.broadcast_to(2.0 * d[7:8], wide)
    return twice * d + jnp.where(first_rows, lam_trace, 0.0)


def plane_product(x, cmat, at):
    high = x.astype(bf16)
    low = (x - high.astype(f32)).astype(bf16)
    rows = x.shape[0]
    both = jnp.dot(jnp.concatenate([high, low], axis=0), cmat[at], preferred_element_type=f32)
    return both[:rows] + both[rows:] + jnp.dot(high, cmat[at + 1], preferred_element_type=f32)


def cells_kernel(
    count, owner, element, disp, nm, grads, micro, green, cmat, send, band_stress, replace, st, *work
):
    half_rows = 8 * G
    lane = lax.broadcasted_iota(jnp.int32, (8, LANES), 1)
    row = lax.broadcasted_iota(jnp.int32, (8, LANES), 0)
    row_wide = lax.broadcasted_iota(jnp.int32, (8, 2 * LANES), 0)
    first_rows = row_wide < 3

    targets = []
    for k in range(4):
        e = element[0, k]
        base = pl.multiple_of(e // LANES * LANES, LANES)
        at = lane == e % LANES

        def pick(tile):
            return jnp.sum(jnp.where(at, tile, 0.0), axis=1, keepdims=True)

        node = pick(nm[:, pl.ds(base, LANES)].astype(f32)).astype(jnp.int32)
        shape = [jnp.broadcast_to(pick(grads[j, :, pl.ds(base, LANES)]), (8, LANES)) for j in range(3)]
        node = jnp.broadcast_to(node, (8, LANES)) - lane
        found = [jnp.zeros((8, LANES), f32) for _ in range(3)]
        for r in range(72):
            hit = node == r * LANES
            for c in range(3):
                values = jnp.broadcast_to(disp[c : c + 1, r * LANES : (r + 1) * LANES], (8, LANES))
                found[c] = jnp.where(hit, values, found[c])
        u = [jnp.sum(found[c], axis=1, keepdims=True) for c in range(3)]

        def total(value):
            return jnp.sum(value, axis=0, keepdims=True)

        parts = [
            total(u[0] * shape[0]),
            total(u[1] * shape[1]),
            total(u[2] * shape[2]),
            0.5 * total(u[1] * shape[2] + u[2] * shape[1]),
            0.5 * total(u[0] * shape[2] + u[2] * shape[0]),
            0.5 * total(u[0] * shape[1] + u[1] * shape[0]),
        ]
        target = jnp.zeros((8, LANES), f32)
        for c in range(6):
            target = jnp.where(row == c, jnp.broadcast_to(parts[c], (8, LANES)), target)
        targets.append(target)

    def slab(k, x, iteration):
        if iteration == 0:
            return micro[k, :, 2 * LANES * x : 2 * LANES * (x + 1)]
        return st[k, 8 * x : 8 * x + 8, :]

    shifts = []
    for k in range(4):
        total = jnp.zeros((8, 2 * LANES), f32)
        for x in range(G):
            total = total + slab(k, x, 0)
        mean = jnp.sum(total, axis=1, keepdims=True) * (1.0 / NV)
        shift = jnp.where(row < 6, targets[k] - mean, 0.0)
        shifts.append(jnp.concatenate([shift, shift], axis=1))

    re_cols, im_cols = slice(0, LANES), slice(LANES, 2 * LANES)
    own_mirror = lane >= 126
    whole_mirror = lax.broadcasted_iota(jnp.int32, (half_rows, LANES), 1) >= 126
    for iteration in range(ITERS):
        for pair in range(2):
            plane, spectrum = work[2 * pair], work[2 * pair + 1]
            at = [[cell * half_rows + 8 * x for x in range(G)] for cell in range(2)]
            for cell in range(2):
                for x in range(G):
                    a = at[cell][x]
                    plane[a : a + 8, :] = slab_stress(slab(2 * pair + cell, x, iteration), first_rows)
            plane[...] = plane_product(plane[...], cmat, 0)
            for cell in range(2):
                values = []
                for x in range(G):
                    a = at[cell][x]
                    re, im = plane[a : a + 8, re_cols], plane[a : a + 8, im_cols]
                    if cell == 0:
                        other = at[1][x]
                        im = jnp.where(own_mirror, plane[other : other + 8, re_cols], im)
                    else:
                        other = at[0][x]
                        re = jnp.where(own_mirror, plane[other : other + 8, im_cols], re)
                    values.append((re, im))
                values = dft16(values, -1)
                for x in range(G):
                    a = at[cell][x]
                    spectrum[a : a + 8, re_cols] = values[x][0]
                    spectrum[a : a + 8, im_cols] = values[x][1]
            for cell in range(2):
                updates = []
                for x in range(G):
                    re = im = None
                    for j in range(6):
                        weight = green[cell, x, j]
                        a = at[cell][x] + j
                        tr = weight * jnp.broadcast_to(spectrum[a : a + 1, re_cols], (8, LANES))
                        ti = weight * jnp.broadcast_to(spectrum[a : a + 1, im_cols], (8, LANES))
                        re = tr if re is None else re + tr
                        im = ti if im is None else im + ti
                    updates.append((re, im))
                values = dft16(updates, 1)
                for x in range(G):
                    a = at[cell][x]
                    plane[a : a + 8, re_cols] = values[x][0]
                    plane[a : a + 8, im_cols] = values[x][1]
            first_im = plane[:half_rows, im_cols]
            second_re = plane[half_rows:, re_cols]
            plane[:half_rows, im_cols] = jnp.where(whole_mirror, second_re, first_im)
            plane[half_rows:, re_cols] = jnp.where(whole_mirror, first_im, second_re)
            update = plane_product(plane[...], cmat, 2)
            for cell in range(2):
                k = 2 * pair + cell
                for x in range(G):
                    a = at[cell][x]
                    value = slab(k, x, iteration) - update[a : a + 8, :]
                    if iteration == 0:
                        value = value + shifts[k]
                    st[k, 8 * x : 8 * x + 8, :] = value

    send[pl.ds(8, 4 * TILES, stride=9), :] = jnp.full((4 * TILES, LANES), -1.0, f32)
    result = jnp.zeros((8, LANES), f32)
    for k in range(4):
        live = k < count[0]
        total = jnp.zeros((8, 2 * LANES), f32)
        for x in range(G):
            total = total + slab_stress(st[k, 8 * x : 8 * x + 8, :], first_rows)
        mean = jnp.sum(total, axis=1, keepdims=True) * (1.0 / NV)
        result = jnp.where((lane == k) & live, jnp.broadcast_to(mean, (8, LANES)), result)
        pool = owner[0, k] & 3

        @pl.when(live)
        def _():
            for i in range(TILES):
                x, part = i // 2, i % 2
                send[pl.ds(9 * (4 * i + pool), 8), :] = st[
                    k, 8 * x : 8 * x + 8, part * LANES : (part + 1) * LANES
                ]
            brick = (owner[0, k] >> 2).astype(f32)
            send[pl.ds(9 * pool + 8, TILES, stride=36), :] = jnp.full((TILES, LANES), brick, f32)

    band_stress[...] = result[0:6, 0:4]
    for k in range(4):
        live_element = jnp.where(k < count[0], element[0, k], -1).astype(f32)
        result = jnp.where((lane == k) & (row == 6), live_element, result)
    replace[...] = result[:, 0:4]


def solve_cells(count, owner, element, disp, nm, grads, micro, green, cmat):
    return pl.pallas_call(
        cells_kernel,
        out_shape=(
            jax.ShapeDtypeStruct((36 * TILES, LANES), f32),
            jax.ShapeDtypeStruct((6, 4), f32),
            jax.ShapeDtypeStruct((8, 4), f32),
        ),
        in_specs=[pl.BlockSpec(memory_space=SMEM)] * 3 + [pl.BlockSpec(memory_space=VMEM)] * 6,
        out_specs=(pl.BlockSpec(memory_space=VMEM),) * 3,
        scratch_shapes=[
            VMEM((4, 8 * G, 2 * LANES), f32),
        ]
        + [VMEM((16 * G, 2 * LANES), f32)] * 4,
        compiler_params=pltpu.CompilerParams(vmem_limit_bytes=56 << 20),
        name="cells",
    )(count, owner, element, disp, nm, grads, micro, green, cmat)


def one_hot_sum(node, values, width):
    def spread(row, rows):
        return jnp.broadcast_to(jnp.broadcast_to(row, (16, width)).astype(bf16)[None], (rows // 16, 16, width)).reshape(
            rows, width
        )

    def index(rows):
        return lax.broadcasted_iota(jnp.int32, (rows, width), 0).astype(f32).astype(bf16)

    coarse = index(HI) == spread((node >> 8).astype(f32), HI)
    fine = index(LO) == spread((node & 255).astype(f32), LO)
    left = jnp.concatenate(
        [jnp.where(coarse, spread(v, HI), jnp.zeros((HI, width), bf16)) for v in values], axis=0
    )
    right = jnp.where(fine, jnp.ones((LO, width), bf16), jnp.zeros((LO, width), bf16))
    return left, right


def halves(value):
    high = value.astype(bf16).astype(f32)
    return high, value - high


def pack_table(disp, table, step):
    largest = jnp.zeros((3, LANES), f32)
    for r in range(72):
        largest = jnp.maximum(largest, jnp.abs(disp[:, r * LANES : (r + 1) * LANES]))
    largest = jnp.maximum(jnp.max(largest, axis=0, keepdims=True), 1e-30)
    step[...] = largest * (1.0 / STEPS)
    scale = jnp.broadcast_to(STEPS / largest, (3, LANES))
    for r in range(72):
        cols = slice(r * LANES, (r + 1) * LANES)
        level = jnp.floor(disp[:, cols] * scale + (OFFSET + 0.5)).astype(jnp.int32)
        last = level[2:3]
        parts = jnp.concatenate([(last & 0x7FF) << 21, (last >> 11) << 21], axis=0)
        table[:, cols] = level[0:2] | parts


def unpack(first, second, step):
    mask = (1 << 21) - 1
    last = lax.shift_right_logical(first, 21) | (lax.shift_right_logical(second, 21) << 11)
    return [(level - OFFSET).astype(f32) * step for level in (first & mask, second & mask, last)]


def macro_tiles(begin, end, unroll, replace, table, step_of, nm, grads, volumes, moduli, sums):
    lane = lax.broadcasted_iota(jnp.int32, (1, LANES), 1).astype(f32)
    steps = jnp.broadcast_to(step_of[...], (8, LANES))

    def scatter(node, forces):
        values = []
        for force in forces:
            values += list(halves(force))
        total = None
        for s in range(0, 8, 2):
            lefts, rights = [], []
            for q in (s, s + 1):
                left, right = one_hot_sum(node[q : q + 1], [v[q : q + 1] for v in values], LANES)
                lefts.append(left)
                rights.append(right)
            product = lax.dot_general(
                jnp.concatenate(lefts, axis=1),
                jnp.concatenate(rights, axis=1),
                (((1,), (1,)), ((), ())),
                preferred_element_type=f32,
            )
            total = product if total is None else total + product
        return total

    def forces_of(t):
        cols = pl.ds(pl.multiple_of(t * LANES, LANES), LANES)
        node = nm[:, cols]
        hi, lo = node >> 7, node & 127
        words = [jnp.zeros((8, LANES), jnp.int32) for _ in range(2)]
        for r in range(72):
            hit = hi == r
            for w in range(2):
                values = jnp.broadcast_to(table[w : w + 1, r * LANES : (r + 1) * LANES], (8, LANES))
                found = jnp.take_along_axis(values, lo, axis=1, mode="promise_in_bounds")
                words[w] = jnp.where(hit, found, words[w])
        u = unpack(*words, jnp.take_along_axis(steps, lo, axis=1, mode="promise_in_bounds"))
        g = [grads[j, :, cols] for j in range(3)]

        def total(value):
            return jnp.sum(value, axis=0, keepdims=True)

        strain = [
            total(u[0] * g[0]),
            total(u[1] * g[1]),
            total(u[2] * g[2]),
            0.5 * total(u[1] * g[2] + u[2] * g[1]),
            0.5 * total(u[0] * g[2] + u[2] * g[0]),
            0.5 * total(u[0] * g[1] + u[1] * g[0]),
        ]
        lam = moduli[0:1, cols]
        mu = moduli[1:2, cols]
        volume = volumes[pl.ds(t, 1), :]
        spherical = lam * (strain[0] + strain[1] + strain[2])
        stress = [spherical + 2.0 * mu * strain[c] for c in range(3)]
        stress += [2.0 * mu * strain[c] for c in range(3, 6)]
        for k in range(4):
            hit = lane == replace[6, k] - lax.convert_element_type(t * LANES, f32)
            stress = [jnp.where(hit, replace[c, k], stress[c]) for c in range(6)]
        xx, yy, zz, yz, xz, xy = [
            jnp.broadcast_to(component * volume, (8, LANES)) for component in stress
        ]
        fx = xx * g[0] + xy * g[1] + xz * g[2]
        fy = xy * g[0] + yy * g[1] + yz * g[2]
        fz = xz * g[0] + yz * g[1] + zz * g[2]
        return node, fx, fy, fz

    def group(step):
        return tuple(forces_of(begin + step * unroll + i) for i in range(unroll))

    def add(carry):
        total = None
        for node, *forces in carry:
            part = scatter(node, forces)
            total = part if total is None else total + part
        sums[...] += total

    def body(step, carry):
        add(carry)
        return group(step)

    add(lax.fori_loop(1, (end - begin) // unroll, body, group(0)))


def macro_first_kernel(unroll, replace, disp, nm, grads, volumes, moduli, sums, table, step):
    pack_table(disp, table, step)
    sums[...] = jnp.zeros_like(sums)
    macro_tiles(0, SPLIT, unroll, replace, table, step, nm, grads, volumes, moduli, sums)


def macro_last_kernel(
    unroll,
    replace,
    core_index,
    pool_index,
    table,
    step,
    nm,
    grads,
    volumes,
    moduli,
    so_far,
    shared,
    own,
    inner,
    outer,
    sums,
    faces,
):
    sums[...] = so_far[...]
    macro_tiles(SPLIT, 64, unroll, replace, table, step, nm, grads, volumes, moduli, sums)

    for c in range(3):
        at = 2 * c * HI
        own[c * HI : (c + 1) * HI, :] = sums[at : at + HI, :] + sums[at + HI : at + 2 * HI, :]

    for pair in range(4):
        first, second = 2 * pair, 2 * pair + 1
        node = jnp.concatenate(
            [
                shared[0, :, first * LANES : (first + 1) * LANES],
                shared[0, :, second * LANES : (second + 1) * LANES],
            ],
            axis=0,
        )
        hi, lo = node >> 7, node & 127
        picked = [jnp.zeros((8, LANES), f32) for _ in range(3)]
        for r in range(72):
            hit = hi == r
            for c in range(3):
                at = c * HI + r // 2
                cols = slice(r % 2 * LANES, (r % 2 + 1) * LANES)
                values = jnp.broadcast_to(own[at : at + 1, cols], (8, LANES))
                found = jnp.take_along_axis(values, lo, axis=1, mode="promise_in_bounds")
                picked[c] = jnp.where(hit, found, picked[c])
        for c in range(3):
            for face in range(4):
                faces[face, c : c + 1, first * LANES : (first + 1) * LANES] = picked[c][face : face + 1]
                faces[face, c : c + 1, second * LANES : (second + 1) * LANES] = picked[c][
                    4 + face : 5 + face
                ]
    core, pool = core_index[0], pool_index[0]
    pools = inner.shape[0] // 2
    inner[...] = jnp.zeros_like(inner)
    inner[(1 - core) * pools + pool] = faces[1 - core]
    outer[...] = faces[core]

    @pl.when(pool > 0)
    def _():
        inner[core * pools + pool - 1] = faces[2]

    @pl.when(pool < pools - 1)
    def _():
        inner[core * pools + pool + 1] = faces[3]


def macro_first(*arguments):
    vmem = pl.BlockSpec(memory_space=VMEM)
    return pl.pallas_call(
        functools.partial(macro_first_kernel, UNROLL),
        out_shape=(
            jax.ShapeDtypeStruct((6 * HI, LO), f32),
            jax.ShapeDtypeStruct((2, 72 * LANES), jnp.int32),
            jax.ShapeDtypeStruct((1, LANES), f32),
        ),
        in_specs=[pl.BlockSpec(memory_space=SMEM)] + [vmem] * 5,
        out_specs=(vmem,) * 3,
        compiler_params=pltpu.CompilerParams(vmem_limit_bytes=32 << 20),
        name="macro_first",
    )(*arguments)


def macro_last(pools, *arguments):
    vmem = pl.BlockSpec(memory_space=VMEM)
    return pl.pallas_call(
        functools.partial(macro_last_kernel, UNROLL),
        out_shape=(
            jax.ShapeDtypeStruct((3 * HI, LO), f32),
            jax.ShapeDtypeStruct((2 * pools, 3, 1024), f32),
            jax.ShapeDtypeStruct((3, 1024), f32),
        ),
        in_specs=[pl.BlockSpec(memory_space=SMEM)] * 3 + [vmem] * 8,
        out_specs=(vmem,) * 3,
        scratch_shapes=[VMEM((6 * HI, LO), f32), VMEM((4, 3, 1024), f32)],
        compiler_params=pltpu.CompilerParams(vmem_limit_bytes=32 << 20),
        name="macro_last",
    )(*arguments)


def assemble_kernel(core_index, pool_index, own, shared, inner, outer, external, mass, out):
    core, pool = core_index[0], pool_index[0]
    pools = inner.shape[0] // 2
    below, above = jnp.maximum(pool - 1, 0), jnp.minimum(pool + 1, pools - 1)
    arrivals = (
        (1 - core, True, lambda c, cols: inner[(1 - core) * pools + pool, c : c + 1, cols]),
        (core, True, lambda c, cols: outer[c : c + 1, cols]),
        (2, pool > 0, lambda c, cols: inner[core * pools + below, c : c + 1, cols]),
        (3, pool < pools - 1, lambda c, cols: inner[core * pools + above, c : c + 1, cols]),
    )
    total = None
    for face, there, arrived in arrivals:
        for part in range(4):
            cols = slice(part * LO, (part + 1) * LO)
            values = []
            for c in range(3):
                value = arrived(c, cols)
                if there is not True:
                    value = jnp.where(there, value, 0.0)
                values += list(halves(value))
            left, right = one_hot_sum(shared[0, pl.ds(face, 1), cols], values, LO)
            product = lax.dot_general(
                left, right, (((1,), (1,)), ((), ())), preferred_element_type=f32
            )
            total = product if total is None else total + product
    for c in range(3):
        at = 2 * c * HI
        whole = own[c * HI : (c + 1) * HI, :] + total[at : at + HI] + total[at + HI : at + 2 * HI]
        for r in range(36):
            out[c : c + 1, r * LO : (r + 1) * LO] = whole[r : r + 1]
    out[...] = (external[...] - out[...]) / mass[...]


def assemble(place, own, shared, inner, outer, external, mass):
    vmem = pl.BlockSpec(memory_space=VMEM)
    return pl.pallas_call(
        assemble_kernel,
        out_shape=jax.ShapeDtypeStruct(external.shape, f32),
        in_specs=[pl.BlockSpec(memory_space=SMEM)] * 2 + [vmem] * 6,
        out_specs=vmem,
        compiler_params=pltpu.CompilerParams(vmem_limit_bytes=32 << 20),
        name="assemble",
    )(*place, own, shared, inner, outer, external, mass)


def sort_kernel(pieces, out, order, places, sem):
    blocks = pieces.shape[0] // 9
    lane = lax.broadcasted_iota(jnp.int32, (blocks, LANES), 1)
    block = lax.broadcasted_iota(jnp.int32, (blocks, LANES), 0)
    hit = pieces[pl.ds(8, blocks, stride=9), :] == lane.astype(f32)
    order[0:1, :] = jnp.min(jnp.where(hit, block, blocks - 1), axis=0, keepdims=True)
    order[1:2, :] = jnp.max(jnp.where(hit, block, 0), axis=0, keepdims=True)
    copy = pltpu.make_async_copy(order, places, sem)
    copy.start()
    copy.wait()
    for b in range(out.shape[0]):
        for s in range(2):
            out[b, s] = pieces[pl.ds(9 * places[s, b], 8), :]


def sort_pieces(pieces, bricks):
    vmem = pl.BlockSpec(memory_space=VMEM)
    return pl.pallas_call(
        sort_kernel,
        out_shape=jax.ShapeDtypeStruct((bricks, 2, 8, LANES), f32),
        in_specs=[vmem],
        out_specs=vmem,
        scratch_shapes=[VMEM((8, LANES), jnp.int32), SMEM((8, LANES), jnp.int32), pltpu.SemaphoreType.DMA],
        compiler_params=pltpu.CompilerParams(vmem_limit_bytes=32 << 20),
        name="sort_pieces",
    )(pieces)


def join_kernel(pieces, out):
    for i in range(TILES):
        for s in range(2):
            out[s, :, i * LANES : (i + 1) * LANES] = pieces[i, s]


def join_pieces(pieces):
    vmem = pl.BlockSpec(memory_space=VMEM)
    return pl.pallas_call(
        join_kernel,
        out_shape=jax.ShapeDtypeStruct((2, 8, NV), f32),
        in_specs=[vmem],
        out_specs=vmem,
        name="join_pieces",
    )(pieces)


def shards(
    displacement,
    node_map,
    shape_grads,
    volumes,
    elastic_moduli,
    external_force,
    nodal_mass,
    shared_nodes,
    band_count,
    band_owner,
    band_element,
    micro_fields,
):
    bricks, pools = lax.axis_size(BRICK), lax.axis_size("pool")
    place = tuple(lax.axis_index(axis).astype(jnp.int32).reshape(1) for axis in ("core", "pool"))
    send, band_stress, replace = solve_cells(
        band_count,
        band_owner,
        band_element,
        displacement,
        node_map,
        shape_grads,
        micro_fields,
        jnp.asarray(green_table()),
        jnp.asarray(plane_tables()),
    )
    pieces = lax.all_to_all(
        send.reshape(bricks * pools, 1, 9 * LANES), BOTH, split_axis=0, concat_axis=0, tiled=True
    )
    dense = (node_map, shape_grads, volumes.reshape(64, LANES), elastic_moduli)
    so_far, table, step = macro_first(replace, displacement, *dense)
    pieces, so_far = lax.optimization_barrier((pieces, so_far))
    sorted_pieces = sort_pieces(pieces.reshape(9 * bricks * pools, LANES), bricks)
    sorted_pieces, so_far = lax.optimization_barrier((sorted_pieces, so_far))
    mine = lax.all_to_all(sorted_pieces, BRICK, split_axis=0, concat_axis=0, tiled=True)
    own, inner, outer = macro_last(pools, replace, *place, table, step, *dense, so_far, shared_nodes)
    inner = lax.all_to_all(inner, ("core", "pool"), split_axis=0, concat_axis=0, tiled=True)
    steps = [(i, i + 1) for i in range(1, bricks - 1, 2)]
    outer = lax.ppermute(outer, BRICK, steps + [(j, i) for i, j in steps])
    owned_fields = join_pieces(mine)
    inner, outer, owned_fields = lax.optimization_barrier((inner, outer, owned_fields))
    acceleration = assemble(
        place, own, shared_nodes, inner, outer, external_force, nodal_mass.reshape(1, -1)
    )
    return (acceleration, band_stress, owned_fields)


def solution(mesh):
    bricks, pools = mesh.devices.shape
    split = jax.sharding.Mesh(
        mesh.devices.reshape(4, bricks // 8, 2, pools), ("row", "pair", "core", "pool")
    )
    placed = (
        P(None, BOTH),
        P(None, BOTH),
        P(None, None, BOTH),
        P(BOTH),
        P(None, BOTH),
        P(None, BOTH),
        P(BOTH),
        P(BOTH, None, None),
        P(BOTH),
        P(BOTH, None),
        P(BOTH, None),
        P(BOTH, None, None),
    )
    return jax.shard_map(
        shards,
        mesh=split,
        in_specs=placed,
        out_specs=(P(None, BOTH), P(None, BOTH), P(BOTH, None, None)),
        check_vma=False,
    )
```

```python
import functools
import math

import jax
import jax.numpy as jnp
import numpy as np
from jax import lax
from jax.experimental import pallas as pl
from jax.experimental.pallas import tpu as pltpu
from jax.sharding import PartitionSpec as P

G = 16
NV = 4096
ITERS = 2
LANES = 128
TILES = 32
HI = 48
LO = 256
STEPS = float((1 << 20) - 2)
OFFSET = 1 << 20
UNROLL = 4
SPLIT = 48
BRICK = ("row", "pair", "core")
BOTH = BRICK + ("pool",)
VMEM = pltpu.VMEM
SMEM = pltpu.SMEM
f32 = jnp.float32
bf16 = jnp.bfloat16

ref_lambda = 5.5
ref_shear = 5.5


def green_table():
    index = np.arange(G)

    def operator(ix, iy, iz):
        wave = [np.where(2 * m < G, m, m - G).astype(np.float64) for m in (ix, iy, iz)]
        kx, ky, kz = np.broadcast_arrays(wave[0], wave[1], wave[2])
        square = kx * kx + ky * ky + kz * kz
        safe = np.where(square > 0, square, 1.0)
        first = np.where(square > 0, 1.0 / (2.0 * ref_shear * safe), 0.0)
        factor = (ref_lambda + ref_shear) / (ref_shear * (ref_lambda + 2.0 * ref_shear))
        second = np.where(square > 0, factor / (safe * safe), 0.0)
        zero, one = np.zeros_like(kx), np.ones_like(kx)
        columns = []
        for j in range(6):
            xx, yy, zz, yz, xz, xy = [one if j == c else zero for c in range(6)]
            wx = xx * kx + xy * ky + xz * kz
            wy = xy * kx + yy * ky + yz * kz
            wz = xz * kx + yz * ky + zz * kz
            s = (wx * kx + wy * ky + wz * kz) * second
            columns.append(
                np.stack(
                    [
                        first * 2 * kx * wx - s * kx * kx,
                        first * 2 * ky * wy - s * ky * ky,
                        first * 2 * kz * wz - s * kz * kz,
                        first * (ky * wz + kz * wy) - s * ky * kz,
                        first * (kx * wz + kz * wx) - s * kx * kz,
                        first * (kx * wy + ky * wx) - s * kx * ky,
                        zero,
                        zero,
                    ]
                )
            )
        return np.stack(columns)

    ix, iy, iz = index[:, None, None], index[None, :, None], index[None, None, :]
    table = 0.5 * (operator(ix, iy, iz) + operator((-ix) % G, (-iy) % G, (-iz) % G)) / NV
    table = table.reshape(6, 8, G, G * G).transpose(2, 0, 1, 3)
    pairs, alone = half_plane()
    even, odd = np.concatenate([pairs, alone[:2]]), np.concatenate([pairs, alone[2:]])
    return np.stack([table[..., even], table[..., odd]]).astype(np.float32)


def half_plane():
    index = np.arange(G * G)
    mirror = (-(index // G)) % G * G + (-(index % G)) % G
    return index[index < mirror], index[index == mirror]


def plane_tables():
    pairs, alone = half_plane()
    plane = np.arange(G * G)

    def angle(k):
        turns = (plane[:, None] // G * (k // G)[None, :] + plane[:, None] % G * (k % G)[None, :]) % G
        return turns * (2 * np.pi / G)

    there = np.concatenate(
        [
            np.cos(angle(pairs)),
            np.cos(angle(alone[:2])),
            -np.sin(angle(pairs)),
            np.cos(angle(alone[2:])),
        ],
        axis=1,
    )
    weight = np.full((G * G, 1), 2.0)
    weight[[126, 127, 254, 255]] = 1.0
    parts = []
    for table in (there, weight * there.T):
        high = table.astype(np.float32).astype(bf16)
        parts += [high, (table - high.astype(np.float64)).astype(np.float32).astype(bf16)]
    return np.stack(parts)


def twiddle(value, power, sign):
    re, im = value
    power %= 16
    if power == 0:
        return re, im
    if power == 4:
        return (-im, re) if sign > 0 else (im, -re)
    if power == 8:
        return -re, -im
    if power == 12:
        return (im, -re) if sign > 0 else (-im, re)
    angle = sign * 2 * math.pi * power / 16
    c, s = math.cos(angle), math.sin(angle)
    if power % 4 == 2:
        h = abs(c)
        a = re if c > 0 else -re
        b = im if c > 0 else -im
        if c * s > 0:
            return (a - b) * h, (a + b) * h
        return (a + b) * h, (b - a) * h
    return re * c - im * s, re * s + im * c


def dft4(v, sign):
    (ar, ai), (br, bi), (cr, ci), (dr, di) = v
    pr, pi_ = ar + cr, ai + ci
    mr, mi = ar - cr, ai - ci
    qr, qi = br + dr, bi + di
    nr, ni = br - dr, bi - di
    if sign < 0:
        jr, ji = ni, -nr
    else:
        jr, ji = -ni, nr
    return [(pr + qr, pi_ + qi), (mr + jr, mi + ji), (pr - qr, pi_ - qi), (mr - jr, mi - ji)]


def dft16(values, sign):
    inner = []
    for n2 in range(4):
        inner.append(dft4([values[n2 + 4 * n1] for n1 in range(4)], sign))
    out = [None] * 16
    for k1 in range(4):
        column = dft4([twiddle(inner[n2][k1], n2 * k1, sign) for n2 in range(4)], sign)
        for k2 in range(4):
            out[k1 + 4 * k2] = column[k2]
    return out


def slab_stress(d, first_rows):
    wide = d.shape
    trace = d[0:1] + d[1:2] + d[2:3]
    lam_trace = jnp.broadcast_to(d[6:7] * trace, wide)
    twice = jnp.broadcast_to(2.0 * d[7:8], wide)
    return twice * d + jnp.where(first_rows, lam_trace, 0.0)


def plane_product(x, cmat, at):
    high = x.astype(bf16)
    low = (x - high.astype(f32)).astype(bf16)
    rows = x.shape[0]
    both = jnp.dot(jnp.concatenate([high, low], axis=0), cmat[at], preferred_element_type=f32)
    return both[:rows] + both[rows:] + jnp.dot(high, cmat[at + 1], preferred_element_type=f32)


def cells_kernel(
    count, owner, element, disp, nm, grads, micro, green, cmat, send, band_stress, replace, st, *work
):
    half_rows = 8 * G
    lane = lax.broadcasted_iota(jnp.int32, (8, LANES), 1)
    row = lax.broadcasted_iota(jnp.int32, (8, LANES), 0)
    row_wide = lax.broadcasted_iota(jnp.int32, (8, 2 * LANES), 0)
    first_rows = row_wide < 3

    targets = []
    for k in range(4):
        e = element[0, k]
        base = pl.multiple_of(e // LANES * LANES, LANES)
        at = lane == e % LANES

        def pick(tile):
            return jnp.sum(jnp.where(at, tile, 0.0), axis=1, keepdims=True)

        node = pick(nm[:, pl.ds(base, LANES)].astype(f32)).astype(jnp.int32)
        shape = [jnp.broadcast_to(pick(grads[j, :, pl.ds(base, LANES)]), (8, LANES)) for j in range(3)]
        node = jnp.broadcast_to(node, (8, LANES)) - lane
        found = [jnp.zeros((8, LANES), f32) for _ in range(3)]
        for r in range(72):
            hit = node == r * LANES
            for c in range(3):
                values = jnp.broadcast_to(disp[c : c + 1, r * LANES : (r + 1) * LANES], (8, LANES))
                found[c] = jnp.where(hit, values, found[c])
        u = [jnp.sum(found[c], axis=1, keepdims=True) for c in range(3)]

        def total(value):
            return jnp.sum(value, axis=0, keepdims=True)

        parts = [
            total(u[0] * shape[0]),
            total(u[1] * shape[1]),
            total(u[2] * shape[2]),
            0.5 * total(u[1] * shape[2] + u[2] * shape[1]),
            0.5 * total(u[0] * shape[2] + u[2] * shape[0]),
            0.5 * total(u[0] * shape[1] + u[1] * shape[0]),
        ]
        target = jnp.zeros((8, LANES), f32)
        for c in range(6):
            target = jnp.where(row == c, jnp.broadcast_to(parts[c], (8, LANES)), target)
        targets.append(target)

    def slab(k, x, iteration):
        if iteration == 0:
            return micro[k, :, 2 * LANES * x : 2 * LANES * (x + 1)]
        return st[k, 8 * x : 8 * x + 8, :]

    shifts = []
    for k in range(4):
        total = jnp.zeros((8, 2 * LANES), f32)
        for x in range(G):
            total = total + slab(k, x, 0)
        mean = jnp.sum(total, axis=1, keepdims=True) * (1.0 / NV)
        shift = jnp.where(row < 6, targets[k] - mean, 0.0)
        shifts.append(jnp.concatenate([shift, shift], axis=1))

    re_cols, im_cols = slice(0, LANES), slice(LANES, 2 * LANES)
    own_mirror = lane >= 126
    whole_mirror = lax.broadcasted_iota(jnp.int32, (half_rows, LANES), 1) >= 126
    for iteration in range(ITERS):
        for pair in range(2):
            plane, spectrum = work[2 * pair], work[2 * pair + 1]
            at = [[cell * half_rows + 8 * x for x in range(G)] for cell in range(2)]
            for cell in range(2):
                for x in range(G):
                    a = at[cell][x]
                    plane[a : a + 8, :] = slab_stress(slab(2 * pair + cell, x, iteration), first_rows)
            plane[...] = plane_product(plane[...], cmat, 0)
            for cell in range(2):
                values = []
                for x in range(G):
                    a = at[cell][x]
                    re, im = plane[a : a + 8, re_cols], plane[a : a + 8, im_cols]
                    if cell == 0:
                        other = at[1][x]
                        im = jnp.where(own_mirror, plane[other : other + 8, re_cols], im)
                    else:
                        other = at[0][x]
                        re = jnp.where(own_mirror, plane[other : other + 8, im_cols], re)
                    values.append((re, im))
                values = dft16(values, -1)
                for x in range(G):
                    a = at[cell][x]
                    spectrum[a : a + 8, re_cols] = values[x][0]
                    spectrum[a : a + 8, im_cols] = values[x][1]
            for cell in range(2):
                updates = []
                for x in range(G):
                    re = im = None
                    for j in range(6):
                        weight = green[cell, x, j]
                        a = at[cell][x] + j
                        tr = weight * jnp.broadcast_to(spectrum[a : a + 1, re_cols], (8, LANES))
                        ti = weight * jnp.broadcast_to(spectrum[a : a + 1, im_cols], (8, LANES))
                        re = tr if re is None else re + tr
                        im = ti if im is None else im + ti
                    updates.append((re, im))
                values = dft16(updates, 1)
                for x in range(G):
                    a = at[cell][x]
                    plane[a : a + 8, re_cols] = values[x][0]
                    plane[a : a + 8, im_cols] = values[x][1]
            first_im = plane[:half_rows, im_cols]
            second_re = plane[half_rows:, re_cols]
            plane[:half_rows, im_cols] = jnp.where(whole_mirror, second_re, first_im)
            plane[half_rows:, re_cols] = jnp.where(whole_mirror, first_im, second_re)
            update = plane_product(plane[...], cmat, 2)
            for cell in range(2):
                k = 2 * pair + cell
                for x in range(G):
                    a = at[cell][x]
                    value = slab(k, x, iteration) - update[a : a + 8, :]
                    if iteration == 0:
                        value = value + shifts[k]
                    st[k, 8 * x : 8 * x + 8, :] = value

    send[pl.ds(8, 4 * TILES, stride=9), :] = jnp.full((4 * TILES, LANES), -1.0, f32)
    result = jnp.zeros((8, LANES), f32)
    for k in range(4):
        live = k < count[0]
        total = jnp.zeros((8, 2 * LANES), f32)
        for x in range(G):
            total = total + slab_stress(st[k, 8 * x : 8 * x + 8, :], first_rows)
        mean = jnp.sum(total, axis=1, keepdims=True) * (1.0 / NV)
        result = jnp.where((lane == k) & live, jnp.broadcast_to(mean, (8, LANES)), result)
        pool = owner[0, k] & 3

        @pl.when(live)
        def _():
            for i in range(TILES):
                x, part = i // 2, i % 2
                send[pl.ds(9 * (4 * i + pool), 8), :] = st[
                    k, 8 * x : 8 * x + 8, part * LANES : (part + 1) * LANES
                ]
            brick = (owner[0, k] >> 2).astype(f32)
            send[pl.ds(9 * pool + 8, TILES, stride=36), :] = jnp.full((TILES, LANES), brick, f32)

    band_stress[...] = result[0:6, 0:4]
    for k in range(4):
        live_element = jnp.where(k < count[0], element[0, k], -1).astype(f32)
        result = jnp.where((lane == k) & (row == 6), live_element, result)
    replace[...] = result[:, 0:4]


def solve_cells(count, owner, element, disp, nm, grads, micro, green, cmat):
    return pl.pallas_call(
        cells_kernel,
        out_shape=(
            jax.ShapeDtypeStruct((36 * TILES, LANES), f32),
            jax.ShapeDtypeStruct((6, 4), f32),
            jax.ShapeDtypeStruct((8, 4), f32),
        ),
        in_specs=[pl.BlockSpec(memory_space=SMEM)] * 3 + [pl.BlockSpec(memory_space=VMEM)] * 6,
        out_specs=(pl.BlockSpec(memory_space=VMEM),) * 3,
        scratch_shapes=[
            VMEM((4, 8 * G, 2 * LANES), f32),
        ]
        + [VMEM((16 * G, 2 * LANES), f32)] * 4,
        compiler_params=pltpu.CompilerParams(vmem_limit_bytes=56 << 20),
        name="cells",
    )(count, owner, element, disp, nm, grads, micro, green, cmat)


def one_hot_sum(node, values, width):
    def spread(row, rows):
        return jnp.broadcast_to(jnp.broadcast_to(row, (16, width)).astype(bf16)[None], (rows // 16, 16, width)).reshape(
            rows, width
        )

    def index(rows):
        return lax.broadcasted_iota(jnp.int32, (rows, width), 0).astype(f32).astype(bf16)

    coarse = index(HI) == spread((node >> 8).astype(f32), HI)
    fine = index(LO) == spread((node & 255).astype(f32), LO)
    left = jnp.concatenate(
        [jnp.where(coarse, spread(v, HI), jnp.zeros((HI, width), bf16)) for v in values], axis=0
    )
    right = jnp.where(fine, jnp.ones((LO, width), bf16), jnp.zeros((LO, width), bf16))
    return left, right


def halves(value):
    high = value.astype(bf16).astype(f32)
    return high, value - high


def pack_table(disp, table, step):
    largest = jnp.zeros((3, LANES), f32)
    for r in range(72):
        largest = jnp.maximum(largest, jnp.abs(disp[:, r * LANES : (r + 1) * LANES]))
    largest = jnp.maximum(jnp.max(largest, axis=0, keepdims=True), 1e-30)
    step[...] = largest * (1.0 / STEPS)
    scale = jnp.broadcast_to(STEPS / largest, (3, LANES))
    for r in range(72):
        cols = slice(r * LANES, (r + 1) * LANES)
        level = jnp.floor(disp[:, cols] * scale + (OFFSET + 0.5)).astype(jnp.int32)
        last = level[2:3]
        parts = jnp.concatenate([(last & 0x7FF) << 21, (last >> 11) << 21], axis=0)
        table[:, cols] = level[0:2] | parts


def unpack(first, second, step):
    mask = (1 << 21) - 1
    last = lax.shift_right_logical(first, 21) | (lax.shift_right_logical(second, 21) << 11)
    return [(level - OFFSET).astype(f32) * step for level in (first & mask, second & mask, last)]


def macro_tiles(begin, end, unroll, replace, table, step_of, nm, grads, volumes, moduli, sums):
    lane = lax.broadcasted_iota(jnp.int32, (1, LANES), 1).astype(f32)
    steps = jnp.broadcast_to(step_of[...], (8, LANES))

    def scatter(node, forces):
        values = []
        for force in forces:
            values += list(halves(force))
        total = None
        for s in range(0, 8, 2):
            lefts, rights = [], []
            for q in (s, s + 1):
                left, right = one_hot_sum(node[q : q + 1], [v[q : q + 1] for v in values], LANES)
                lefts.append(left)
                rights.append(right)
            product = lax.dot_general(
                jnp.concatenate(lefts, axis=1),
                jnp.concatenate(rights, axis=1),
                (((1,), (1,)), ((), ())),
                preferred_element_type=f32,
            )
            total = product if total is None else total + product
        return total

    def forces_of(t):
        cols = pl.ds(pl.multiple_of(t * LANES, LANES), LANES)
        node = nm[:, cols]
        hi, lo = node >> 7, node & 127
        words = [jnp.zeros((8, LANES), jnp.int32) for _ in range(2)]
        for r in range(72):
            hit = hi == r
            for w in range(2):
                values = jnp.broadcast_to(table[w : w + 1, r * LANES : (r + 1) * LANES], (8, LANES))
                found = jnp.take_along_axis(values, lo, axis=1, mode="promise_in_bounds")
                words[w] = jnp.where(hit, found, words[w])
        u = unpack(*words, jnp.take_along_axis(steps, lo, axis=1, mode="promise_in_bounds"))
        g = [grads[j, :, cols] for j in range(3)]

        def total(value):
            return jnp.sum(value, axis=0, keepdims=True)

        strain = [
            total(u[0] * g[0]),
            total(u[1] * g[1]),
            total(u[2] * g[2]),
            0.5 * total(u[1] * g[2] + u[2] * g[1]),
            0.5 * total(u[0] * g[2] + u[2] * g[0]),
            0.5 * total(u[0] * g[1] + u[1] * g[0]),
        ]
        lam = moduli[0:1, cols]
        mu = moduli[1:2, cols]
        volume = volumes[pl.ds(t, 1), :]
        spherical = lam * (strain[0] + strain[1] + strain[2])
        stress = [spherical + 2.0 * mu * strain[c] for c in range(3)]
        stress += [2.0 * mu * strain[c] for c in range(3, 6)]
        for k in range(4):
            hit = lane == replace[6, k] - lax.convert_element_type(t * LANES, f32)
            stress = [jnp.where(hit, replace[c, k], stress[c]) for c in range(6)]
        xx, yy, zz, yz, xz, xy = [
            jnp.broadcast_to(component * volume, (8, LANES)) for component in stress
        ]
        fx = xx * g[0] + xy * g[1] + xz * g[2]
        fy = xy * g[0] + yy * g[1] + yz * g[2]
        fz = xz * g[0] + yz * g[1] + zz * g[2]
        return node, fx, fy, fz

    def group(step):
        return tuple(forces_of(begin + step * unroll + i) for i in range(unroll))

    def add(carry):
        total = None
        for node, *forces in carry:
            part = scatter(node, forces)
            total = part if total is None else total + part
        sums[...] += total

    def body(step, carry):
        add(carry)
        return group(step)

    add(lax.fori_loop(1, (end - begin) // unroll, body, group(0)))


def macro_first_kernel(
    unroll, replace, disp, nm, grads, volumes, moduli, shared, sums, table, step, face_nodes
):
    for i in range(4):
        for half in range(2):
            cols = slice((2 * i + half) * LANES, (2 * i + half + 1) * LANES)
            face_nodes[i, 4 * half : 4 * half + 4, :] = shared[0, :, cols]
    pack_table(disp, table, step)
    sums[...] = jnp.zeros_like(sums)
    macro_tiles(0, SPLIT, unroll, replace, table, step, nm, grads, volumes, moduli, sums)


def face_lists(core, pool):
    return 1 - core, core, 3 - (pool & 1), 2 + (pool & 1)


def macro_last_kernel(
    unroll,
    replace,
    core_index,
    pool_index,
    table,
    step,
    nm,
    grads,
    volumes,
    moduli,
    so_far,
    face_nodes,
    own,
    to_core,
    to_brick,
    to_even,
    to_odd,
    sums,
    faces,
):
    sums[...] = so_far[...]
    macro_tiles(SPLIT, 64, unroll, replace, table, step, nm, grads, volumes, moduli, sums)

    for c in range(3):
        at = 2 * c * HI
        own[c * HI : (c + 1) * HI, :] = sums[at : at + HI, :] + sums[at + HI : at + 2 * HI, :]

    for pair in range(4):
        first, second = 2 * pair, 2 * pair + 1
        node = face_nodes[pair]
        hi, lo = node >> 7, node & 127
        picked = [jnp.zeros((8, LANES), f32) for _ in range(3)]
        for r in range(72):
            hit = hi == r
            for c in range(3):
                at = c * HI + r // 2
                cols = slice(r % 2 * LANES, (r % 2 + 1) * LANES)
                values = jnp.broadcast_to(own[at : at + 1, cols], (8, LANES))
                found = jnp.take_along_axis(values, lo, axis=1, mode="promise_in_bounds")
                picked[c] = jnp.where(hit, found, picked[c])
        for c in range(3):
            for face in range(4):
                faces[face, c : c + 1, first * LANES : (first + 1) * LANES] = picked[c][face : face + 1]
                faces[face, c : c + 1, second * LANES : (second + 1) * LANES] = picked[c][
                    4 + face : 5 + face
                ]
    lists = face_lists(core_index[0], pool_index[0])
    for face, out in zip(lists, (to_core, to_brick, to_even, to_odd)):
        out[...] = faces[face]


def macro_first(*arguments):
    vmem = pl.BlockSpec(memory_space=VMEM)
    return pl.pallas_call(
        functools.partial(macro_first_kernel, UNROLL),
        out_shape=(
            jax.ShapeDtypeStruct((6 * HI, LO), f32),
            jax.ShapeDtypeStruct((2, 72 * LANES), jnp.int32),
            jax.ShapeDtypeStruct((1, LANES), f32),
            jax.ShapeDtypeStruct((4, 8, LANES), jnp.int32),
        ),
        in_specs=[pl.BlockSpec(memory_space=SMEM)] + [vmem] * 6,
        out_specs=(vmem,) * 4,
        compiler_params=pltpu.CompilerParams(vmem_limit_bytes=32 << 20),
        name="macro_first",
    )(*arguments)


def macro_last(*arguments):
    vmem = pl.BlockSpec(memory_space=VMEM)
    return pl.pallas_call(
        functools.partial(macro_last_kernel, UNROLL),
        out_shape=(
            jax.ShapeDtypeStruct((3 * HI, LO), f32),
        )
        + (jax.ShapeDtypeStruct((3, 1024), f32),) * 4,
        in_specs=[pl.BlockSpec(memory_space=SMEM)] * 3 + [vmem] * 8,
        out_specs=(vmem,) * 5,
        scratch_shapes=[VMEM((6 * HI, LO), f32), VMEM((4, 3, 1024), f32)],
        compiler_params=pltpu.CompilerParams(vmem_limit_bytes=32 << 20),
        name="macro_last",
    )(*arguments)


def assemble_kernel(core_index, pool_index, own, shared, r0, r1, r2, r3, external, mass, out):
    total = None
    for face, arrived in zip(face_lists(core_index[0], pool_index[0]), (r0, r1, r2, r3)):
        for part in range(4):
            cols = slice(part * LO, (part + 1) * LO)
            values = []
            for c in range(3):
                values += list(halves(arrived[c : c + 1, cols]))
            left, right = one_hot_sum(shared[0, pl.ds(face, 1), cols], values, LO)
            product = lax.dot_general(
                left, right, (((1,), (1,)), ((), ())), preferred_element_type=f32
            )
            total = product if total is None else total + product
    for c in range(3):
        at = 2 * c * HI
        whole = own[c * HI : (c + 1) * HI, :] + total[at : at + HI] + total[at + HI : at + 2 * HI]
        for r in range(36):
            out[c : c + 1, r * LO : (r + 1) * LO] = whole[r : r + 1]
    out[...] = (external[...] - out[...]) / mass[...]


def assemble(place, own, shared, arrived, external, mass):
    vmem = pl.BlockSpec(memory_space=VMEM)
    return pl.pallas_call(
        assemble_kernel,
        out_shape=jax.ShapeDtypeStruct(external.shape, f32),
        in_specs=[pl.BlockSpec(memory_space=SMEM)] * 2 + [vmem] * 8,
        out_specs=vmem,
        compiler_params=pltpu.CompilerParams(vmem_limit_bytes=32 << 20),
        name="assemble",
    )(*place, own, shared, *arrived, external, mass)


def sort_kernel(pieces, out, order, places, sem):
    blocks = pieces.shape[0] // 9
    lane = lax.broadcasted_iota(jnp.int32, (blocks, LANES), 1)
    block = lax.broadcasted_iota(jnp.int32, (blocks, LANES), 0)
    hit = pieces[pl.ds(8, blocks, stride=9), :] == lane.astype(f32)
    order[0:1, :] = jnp.min(jnp.where(hit, block, blocks - 1), axis=0, keepdims=True)
    order[1:2, :] = jnp.max(jnp.where(hit, block, 0), axis=0, keepdims=True)
    copy = pltpu.make_async_copy(order, places, sem)
    copy.start()
    copy.wait()
    for b in range(out.shape[0]):
        for s in range(2):
            out[b, s] = pieces[pl.ds(9 * places[s, b], 8), :]


def sort_pieces(pieces, bricks):
    vmem = pl.BlockSpec(memory_space=VMEM)
    return pl.pallas_call(
        sort_kernel,
        out_shape=jax.ShapeDtypeStruct((bricks, 2, 8, LANES), f32),
        in_specs=[vmem],
        out_specs=vmem,
        scratch_shapes=[VMEM((8, LANES), jnp.int32), SMEM((8, LANES), jnp.int32), pltpu.SemaphoreType.DMA],
        compiler_params=pltpu.CompilerParams(vmem_limit_bytes=32 << 20),
        name="sort_pieces",
    )(pieces)


def join_kernel(pieces, out):
    for i in range(TILES):
        for s in range(2):
            out[s, :, i * LANES : (i + 1) * LANES] = pieces[i, s]


def join_pieces(pieces):
    vmem = pl.BlockSpec(memory_space=VMEM)
    return pl.pallas_call(
        join_kernel,
        out_shape=jax.ShapeDtypeStruct((2, 8, NV), f32),
        in_specs=[vmem],
        out_specs=vmem,
        name="join_pieces",
    )(pieces)


def shards(
    displacement,
    node_map,
    shape_grads,
    volumes,
    elastic_moduli,
    external_force,
    nodal_mass,
    shared_nodes,
    band_count,
    band_owner,
    band_element,
    micro_fields,
):
    bricks, pools = lax.axis_size(BRICK), lax.axis_size("pool")
    place = tuple(lax.axis_index(axis).astype(jnp.int32).reshape(1) for axis in ("core", "pool"))
    send, band_stress, replace = solve_cells(
        band_count,
        band_owner,
        band_element,
        displacement,
        node_map,
        shape_grads,
        micro_fields,
        jnp.asarray(green_table()),
        jnp.asarray(plane_tables()),
    )
    pieces = lax.all_to_all(
        send.reshape(bricks * pools, 1, 9 * LANES), BOTH, split_axis=0, concat_axis=0, tiled=True
    )
    dense = (node_map, shape_grads, volumes.reshape(64, LANES), elastic_moduli)
    so_far, table, step, face_nodes = macro_first(replace, displacement, *dense, shared_nodes)
    pieces, so_far = lax.optimization_barrier((pieces, so_far))
    sorted_pieces = sort_pieces(pieces.reshape(9 * bricks * pools, LANES), bricks)
    sorted_pieces, so_far = lax.optimization_barrier((sorted_pieces, so_far))
    mine = lax.all_to_all(sorted_pieces, BRICK, split_axis=0, concat_axis=0, tiled=True)
    own, *faces = macro_last(replace, *place, table, step, *dense, so_far, face_nodes)

    def swap(array, axis, size, first):
        steps = [(i, i + 1) for i in range(first, size - 1, 2)]
        return lax.ppermute(array, axis, steps + [(j, i) for i, j in steps])

    arrived = (
        swap(faces[0], "core", 2, 0),
        swap(faces[1], BRICK, bricks, 1),
        swap(faces[2], "pool", pools, 0),
        swap(faces[3], "pool", pools, 1),
    )
    owned_fields = join_pieces(mine)
    *arrived, owned_fields = lax.optimization_barrier((*arrived, owned_fields))
    acceleration = assemble(
        place, own, shared_nodes, arrived, external_force, nodal_mass.reshape(1, -1)
    )
    return (acceleration, band_stress, owned_fields)


def solution(mesh):
    bricks, pools = mesh.devices.shape
    split = jax.sharding.Mesh(
        mesh.devices.reshape(4, bricks // 8, 2, pools), ("row", "pair", "core", "pool")
    )
    placed = (
        P(None, BOTH),
        P(None, BOTH),
        P(None, None, BOTH),
        P(BOTH),
        P(None, BOTH),
        P(None, BOTH),
        P(BOTH),
        P(BOTH, None, None),
        P(BOTH),
        P(BOTH, None),
        P(BOTH, None),
        P(BOTH, None, None),
    )
    return jax.shard_map(
        shards,
        mesh=split,
        in_specs=placed,
        out_specs=(P(None, BOTH), P(None, BOTH), P(BOTH, None, None)),
        check_vma=False,
    )
```

```python
import functools
import math

import jax
import jax.numpy as jnp
import numpy as np
from jax import lax
from jax.experimental import pallas as pl
from jax.experimental.pallas import tpu as pltpu
from jax.sharding import PartitionSpec as P

G = 16
NV = 4096
ITERS = 2
LANES = 128
TILES = 32
HI = 48
LO = 256
STEPS = float((1 << 20) - 2)
OFFSET = 1 << 20
UNROLL = 4
SPLIT = 48
BRICK = ("row", "pair", "core")
BOTH = BRICK + ("pool",)
VMEM = pltpu.VMEM
SMEM = pltpu.SMEM
f32 = jnp.float32
bf16 = jnp.bfloat16

ref_lambda = 5.5
ref_shear = 5.5


def green_table():
    index = np.arange(G)

    def operator(ix, iy, iz):
        wave = [np.where(2 * m < G, m, m - G).astype(np.float64) for m in (ix, iy, iz)]
        kx, ky, kz = np.broadcast_arrays(wave[0], wave[1], wave[2])
        square = kx * kx + ky * ky + kz * kz
        safe = np.where(square > 0, square, 1.0)
        first = np.where(square > 0, 1.0 / (2.0 * ref_shear * safe), 0.0)
        factor = (ref_lambda + ref_shear) / (ref_shear * (ref_lambda + 2.0 * ref_shear))
        second = np.where(square > 0, factor / (safe * safe), 0.0)
        zero, one = np.zeros_like(kx), np.ones_like(kx)
        columns = []
        for j in range(6):
            xx, yy, zz, yz, xz, xy = [one if j == c else zero for c in range(6)]
            wx = xx * kx + xy * ky + xz * kz
            wy = xy * kx + yy * ky + yz * kz
            wz = xz * kx + yz * ky + zz * kz
            s = (wx * kx + wy * ky + wz * kz) * second
            columns.append(
                np.stack(
                    [
                        first * 2 * kx * wx - s * kx * kx,
                        first * 2 * ky * wy - s * ky * ky,
                        first * 2 * kz * wz - s * kz * kz,
                        first * (ky * wz + kz * wy) - s * ky * kz,
                        first * (kx * wz + kz * wx) - s * kx * kz,
                        first * (kx * wy + ky * wx) - s * kx * ky,
                        zero,
                        zero,
                    ]
                )
            )
        return np.stack(columns)

    ix, iy, iz = index[:, None, None], index[None, :, None], index[None, None, :]
    table = 0.5 * (operator(ix, iy, iz) + operator((-ix) % G, (-iy) % G, (-iz) % G)) / NV
    table = table.reshape(6, 8, G, G * G).transpose(2, 0, 1, 3)
    pairs, alone = half_plane()
    even, odd = np.concatenate([pairs, alone[:2]]), np.concatenate([pairs, alone[2:]])
    return np.stack([table[..., even], table[..., odd]]).astype(np.float32)


def half_plane():
    index = np.arange(G * G)
    mirror = (-(index // G)) % G * G + (-(index % G)) % G
    return index[index < mirror], index[index == mirror]


def plane_tables():
    pairs, alone = half_plane()
    plane = np.arange(G * G)

    def angle(k):
        turns = (plane[:, None] // G * (k // G)[None, :] + plane[:, None] % G * (k % G)[None, :]) % G
        return turns * (2 * np.pi / G)

    there = np.concatenate(
        [
            np.cos(angle(pairs)),
            np.cos(angle(alone[:2])),
            -np.sin(angle(pairs)),
            np.cos(angle(alone[2:])),
        ],
        axis=1,
    )
    weight = np.full((G * G, 1), 2.0)
    weight[[126, 127, 254, 255]] = 1.0
    parts = []
    for table in (there, weight * there.T):
        high = table.astype(np.float32).astype(bf16)
        parts += [high, (table - high.astype(np.float64)).astype(np.float32).astype(bf16)]
    return np.stack(parts)


def twiddle(value, power, sign):
    re, im = value
    power %= 16
    if power == 0:
        return re, im
    if power == 4:
        return (-im, re) if sign > 0 else (im, -re)
    if power == 8:
        return -re, -im
    if power == 12:
        return (im, -re) if sign > 0 else (-im, re)
    angle = sign * 2 * math.pi * power / 16
    c, s = math.cos(angle), math.sin(angle)
    if power % 4 == 2:
        h = abs(c)
        a = re if c > 0 else -re
        b = im if c > 0 else -im
        if c * s > 0:
            return (a - b) * h, (a + b) * h
        return (a + b) * h, (b - a) * h
    return re * c - im * s, re * s + im * c


def dft4(v, sign):
    (ar, ai), (br, bi), (cr, ci), (dr, di) = v
    pr, pi_ = ar + cr, ai + ci
    mr, mi = ar - cr, ai - ci
    qr, qi = br + dr, bi + di
    nr, ni = br - dr, bi - di
    if sign < 0:
        jr, ji = ni, -nr
    else:
        jr, ji = -ni, nr
    return [(pr + qr, pi_ + qi), (mr + jr, mi + ji), (pr - qr, pi_ - qi), (mr - jr, mi - ji)]


def dft16(values, sign):
    inner = []
    for n2 in range(4):
        inner.append(dft4([values[n2 + 4 * n1] for n1 in range(4)], sign))
    out = [None] * 16
    for k1 in range(4):
        column = dft4([twiddle(inner[n2][k1], n2 * k1, sign) for n2 in range(4)], sign)
        for k2 in range(4):
            out[k1 + 4 * k2] = column[k2]
    return out


def slab_stress(d, first_rows):
    wide = d.shape
    trace = d[0:1] + d[1:2] + d[2:3]
    lam_trace = jnp.broadcast_to(d[6:7] * trace, wide)
    twice = jnp.broadcast_to(2.0 * d[7:8], wide)
    return twice * d + jnp.where(first_rows, lam_trace, 0.0)


def plane_product(x, cmat, at):
    high = x.astype(bf16)
    low = (x - high.astype(f32)).astype(bf16)
    rows = x.shape[0]
    both = jnp.dot(jnp.concatenate([high, low], axis=0), cmat[at], preferred_element_type=f32)
    return both[:rows] + both[rows:] + jnp.dot(high, cmat[at + 1], preferred_element_type=f32)


def cells_kernel(
    count, owner, element, disp, nm, grads, micro, green, cmat, send, band_stress, replace, st, *work
):
    half_rows = 8 * G
    lane = lax.broadcasted_iota(jnp.int32, (8, LANES), 1)
    row = lax.broadcasted_iota(jnp.int32, (8, LANES), 0)
    row_wide = lax.broadcasted_iota(jnp.int32, (8, 2 * LANES), 0)
    first_rows = row_wide < 3

    targets = []
    for k in range(4):
        e = element[0, k]
        base = pl.multiple_of(e // LANES * LANES, LANES)
        at = lane == e % LANES

        def pick(tile):
            return jnp.sum(jnp.where(at, tile, 0.0), axis=1, keepdims=True)

        node = pick(nm[:, pl.ds(base, LANES)].astype(f32)).astype(jnp.int32)
        shape = [jnp.broadcast_to(pick(grads[j, :, pl.ds(base, LANES)]), (8, LANES)) for j in range(3)]
        node = jnp.broadcast_to(node, (8, LANES)) - lane
        found = [jnp.zeros((8, LANES), f32) for _ in range(3)]
        for r in range(72):
            hit = node == r * LANES
            for c in range(3):
                values = jnp.broadcast_to(disp[c : c + 1, r * LANES : (r + 1) * LANES], (8, LANES))
                found[c] = jnp.where(hit, values, found[c])
        u = [jnp.sum(found[c], axis=1, keepdims=True) for c in range(3)]

        def total(value):
            return jnp.sum(value, axis=0, keepdims=True)

        parts = [
            total(u[0] * shape[0]),
            total(u[1] * shape[1]),
            total(u[2] * shape[2]),
            0.5 * total(u[1] * shape[2] + u[2] * shape[1]),
            0.5 * total(u[0] * shape[2] + u[2] * shape[0]),
            0.5 * total(u[0] * shape[1] + u[1] * shape[0]),
        ]
        target = jnp.zeros((8, LANES), f32)
        for c in range(6):
            target = jnp.where(row == c, jnp.broadcast_to(parts[c], (8, LANES)), target)
        targets.append(target)

    def slab(k, x, iteration):
        if iteration == 0:
            return micro[k, :, 2 * LANES * x : 2 * LANES * (x + 1)]
        return st[k, 8 * x : 8 * x + 8, :]

    shifts = []
    for k in range(4):
        total = jnp.zeros((8, 2 * LANES), f32)
        for x in range(G):
            total = total + slab(k, x, 0)
        mean = jnp.sum(total, axis=1, keepdims=True) * (1.0 / NV)
        shift = jnp.where(row < 6, targets[k] - mean, 0.0)
        shifts.append(jnp.concatenate([shift, shift], axis=1))

    re_cols, im_cols = slice(0, LANES), slice(LANES, 2 * LANES)
    own_mirror = lane >= 126
    whole_mirror = lax.broadcasted_iota(jnp.int32, (half_rows, LANES), 1) >= 126
    for iteration in range(ITERS):
        for pair in range(2):
            plane, spectrum = work[2 * pair], work[2 * pair + 1]
            at = [[cell * half_rows + 8 * x for x in range(G)] for cell in range(2)]
            for cell in range(2):
                for x in range(G):
                    a = at[cell][x]
                    plane[a : a + 8, :] = slab_stress(slab(2 * pair + cell, x, iteration), first_rows)
            plane[...] = plane_product(plane[...], cmat, 0)
            for cell in range(2):
                values = []
                for x in range(G):
                    a = at[cell][x]
                    re, im = plane[a : a + 8, re_cols], plane[a : a + 8, im_cols]
                    if cell == 0:
                        other = at[1][x]
                        im = jnp.where(own_mirror, plane[other : other + 8, re_cols], im)
                    else:
                        other = at[0][x]
                        re = jnp.where(own_mirror, plane[other : other + 8, im_cols], re)
                    values.append((re, im))
                values = dft16(values, -1)
                for x in range(G):
                    a = at[cell][x]
                    spectrum[a : a + 8, re_cols] = values[x][0]
                    spectrum[a : a + 8, im_cols] = values[x][1]
            for cell in range(2):
                updates = []
                for x in range(G):
                    re = im = None
                    for j in range(6):
                        weight = green[cell, x, j]
                        a = at[cell][x] + j
                        tr = weight * jnp.broadcast_to(spectrum[a : a + 1, re_cols], (8, LANES))
                        ti = weight * jnp.broadcast_to(spectrum[a : a + 1, im_cols], (8, LANES))
                        re = tr if re is None else re + tr
                        im = ti if im is None else im + ti
                    updates.append((re, im))
                values = dft16(updates, 1)
                for x in range(G):
                    a = at[cell][x]
                    plane[a : a + 8, re_cols] = values[x][0]
                    plane[a : a + 8, im_cols] = values[x][1]
            first_im = plane[:half_rows, im_cols]
            second_re = plane[half_rows:, re_cols]
            plane[:half_rows, im_cols] = jnp.where(whole_mirror, second_re, first_im)
            plane[half_rows:, re_cols] = jnp.where(whole_mirror, first_im, second_re)
            update = plane_product(plane[...], cmat, 2)
            for cell in range(2):
                k = 2 * pair + cell
                for x in range(G):
                    a = at[cell][x]
                    value = slab(k, x, iteration) - update[a : a + 8, :]
                    if iteration == 0:
                        value = value + shifts[k]
                    st[k, 8 * x : 8 * x + 8, :] = value

    send[pl.ds(8, 4 * TILES, stride=9), :] = jnp.full((4 * TILES, LANES), -1.0, f32)
    result = jnp.zeros((8, LANES), f32)
    for k in range(4):
        live = k < count[0]
        total = jnp.zeros((8, 2 * LANES), f32)
        for x in range(G):
            total = total + slab_stress(st[k, 8 * x : 8 * x + 8, :], first_rows)
        mean = jnp.where(live, jnp.sum(total, axis=1, keepdims=True) * (1.0 / NV), 0.0)
        mean = jnp.broadcast_to(mean, (8, LANES))
        result = jnp.where(lane == k, mean, result)
        across = jnp.sum(jnp.where(lane == row, mean, 0.0), axis=0, keepdims=True)
        band_stress[k : k + 1, :] = across[:, 0:6]
        pool = owner[0, k] & 3

        @pl.when(live)
        def _():
            for i in range(TILES):
                x, part = i // 2, i % 2
                send[pl.ds(9 * (4 * i + pool), 8), :] = st[
                    k, 8 * x : 8 * x + 8, part * LANES : (part + 1) * LANES
                ]
            brick = (owner[0, k] >> 2).astype(f32)
            send[pl.ds(9 * pool + 8, TILES, stride=36), :] = jnp.full((TILES, LANES), brick, f32)

    for k in range(4):
        live_element = jnp.where(k < count[0], element[0, k], -1).astype(f32)
        result = jnp.where((lane == k) & (row == 6), live_element, result)
    replace[...] = result[:, 0:4]


def solve_cells(count, owner, element, disp, nm, grads, micro, green, cmat):
    return pl.pallas_call(
        cells_kernel,
        out_shape=(
            jax.ShapeDtypeStruct((36 * TILES, LANES), f32),
            jax.ShapeDtypeStruct((4, 6), f32),
            jax.ShapeDtypeStruct((8, 4), f32),
        ),
        in_specs=[pl.BlockSpec(memory_space=SMEM)] * 3 + [pl.BlockSpec(memory_space=VMEM)] * 6,
        out_specs=(pl.BlockSpec(memory_space=VMEM),) * 3,
        scratch_shapes=[
            VMEM((4, 8 * G, 2 * LANES), f32),
        ]
        + [VMEM((16 * G, 2 * LANES), f32)] * 4,
        compiler_params=pltpu.CompilerParams(vmem_limit_bytes=56 << 20),
        name="cells",
    )(count, owner, element, disp, nm, grads, micro, green, cmat)


def one_hot_sum(node, values, width):
    def spread(row, rows):
        return jnp.broadcast_to(jnp.broadcast_to(row, (16, width)).astype(bf16)[None], (rows // 16, 16, width)).reshape(
            rows, width
        )

    def index(rows):
        return lax.broadcasted_iota(jnp.int32, (rows, width), 0).astype(f32).astype(bf16)

    coarse = index(HI) == spread((node >> 8).astype(f32), HI)
    fine = index(LO) == spread((node & 255).astype(f32), LO)
    left = jnp.concatenate(
        [jnp.where(coarse, spread(v, HI), jnp.zeros((HI, width), bf16)) for v in values], axis=0
    )
    right = jnp.where(fine, jnp.ones((LO, width), bf16), jnp.zeros((LO, width), bf16))
    return left, right


def halves(value):
    high = value.astype(bf16).astype(f32)
    return high, value - high


def pack_table(disp, table, step):
    largest = jnp.zeros((3, LANES), f32)
    for r in range(72):
        largest = jnp.maximum(largest, jnp.abs(disp[:, r * LANES : (r + 1) * LANES]))
    largest = jnp.maximum(jnp.max(largest, axis=0, keepdims=True), 1e-30)
    step[...] = largest * (1.0 / STEPS)
    scale = jnp.broadcast_to(STEPS / largest, (3, LANES))
    for r in range(72):
        cols = slice(r * LANES, (r + 1) * LANES)
        level = jnp.floor(disp[:, cols] * scale + (OFFSET + 0.5)).astype(jnp.int32)
        last = level[2:3]
        parts = jnp.concatenate([(last & 0x7FF) << 21, (last >> 11) << 21], axis=0)
        table[:, cols] = level[0:2] | parts


def unpack(first, second, step):
    mask = (1 << 21) - 1
    last = lax.shift_right_logical(first, 21) | (lax.shift_right_logical(second, 21) << 11)
    return [(level - OFFSET).astype(f32) * step for level in (first & mask, second & mask, last)]


def macro_tiles(begin, end, unroll, replace, table, step_of, nm, grads, volumes, moduli, sums):
    lane = lax.broadcasted_iota(jnp.int32, (1, LANES), 1).astype(f32)
    steps = jnp.broadcast_to(step_of[...], (8, LANES))

    def scatter(node, forces):
        values = []
        for force in forces:
            values += list(halves(force))
        total = None
        for s in range(0, 8, 2):
            lefts, rights = [], []
            for q in (s, s + 1):
                left, right = one_hot_sum(node[q : q + 1], [v[q : q + 1] for v in values], LANES)
                lefts.append(left)
                rights.append(right)
            product = lax.dot_general(
                jnp.concatenate(lefts, axis=1),
                jnp.concatenate(rights, axis=1),
                (((1,), (1,)), ((), ())),
                preferred_element_type=f32,
            )
            total = product if total is None else total + product
        return total

    def forces_of(t):
        cols = pl.ds(pl.multiple_of(t * LANES, LANES), LANES)
        node = nm[:, cols]
        hi, lo = node >> 7, node & 127
        words = [jnp.zeros((8, LANES), jnp.int32) for _ in range(2)]
        for r in range(72):
            hit = hi == r
            for w in range(2):
                values = jnp.broadcast_to(table[w : w + 1, r * LANES : (r + 1) * LANES], (8, LANES))
                found = jnp.take_along_axis(values, lo, axis=1, mode="promise_in_bounds")
                words[w] = jnp.where(hit, found, words[w])
        u = unpack(*words, jnp.take_along_axis(steps, lo, axis=1, mode="promise_in_bounds"))
        g = [grads[j, :, cols] for j in range(3)]

        def total(value):
            return jnp.sum(value, axis=0, keepdims=True)

        strain = [
            total(u[0] * g[0]),
            total(u[1] * g[1]),
            total(u[2] * g[2]),
            0.5 * total(u[1] * g[2] + u[2] * g[1]),
            0.5 * total(u[0] * g[2] + u[2] * g[0]),
            0.5 * total(u[0] * g[1] + u[1] * g[0]),
        ]
        lam = moduli[0:1, cols]
        mu = moduli[1:2, cols]
        volume = volumes[pl.ds(t, 1), :]
        spherical = lam * (strain[0] + strain[1] + strain[2])
        stress = [spherical + 2.0 * mu * strain[c] for c in range(3)]
        stress += [2.0 * mu * strain[c] for c in range(3, 6)]
        for k in range(4):
            hit = lane == replace[6, k] - lax.convert_element_type(t * LANES, f32)
            stress = [jnp.where(hit, replace[c, k], stress[c]) for c in range(6)]
        xx, yy, zz, yz, xz, xy = [
            jnp.broadcast_to(component * volume, (8, LANES)) for component in stress
        ]
        fx = xx * g[0] + xy * g[1] + xz * g[2]
        fy = xy * g[0] + yy * g[1] + yz * g[2]
        fz = xz * g[0] + yz * g[1] + zz * g[2]
        return node, fx, fy, fz

    def group(step):
        return tuple(forces_of(begin + step * unroll + i) for i in range(unroll))

    def add(carry):
        total = None
        for node, *forces in carry:
            part = scatter(node, forces)
            total = part if total is None else total + part
        sums[...] += total

    def body(step, carry):
        add(carry)
        return group(step)

    add(lax.fori_loop(1, (end - begin) // unroll, body, group(0)))


def macro_first_kernel(
    unroll, replace, disp, nm, grads, volumes, moduli, shared, sums, table, step, face_nodes
):
    for i in range(4):
        for half in range(2):
            cols = slice((2 * i + half) * LANES, (2 * i + half + 1) * LANES)
            face_nodes[i, 4 * half : 4 * half + 4, :] = shared[0, :, cols]
    pack_table(disp, table, step)
    sums[...] = jnp.zeros_like(sums)
    macro_tiles(0, SPLIT, unroll, replace, table, step, nm, grads, volumes, moduli, sums)


def face_lists(core, pool):
    return 1 - core, core, 3 - (pool & 1), 2 + (pool & 1)


def macro_last_kernel(
    unroll,
    replace,
    core_index,
    pool_index,
    table,
    step,
    nm,
    grads,
    volumes,
    moduli,
    so_far,
    face_nodes,
    own,
    to_core,
    to_brick,
    to_even,
    to_odd,
    sums,
    faces,
):
    sums[...] = so_far[...]
    macro_tiles(SPLIT, 64, unroll, replace, table, step, nm, grads, volumes, moduli, sums)

    for c in range(3):
        at = 2 * c * HI
        own[c * HI : (c + 1) * HI, :] = sums[at : at + HI, :] + sums[at + HI : at + 2 * HI, :]

    for pair in range(4):
        first, second = 2 * pair, 2 * pair + 1
        node = face_nodes[pair]
        hi, lo = node >> 7, node & 127
        picked = [jnp.zeros((8, LANES), f32) for _ in range(3)]
        for r in range(72):
            hit = hi == r
            for c in range(3):
                at = c * HI + r // 2
                cols = slice(r % 2 * LANES, (r % 2 + 1) * LANES)
                values = jnp.broadcast_to(own[at : at + 1, cols], (8, LANES))
                found = jnp.take_along_axis(values, lo, axis=1, mode="promise_in_bounds")
                picked[c] = jnp.where(hit, found, picked[c])
        for c in range(3):
            for face in range(4):
                faces[face, c : c + 1, first * LANES : (first + 1) * LANES] = picked[c][face : face + 1]
                faces[face, c : c + 1, second * LANES : (second + 1) * LANES] = picked[c][
                    4 + face : 5 + face
                ]
    lists = face_lists(core_index[0], pool_index[0])
    for face, out in zip(lists, (to_core, to_brick, to_even, to_odd)):
        out[...] = faces[face]


def macro_first(*arguments):
    vmem = pl.BlockSpec(memory_space=VMEM)
    return pl.pallas_call(
        functools.partial(macro_first_kernel, UNROLL),
        out_shape=(
            jax.ShapeDtypeStruct((6 * HI, LO), f32),
            jax.ShapeDtypeStruct((2, 72 * LANES), jnp.int32),
            jax.ShapeDtypeStruct((1, LANES), f32),
            jax.ShapeDtypeStruct((4, 8, LANES), jnp.int32),
        ),
        in_specs=[pl.BlockSpec(memory_space=SMEM)] + [vmem] * 6,
        out_specs=(vmem,) * 4,
        compiler_params=pltpu.CompilerParams(vmem_limit_bytes=32 << 20),
        name="macro_first",
    )(*arguments)


def macro_last(*arguments):
    vmem = pl.BlockSpec(memory_space=VMEM)
    return pl.pallas_call(
        functools.partial(macro_last_kernel, UNROLL),
        out_shape=(
            jax.ShapeDtypeStruct((3 * HI, LO), f32),
        )
        + (jax.ShapeDtypeStruct((3, 1024), f32),) * 4,
        in_specs=[pl.BlockSpec(memory_space=SMEM)] * 3 + [vmem] * 8,
        out_specs=(vmem,) * 5,
        scratch_shapes=[VMEM((6 * HI, LO), f32), VMEM((4, 3, 1024), f32)],
        compiler_params=pltpu.CompilerParams(vmem_limit_bytes=32 << 20),
        name="macro_last",
    )(*arguments)


def assemble_kernel(
    core_index, pool_index, own, shared, r0, r1, r2, r3, external, mass, pieces, out, fields, joined, sem
):
    for i in range(TILES):
        for s in range(2):
            joined[s, :, i * LANES : (i + 1) * LANES] = pieces[i, s]
    copy = pltpu.make_async_copy(joined, fields, sem)
    copy.start()
    total = None
    for face, arrived in zip(face_lists(core_index[0], pool_index[0]), (r0, r1, r2, r3)):
        for part in range(4):
            cols = slice(part * LO, (part + 1) * LO)
            values = []
            for c in range(3):
                values += list(halves(arrived[c : c + 1, cols]))
            left, right = one_hot_sum(shared[0, pl.ds(face, 1), cols], values, LO)
            product = lax.dot_general(
                left, right, (((1,), (1,)), ((), ())), preferred_element_type=f32
            )
            total = product if total is None else total + product
    for c in range(3):
        at = 2 * c * HI
        whole = own[c * HI : (c + 1) * HI, :] + total[at : at + HI] + total[at + HI : at + 2 * HI]
        for r in range(36):
            out[c : c + 1, r * LO : (r + 1) * LO] = whole[r : r + 1]
    out[...] = (external[...] - out[...]) / mass[...]
    copy.wait()


def assemble(place, own, shared, arrived, external, mass, pieces):
    vmem = pl.BlockSpec(memory_space=VMEM)
    return pl.pallas_call(
        assemble_kernel,
        out_shape=(
            jax.ShapeDtypeStruct(external.shape, f32),
            jax.ShapeDtypeStruct((2, 8, NV), f32),
        ),
        in_specs=[pl.BlockSpec(memory_space=SMEM)] * 2 + [vmem] * 9,
        out_specs=(vmem, pl.BlockSpec(memory_space=pl.ANY)),
        scratch_shapes=[VMEM((2, 8, NV), f32), pltpu.SemaphoreType.DMA],
        compiler_params=pltpu.CompilerParams(vmem_limit_bytes=32 << 20),
        name="assemble",
    )(*place, own, shared, *arrived, external, mass, pieces)


def sort_kernel(pieces, out, order, places, sem):
    blocks = pieces.shape[0] // 9
    lane = lax.broadcasted_iota(jnp.int32, (blocks, LANES), 1)
    block = lax.broadcasted_iota(jnp.int32, (blocks, LANES), 0)
    hit = pieces[pl.ds(8, blocks, stride=9), :] == lane.astype(f32)
    order[0:1, :] = jnp.min(jnp.where(hit, block, blocks - 1), axis=0, keepdims=True)
    order[1:2, :] = jnp.max(jnp.where(hit, block, 0), axis=0, keepdims=True)
    copy = pltpu.make_async_copy(order, places, sem)
    copy.start()
    copy.wait()
    for b in range(out.shape[0]):
        for s in range(2):
            out[b, s] = pieces[pl.ds(9 * places[s, b], 8), :]


def sort_pieces(pieces, bricks):
    vmem = pl.BlockSpec(memory_space=VMEM)
    return pl.pallas_call(
        sort_kernel,
        out_shape=jax.ShapeDtypeStruct((bricks, 2, 8, LANES), f32),
        in_specs=[vmem],
        out_specs=vmem,
        scratch_shapes=[VMEM((8, LANES), jnp.int32), SMEM((8, LANES), jnp.int32), pltpu.SemaphoreType.DMA],
        compiler_params=pltpu.CompilerParams(vmem_limit_bytes=32 << 20),
        name="sort_pieces",
    )(pieces)


def shards(
    displacement,
    node_map,
    shape_grads,
    volumes,
    elastic_moduli,
    external_force,
    nodal_mass,
    shared_nodes,
    band_count,
    band_owner,
    band_element,
    micro_fields,
):
    bricks, pools = lax.axis_size(BRICK), lax.axis_size("pool")
    place = tuple(lax.axis_index(axis).astype(jnp.int32).reshape(1) for axis in ("core", "pool"))
    send, band_stress, replace = solve_cells(
        band_count,
        band_owner,
        band_element,
        displacement,
        node_map,
        shape_grads,
        micro_fields,
        jnp.asarray(green_table()),
        jnp.asarray(plane_tables()),
    )
    pieces = lax.all_to_all(
        send.reshape(bricks * pools, 1, 9 * LANES), BOTH, split_axis=0, concat_axis=0, tiled=True
    )
    dense = (node_map, shape_grads, volumes.reshape(64, LANES), elastic_moduli)
    so_far, table, step, face_nodes = macro_first(replace, displacement, *dense, shared_nodes)
    pieces, so_far = lax.optimization_barrier((pieces, so_far))
    sorted_pieces = sort_pieces(pieces.reshape(9 * bricks * pools, LANES), bricks)
    sorted_pieces, so_far = lax.optimization_barrier((sorted_pieces, so_far))
    mine = lax.all_to_all(sorted_pieces, BRICK, split_axis=0, concat_axis=0, tiled=True)
    own, *faces = macro_last(replace, *place, table, step, *dense, so_far, face_nodes)

    def swap(array, axis, size, first):
        steps = [(i, i + 1) for i in range(first, size - 1, 2)]
        return lax.ppermute(array, axis, steps + [(j, i) for i, j in steps])

    arrived = (
        swap(faces[0], "core", 2, 0),
        swap(faces[1], BRICK, bricks, 1),
        swap(faces[2], "pool", pools, 0),
        swap(faces[3], "pool", pools, 1),
    )
    acceleration, owned_fields = assemble(
        place, own, shared_nodes, arrived, external_force, nodal_mass.reshape(1, -1), mine
    )
    return (acceleration, band_stress.T, owned_fields)


def solution(mesh):
    bricks, pools = mesh.devices.shape
    split = jax.sharding.Mesh(
        mesh.devices.reshape(4, bricks // 8, 2, pools), ("row", "pair", "core", "pool")
    )
    placed = (
        P(None, BOTH),
        P(None, BOTH),
        P(None, None, BOTH),
        P(BOTH),
        P(None, BOTH),
        P(None, BOTH),
        P(BOTH),
        P(BOTH, None, None),
        P(BOTH),
        P(BOTH, None),
        P(BOTH, None),
        P(BOTH, None, None),
    )
    return jax.shard_map(
        shards,
        mesh=split,
        in_specs=placed,
        out_specs=(P(None, BOTH), P(None, BOTH), P(BOTH, None, None)),
        check_vma=False,
    )
```

```python
import functools
import math

import jax
import jax.numpy as jnp
import numpy as np
from jax import lax
from jax.experimental import pallas as pl
from jax.experimental.pallas import tpu as pltpu
from jax.sharding import PartitionSpec as P

G = 16
NV = 4096
ITERS = 2
LANES = 128
TILES = 32
HI = 48
LO = 256
STEPS = float((1 << 20) - 2)
OFFSET = 1 << 20
UNROLL = 4
SPLIT = 48
BRICK = ("row", "pair", "core")
BOTH = BRICK + ("pool",)
VMEM = pltpu.VMEM
SMEM = pltpu.SMEM
f32 = jnp.float32
bf16 = jnp.bfloat16

ref_lambda = 5.5
ref_shear = 5.5


def green_table():
    index = np.arange(G)

    def operator(ix, iy, iz):
        wave = [np.where(2 * m < G, m, m - G).astype(np.float64) for m in (ix, iy, iz)]
        kx, ky, kz = np.broadcast_arrays(wave[0], wave[1], wave[2])
        square = kx * kx + ky * ky + kz * kz
        safe = np.where(square > 0, square, 1.0)
        first = np.where(square > 0, 1.0 / (2.0 * ref_shear * safe), 0.0)
        factor = (ref_lambda + ref_shear) / (ref_shear * (ref_lambda + 2.0 * ref_shear))
        second = np.where(square > 0, factor / (safe * safe), 0.0)
        zero, one = np.zeros_like(kx), np.ones_like(kx)
        columns = []
        for j in range(6):
            xx, yy, zz, yz, xz, xy = [one if j == c else zero for c in range(6)]
            wx = xx * kx + xy * ky + xz * kz
            wy = xy * kx + yy * ky + yz * kz
            wz = xz * kx + yz * ky + zz * kz
            s = (wx * kx + wy * ky + wz * kz) * second
            columns.append(
                np.stack(
                    [
                        first * 2 * kx * wx - s * kx * kx,
                        first * 2 * ky * wy - s * ky * ky,
                        first * 2 * kz * wz - s * kz * kz,
                        first * (ky * wz + kz * wy) - s * ky * kz,
                        first * (kx * wz + kz * wx) - s * kx * kz,
                        first * (kx * wy + ky * wx) - s * kx * ky,
                        zero,
                        zero,
                    ]
                )
            )
        return np.stack(columns)

    ix, iy, iz = index[:, None, None], index[None, :, None], index[None, None, :]
    table = 0.5 * (operator(ix, iy, iz) + operator((-ix) % G, (-iy) % G, (-iz) % G)) / NV
    table = table.reshape(6, 8, G, G * G).transpose(2, 0, 1, 3)
    pairs, alone = half_plane()
    even, odd = np.concatenate([pairs, alone[:2]]), np.concatenate([pairs, alone[2:]])
    return np.stack([table[..., even], table[..., odd]]).astype(np.float32)


def half_plane():
    index = np.arange(G * G)
    mirror = (-(index // G)) % G * G + (-(index % G)) % G
    return index[index < mirror], index[index == mirror]


def plane_tables():
    pairs, alone = half_plane()
    plane = np.arange(G * G)

    def angle(k):
        turns = (plane[:, None] // G * (k // G)[None, :] + plane[:, None] % G * (k % G)[None, :]) % G
        return turns * (2 * np.pi / G)

    there = np.concatenate(
        [
            np.cos(angle(pairs)),
            np.cos(angle(alone[:2])),
            -np.sin(angle(pairs)),
            np.cos(angle(alone[2:])),
        ],
        axis=1,
    )
    weight = np.full((G * G, 1), 2.0)
    weight[[126, 127, 254, 255]] = 1.0
    parts = []
    for table in (there, weight * there.T):
        high = table.astype(np.float32).astype(bf16)
        parts += [high, (table - high.astype(np.float64)).astype(np.float32).astype(bf16)]
    return np.stack(parts)


def twiddle(value, power, sign):
    re, im = value
    power %= 16
    if power == 0:
        return re, im
    if power == 4:
        return (-im, re) if sign > 0 else (im, -re)
    if power == 8:
        return -re, -im
    if power == 12:
        return (im, -re) if sign > 0 else (-im, re)
    angle = sign * 2 * math.pi * power / 16
    c, s = math.cos(angle), math.sin(angle)
    if power % 4 == 2:
        h = abs(c)
        a = re if c > 0 else -re
        b = im if c > 0 else -im
        if c * s > 0:
            return (a - b) * h, (a + b) * h
        return (a + b) * h, (b - a) * h
    return re * c - im * s, re * s + im * c


def dft4(v, sign):
    (ar, ai), (br, bi), (cr, ci), (dr, di) = v
    pr, pi_ = ar + cr, ai + ci
    mr, mi = ar - cr, ai - ci
    qr, qi = br + dr, bi + di
    nr, ni = br - dr, bi - di
    if sign < 0:
        jr, ji = ni, -nr
    else:
        jr, ji = -ni, nr
    return [(pr + qr, pi_ + qi), (mr + jr, mi + ji), (pr - qr, pi_ - qi), (mr - jr, mi - ji)]


def dft16(values, sign):
    inner = []
    for n2 in range(4):
        inner.append(dft4([values[n2 + 4 * n1] for n1 in range(4)], sign))
    out = [None] * 16
    for k1 in range(4):
        column = dft4([twiddle(inner[n2][k1], n2 * k1, sign) for n2 in range(4)], sign)
        for k2 in range(4):
            out[k1 + 4 * k2] = column[k2]
    return out


def slab_stress(d, first_rows):
    wide = d.shape
    trace = d[0:1] + d[1:2] + d[2:3]
    lam_trace = jnp.broadcast_to(d[6:7] * trace, wide)
    twice = jnp.broadcast_to(2.0 * d[7:8], wide)
    return twice * d + jnp.where(first_rows, lam_trace, 0.0)


def plane_product(x, cmat, at):
    high = x.astype(bf16)
    low = (x - high.astype(f32)).astype(bf16)
    rows = x.shape[0]
    both = jnp.dot(jnp.concatenate([high, low], axis=0), cmat[at], preferred_element_type=f32)
    return both[:rows] + both[rows:] + jnp.dot(high, cmat[at + 1], preferred_element_type=f32)


def cells_kernel(
    count, owner, element, disp, nm, grads, micro, green, cmat, send, band_stress, replace, st, *work
):
    half_rows = 8 * G
    lane = lax.broadcasted_iota(jnp.int32, (8, LANES), 1)
    row = lax.broadcasted_iota(jnp.int32, (8, LANES), 0)
    row_wide = lax.broadcasted_iota(jnp.int32, (8, 2 * LANES), 0)
    first_rows = row_wide < 3

    targets = []
    for k in range(4):
        e = element[0, k]
        base = pl.multiple_of(e // LANES * LANES, LANES)
        at = lane == e % LANES

        def pick(tile):
            return jnp.sum(jnp.where(at, tile, 0.0), axis=1, keepdims=True)

        node = pick(nm[:, pl.ds(base, LANES)].astype(f32)).astype(jnp.int32)
        shape = [jnp.broadcast_to(pick(grads[j, :, pl.ds(base, LANES)]), (8, LANES)) for j in range(3)]
        node = jnp.broadcast_to(node, (8, LANES)) - lane
        found = [jnp.zeros((8, LANES), f32) for _ in range(3)]
        for r in range(72):
            hit = node == r * LANES
            for c in range(3):
                values = jnp.broadcast_to(disp[c : c + 1, r * LANES : (r + 1) * LANES], (8, LANES))
                found[c] = jnp.where(hit, values, found[c])
        u = [jnp.sum(found[c], axis=1, keepdims=True) for c in range(3)]

        def total(value):
            return jnp.sum(value, axis=0, keepdims=True)

        parts = [
            total(u[0] * shape[0]),
            total(u[1] * shape[1]),
            total(u[2] * shape[2]),
            0.5 * total(u[1] * shape[2] + u[2] * shape[1]),
            0.5 * total(u[0] * shape[2] + u[2] * shape[0]),
            0.5 * total(u[0] * shape[1] + u[1] * shape[0]),
        ]
        target = jnp.zeros((8, LANES), f32)
        for c in range(6):
            target = jnp.where(row == c, jnp.broadcast_to(parts[c], (8, LANES)), target)
        targets.append(target)

    def slab(k, x, iteration):
        if iteration == 0:
            return micro[k, :, 2 * LANES * x : 2 * LANES * (x + 1)]
        return st[k, 8 * x : 8 * x + 8, :]

    shifts = []
    for k in range(4):
        total = jnp.zeros((8, 2 * LANES), f32)
        for x in range(G):
            total = total + slab(k, x, 0)
        mean = jnp.sum(total, axis=1, keepdims=True) * (1.0 / NV)
        shift = jnp.where(row < 6, targets[k] - mean, 0.0)
        shifts.append(jnp.concatenate([shift, shift], axis=1))

    re_cols, im_cols = slice(0, LANES), slice(LANES, 2 * LANES)
    own_mirror = lane >= 126
    whole_mirror = lax.broadcasted_iota(jnp.int32, (half_rows, LANES), 1) >= 126
    for iteration in range(ITERS):
        for pair in range(2):
            plane, spectrum = work[2 * pair], work[2 * pair + 1]
            at = [[cell * half_rows + 8 * x for x in range(G)] for cell in range(2)]
            for cell in range(2):
                for x in range(G):
                    a = at[cell][x]
                    plane[a : a + 8, :] = slab_stress(slab(2 * pair + cell, x, iteration), first_rows)
            plane[...] = plane_product(plane[...], cmat, 0)
            for cell in range(2):
                values = []
                for x in range(G):
                    a = at[cell][x]
                    re, im = plane[a : a + 8, re_cols], plane[a : a + 8, im_cols]
                    if cell == 0:
                        other = at[1][x]
                        im = jnp.where(own_mirror, plane[other : other + 8, re_cols], im)
                    else:
                        other = at[0][x]
                        re = jnp.where(own_mirror, plane[other : other + 8, im_cols], re)
                    values.append((re, im))
                values = dft16(values, -1)
                for x in range(G):
                    a = at[cell][x]
                    spectrum[a : a + 8, re_cols] = values[x][0]
                    spectrum[a : a + 8, im_cols] = values[x][1]
            for cell in range(2):
                updates = []
                for x in range(G):
                    re = im = None
                    for j in range(6):
                        weight = green[cell, x, j]
                        a = at[cell][x] + j
                        tr = weight * jnp.broadcast_to(spectrum[a : a + 1, re_cols], (8, LANES))
                        ti = weight * jnp.broadcast_to(spectrum[a : a + 1, im_cols], (8, LANES))
                        re = tr if re is None else re + tr
                        im = ti if im is None else im + ti
                    updates.append((re, im))
                values = dft16(updates, 1)
                for x in range(G):
                    a = at[cell][x]
                    plane[a : a + 8, re_cols] = values[x][0]
                    plane[a : a + 8, im_cols] = values[x][1]
            first_im = plane[:half_rows, im_cols]
            second_re = plane[half_rows:, re_cols]
            plane[:half_rows, im_cols] = jnp.where(whole_mirror, second_re, first_im)
            plane[half_rows:, re_cols] = jnp.where(whole_mirror, first_im, second_re)
            update = plane_product(plane[...], cmat, 2)
            for cell in range(2):
                k = 2 * pair + cell
                for x in range(G):
                    a = at[cell][x]
                    value = slab(k, x, iteration) - update[a : a + 8, :]
                    if iteration == 0:
                        value = value + shifts[k]
                    st[k, 8 * x : 8 * x + 8, :] = value

    send[pl.ds(8, 4 * TILES, stride=9), :] = jnp.full((4 * TILES, LANES), -1.0, f32)
    result = jnp.zeros((8, LANES), f32)
    for k in range(4):
        live = k < count[0]
        total = jnp.zeros((8, 2 * LANES), f32)
        for x in range(G):
            total = total + slab_stress(st[k, 8 * x : 8 * x + 8, :], first_rows)
        mean = jnp.where(live, jnp.sum(total, axis=1, keepdims=True) * (1.0 / NV), 0.0)
        mean = jnp.broadcast_to(mean, (8, LANES))
        result = jnp.where(lane == k, mean, result)
        across = jnp.sum(jnp.where(lane == row, mean, 0.0), axis=0, keepdims=True)
        band_stress[k : k + 1, :] = across[:, 0:6]
        pool = owner[0, k] & 3

        @pl.when(live)
        def _():
            for i in range(TILES):
                x, part = i // 2, i % 2
                send[pl.ds(9 * (4 * i + pool), 8), :] = st[
                    k, 8 * x : 8 * x + 8, part * LANES : (part + 1) * LANES
                ]
            brick = (owner[0, k] >> 2).astype(f32)
            send[pl.ds(9 * pool + 8, TILES, stride=36), :] = jnp.full((TILES, LANES), brick, f32)

    for k in range(4):
        live_element = jnp.where(k < count[0], element[0, k], -1).astype(f32)
        result = jnp.where((lane == k) & (row == 6), live_element, result)
    replace[...] = result[:, 0:4]


def solve_cells(count, owner, element, disp, nm, grads, micro, green, cmat):
    return pl.pallas_call(
        cells_kernel,
        out_shape=(
            jax.ShapeDtypeStruct((36 * TILES, LANES), f32),
            jax.ShapeDtypeStruct((4, 6), f32),
            jax.ShapeDtypeStruct((8, 4), f32),
        ),
        in_specs=[pl.BlockSpec(memory_space=SMEM)] * 3 + [pl.BlockSpec(memory_space=VMEM)] * 6,
        out_specs=(pl.BlockSpec(memory_space=VMEM),) * 3,
        scratch_shapes=[
            VMEM((4, 8 * G, 2 * LANES), f32),
        ]
        + [VMEM((16 * G, 2 * LANES), f32)] * 4,
        compiler_params=pltpu.CompilerParams(vmem_limit_bytes=56 << 20),
        name="cells",
    )(count, owner, element, disp, nm, grads, micro, green, cmat)


def one_hot_sum(node, values, width):
    def spread(row, rows):
        return jnp.broadcast_to(jnp.broadcast_to(row, (16, width)).astype(bf16)[None], (rows // 16, 16, width)).reshape(
            rows, width
        )

    def index(rows):
        return lax.broadcasted_iota(jnp.int32, (rows, width), 0).astype(f32).astype(bf16)

    coarse = index(HI) == spread((node >> 8).astype(f32), HI)
    fine = index(LO) == spread((node & 255).astype(f32), LO)
    left = jnp.concatenate(
        [jnp.where(coarse, spread(v, HI), jnp.zeros((HI, width), bf16)) for v in values], axis=0
    )
    right = jnp.where(fine, jnp.ones((LO, width), bf16), jnp.zeros((LO, width), bf16))
    return left, right


def halves(value):
    high = value.astype(bf16).astype(f32)
    return high, value - high


def pack_table(disp, table, step):
    largest = jnp.zeros((3, LANES), f32)
    for r in range(72):
        largest = jnp.maximum(largest, jnp.abs(disp[:, r * LANES : (r + 1) * LANES]))
    largest = jnp.maximum(jnp.max(largest, axis=0, keepdims=True), 1e-30)
    step[...] = largest * (1.0 / STEPS)
    scale = jnp.broadcast_to(STEPS / largest, (3, LANES))
    for r in range(72):
        cols = slice(r * LANES, (r + 1) * LANES)
        level = jnp.floor(disp[:, cols] * scale + (OFFSET + 0.5)).astype(jnp.int32)
        last = level[2:3]
        parts = jnp.concatenate([(last & 0x7FF) << 21, (last >> 11) << 21], axis=0)
        table[:, cols] = level[0:2] | parts


def unpack(first, second, step):
    mask = (1 << 21) - 1
    last = lax.shift_right_logical(first, 21) | (lax.shift_right_logical(second, 21) << 11)
    return [(level - OFFSET).astype(f32) * step for level in (first & mask, second & mask, last)]


def macro_tiles(begin, end, unroll, replace, table, step_of, nm, grads, volumes, moduli, sums):
    lane = lax.broadcasted_iota(jnp.int32, (1, LANES), 1).astype(f32)
    steps = jnp.broadcast_to(step_of[...], (8, LANES))

    def scatter(node, forces):
        values = []
        for force in forces:
            values += list(halves(force))
        total = None
        for s in range(0, 8, 2):
            lefts, rights = [], []
            for q in (s, s + 1):
                left, right = one_hot_sum(node[q : q + 1], [v[q : q + 1] for v in values], LANES)
                lefts.append(left)
                rights.append(right)
            product = lax.dot_general(
                jnp.concatenate(lefts, axis=1),
                jnp.concatenate(rights, axis=1),
                (((1,), (1,)), ((), ())),
                preferred_element_type=f32,
            )
            total = product if total is None else total + product
        return total

    def forces_of(t):
        cols = pl.ds(pl.multiple_of(t * LANES, LANES), LANES)
        node = nm[:, cols]
        hi, lo = node >> 7, node & 127
        words = [jnp.zeros((8, LANES), jnp.int32) for _ in range(2)]
        for r in range(72):
            hit = hi == r
            for w in range(2):
                values = jnp.broadcast_to(table[w : w + 1, r * LANES : (r + 1) * LANES], (8, LANES))
                found = jnp.take_along_axis(values, lo, axis=1, mode="promise_in_bounds")
                words[w] = jnp.where(hit, found, words[w])
        u = unpack(*words, jnp.take_along_axis(steps, lo, axis=1, mode="promise_in_bounds"))
        g = [grads[j, :, cols] for j in range(3)]

        def total(value):
            return jnp.sum(value, axis=0, keepdims=True)

        strain = [
            total(u[0] * g[0]),
            total(u[1] * g[1]),
            total(u[2] * g[2]),
            0.5 * total(u[1] * g[2] + u[2] * g[1]),
            0.5 * total(u[0] * g[2] + u[2] * g[0]),
            0.5 * total(u[0] * g[1] + u[1] * g[0]),
        ]
        lam = moduli[0:1, cols]
        mu = moduli[1:2, cols]
        volume = volumes[pl.ds(t, 1), :]
        spherical = lam * (strain[0] + strain[1] + strain[2])
        stress = [spherical + 2.0 * mu * strain[c] for c in range(3)]
        stress += [2.0 * mu * strain[c] for c in range(3, 6)]
        for k in range(4):
            hit = lane == replace[6, k] - lax.convert_element_type(t * LANES, f32)
            stress = [jnp.where(hit, replace[c, k], stress[c]) for c in range(6)]
        xx, yy, zz, yz, xz, xy = [
            jnp.broadcast_to(component * volume, (8, LANES)) for component in stress
        ]
        fx = xx * g[0] + xy * g[1] + xz * g[2]
        fy = xy * g[0] + yy * g[1] + yz * g[2]
        fz = xz * g[0] + yz * g[1] + zz * g[2]
        return node, fx, fy, fz

    def group(step):
        return tuple(forces_of(begin + step * unroll + i) for i in range(unroll))

    def add(carry):
        total = None
        for node, *forces in carry:
            part = scatter(node, forces)
            total = part if total is None else total + part
        sums[...] += total

    def body(step, carry):
        add(carry)
        return group(step)

    add(lax.fori_loop(1, (end - begin) // unroll, body, group(0)))


def macro_first_kernel(
    unroll, replace, disp, nm, grads, volumes, moduli, shared, sums, table, step, face_nodes
):
    for i in range(4):
        for half in range(2):
            cols = slice((2 * i + half) * LANES, (2 * i + half + 1) * LANES)
            face_nodes[i, 4 * half : 4 * half + 4, :] = shared[0, :, cols]
    pack_table(disp, table, step)
    sums[...] = jnp.zeros_like(sums)
    macro_tiles(0, SPLIT, unroll, replace, table, step, nm, grads, volumes, moduli, sums)


def face_lists(core, pool):
    return core, 2 + (pool & 1), 3 - (pool & 1), 1 - core


def macro_last_kernel(
    unroll,
    replace,
    core_index,
    pool_index,
    table,
    step,
    nm,
    grads,
    volumes,
    moduli,
    so_far,
    face_nodes,
    own,
    to_brick,
    to_odd,
    to_even,
    to_core,
    sums,
    faces,
):
    sums[...] = so_far[...]
    macro_tiles(SPLIT, 64, unroll, replace, table, step, nm, grads, volumes, moduli, sums)

    for c in range(3):
        at = 2 * c * HI
        own[c * HI : (c + 1) * HI, :] = sums[at : at + HI, :] + sums[at + HI : at + 2 * HI, :]

    for pair in range(4):
        first, second = 2 * pair, 2 * pair + 1
        node = face_nodes[pair]
        hi, lo = node >> 7, node & 127
        picked = [jnp.zeros((8, LANES), f32) for _ in range(3)]
        for r in range(72):
            hit = hi == r
            for c in range(3):
                at = c * HI + r // 2
                cols = slice(r % 2 * LANES, (r % 2 + 1) * LANES)
                values = jnp.broadcast_to(own[at : at + 1, cols], (8, LANES))
                found = jnp.take_along_axis(values, lo, axis=1, mode="promise_in_bounds")
                picked[c] = jnp.where(hit, found, picked[c])
        for c in range(3):
            for face in range(4):
                faces[face, c : c + 1, first * LANES : (first + 1) * LANES] = picked[c][face : face + 1]
                faces[face, c : c + 1, second * LANES : (second + 1) * LANES] = picked[c][
                    4 + face : 5 + face
                ]
    lists = face_lists(core_index[0], pool_index[0])
    for face, out in zip(lists, (to_brick, to_odd, to_even, to_core)):
        out[...] = faces[face]


def macro_first(*arguments):
    vmem = pl.BlockSpec(memory_space=VMEM)
    return pl.pallas_call(
        functools.partial(macro_first_kernel, UNROLL),
        out_shape=(
            jax.ShapeDtypeStruct((6 * HI, LO), f32),
            jax.ShapeDtypeStruct((2, 72 * LANES), jnp.int32),
            jax.ShapeDtypeStruct((1, LANES), f32),
            jax.ShapeDtypeStruct((4, 8, LANES), jnp.int32),
        ),
        in_specs=[pl.BlockSpec(memory_space=SMEM)] + [vmem] * 6,
        out_specs=(vmem,) * 4,
        compiler_params=pltpu.CompilerParams(vmem_limit_bytes=32 << 20),
        name="macro_first",
    )(*arguments)


def macro_last(*arguments):
    vmem = pl.BlockSpec(memory_space=VMEM)
    return pl.pallas_call(
        functools.partial(macro_last_kernel, UNROLL),
        out_shape=(
            jax.ShapeDtypeStruct((3 * HI, LO), f32),
        )
        + (jax.ShapeDtypeStruct((3, 1024), f32),) * 4,
        in_specs=[pl.BlockSpec(memory_space=SMEM)] * 3 + [vmem] * 8,
        out_specs=(vmem,) * 5,
        scratch_shapes=[VMEM((6 * HI, LO), f32), VMEM((4, 3, 1024), f32)],
        compiler_params=pltpu.CompilerParams(vmem_limit_bytes=32 << 20),
        name="macro_last",
    )(*arguments)


def assemble_kernel(
    core_index, pool_index, own, shared, r0, r1, r2, r3, external, mass, pieces, out, fields, joined, sem
):
    for i in range(TILES):
        for s in range(2):
            joined[s, :, i * LANES : (i + 1) * LANES] = pieces[i, s]
    copy = pltpu.make_async_copy(joined, fields, sem)
    copy.start()
    total = None
    for face, arrived in zip(face_lists(core_index[0], pool_index[0]), (r0, r1, r2, r3)):
        for part in range(4):
            cols = slice(part * LO, (part + 1) * LO)
            values = []
            for c in range(3):
                values += list(halves(arrived[c : c + 1, cols]))
            left, right = one_hot_sum(shared[0, pl.ds(face, 1), cols], values, LO)
            product = lax.dot_general(
                left, right, (((1,), (1,)), ((), ())), preferred_element_type=f32
            )
            total = product if total is None else total + product
    for c in range(3):
        at = 2 * c * HI
        whole = own[c * HI : (c + 1) * HI, :] + total[at : at + HI] + total[at + HI : at + 2 * HI]
        for r in range(36):
            out[c : c + 1, r * LO : (r + 1) * LO] = whole[r : r + 1]
    out[...] = (external[...] - out[...]) / mass[...]
    copy.wait()


def assemble(place, own, shared, arrived, external, mass, pieces):
    vmem = pl.BlockSpec(memory_space=VMEM)
    return pl.pallas_call(
        assemble_kernel,
        out_shape=(
            jax.ShapeDtypeStruct(external.shape, f32),
            jax.ShapeDtypeStruct((2, 8, NV), f32),
        ),
        in_specs=[pl.BlockSpec(memory_space=SMEM)] * 2 + [vmem] * 9,
        out_specs=(vmem, pl.BlockSpec(memory_space=pl.ANY)),
        scratch_shapes=[VMEM((2, 8, NV), f32), pltpu.SemaphoreType.DMA],
        compiler_params=pltpu.CompilerParams(vmem_limit_bytes=32 << 20),
        name="assemble",
    )(*place, own, shared, *arrived, external, mass, pieces)


def sort_kernel(pieces, out, order, places, sem):
    blocks = pieces.shape[0] // 9
    lane = lax.broadcasted_iota(jnp.int32, (blocks, LANES), 1)
    block = lax.broadcasted_iota(jnp.int32, (blocks, LANES), 0)
    hit = pieces[pl.ds(8, blocks, stride=9), :] == lane.astype(f32)
    order[0:1, :] = jnp.min(jnp.where(hit, block, blocks - 1), axis=0, keepdims=True)
    order[1:2, :] = jnp.max(jnp.where(hit, block, 0), axis=0, keepdims=True)
    copy = pltpu.make_async_copy(order, places, sem)
    copy.start()
    copy.wait()
    for b in range(out.shape[0]):
        for s in range(2):
            out[b, s] = pieces[pl.ds(9 * places[s, b], 8), :]


def sort_pieces(pieces, bricks):
    vmem = pl.BlockSpec(memory_space=VMEM)
    return pl.pallas_call(
        sort_kernel,
        out_shape=jax.ShapeDtypeStruct((bricks, 2, 8, LANES), f32),
        in_specs=[vmem],
        out_specs=vmem,
        scratch_shapes=[VMEM((8, LANES), jnp.int32), SMEM((8, LANES), jnp.int32), pltpu.SemaphoreType.DMA],
        compiler_params=pltpu.CompilerParams(vmem_limit_bytes=32 << 20),
        name="sort_pieces",
    )(pieces)


def shards(
    displacement,
    node_map,
    shape_grads,
    volumes,
    elastic_moduli,
    external_force,
    nodal_mass,
    shared_nodes,
    band_count,
    band_owner,
    band_element,
    micro_fields,
):
    bricks, pools = lax.axis_size(BRICK), lax.axis_size("pool")
    place = tuple(lax.axis_index(axis).astype(jnp.int32).reshape(1) for axis in ("core", "pool"))
    send, band_stress, replace = solve_cells(
        band_count,
        band_owner,
        band_element,
        displacement,
        node_map,
        shape_grads,
        micro_fields,
        jnp.asarray(green_table()),
        jnp.asarray(plane_tables()),
    )
    pieces = lax.all_to_all(
        send.reshape(bricks * pools, 1, 9 * LANES), BOTH, split_axis=0, concat_axis=0, tiled=True
    )
    dense = (node_map, shape_grads, volumes.reshape(64, LANES), elastic_moduli)
    so_far, table, step, face_nodes = macro_first(replace, displacement, *dense, shared_nodes)
    pieces, so_far = lax.optimization_barrier((pieces, so_far))
    sorted_pieces = sort_pieces(pieces.reshape(9 * bricks * pools, LANES), bricks)
    sorted_pieces, so_far = lax.optimization_barrier((sorted_pieces, so_far))
    mine = lax.all_to_all(sorted_pieces, BRICK, split_axis=0, concat_axis=0, tiled=True)
    own, *faces = macro_last(replace, *place, table, step, *dense, so_far, face_nodes)

    def swap(array, axis, size, first):
        steps = [(i, i + 1) for i in range(first, size - 1, 2)]
        return lax.ppermute(array, axis, steps + [(j, i) for i, j in steps])

    arrived = (
        swap(faces[0], BRICK, bricks, 1),
        swap(faces[1], "pool", pools, 1),
        swap(faces[2], "pool", pools, 0),
        swap(faces[3], "core", 2, 0),
    )
    acceleration, owned_fields = assemble(
        place, own, shared_nodes, arrived, external_force, nodal_mass.reshape(1, -1), mine
    )
    return (acceleration, band_stress.T, owned_fields)


def solution(mesh):
    bricks, pools = mesh.devices.shape
    split = jax.sharding.Mesh(
        mesh.devices.reshape(4, bricks // 8, 2, pools), ("row", "pair", "core", "pool")
    )
    placed = (
        P(None, BOTH),
        P(None, BOTH),
        P(None, None, BOTH),
        P(BOTH),
        P(None, BOTH),
        P(None, BOTH),
        P(BOTH),
        P(BOTH, None, None),
        P(BOTH),
        P(BOTH, None),
        P(BOTH, None),
        P(BOTH, None, None),
    )
    return jax.shard_map(
        shards,
        mesh=split,
        in_specs=placed,
        out_specs=(P(None, BOTH), P(None, BOTH), P(BOTH, None, None)),
        check_vma=False,
    )
```

```python
import functools
import math

import jax
import jax.numpy as jnp
import numpy as np
from jax import lax
from jax.experimental import pallas as pl
from jax.experimental.pallas import tpu as pltpu
from jax.sharding import PartitionSpec as P

G = 16
NV = 4096
ITERS = 2
LANES = 128
TILES = 32
HI = 48
LO = 256
STEPS = float((1 << 20) - 2)
OFFSET = 1 << 20
UNROLL = 4
SPLIT = 48
BRICK = ("row", "pair", "core")
BOTH = BRICK + ("pool",)
VMEM = pltpu.VMEM
SMEM = pltpu.SMEM
f32 = jnp.float32
bf16 = jnp.bfloat16

ref_lambda = 5.5
ref_shear = 5.5


def green_table():
    index = np.arange(G)

    def operator(ix, iy, iz):
        wave = [np.where(2 * m < G, m, m - G).astype(np.float64) for m in (ix, iy, iz)]
        kx, ky, kz = np.broadcast_arrays(wave[0], wave[1], wave[2])
        square = kx * kx + ky * ky + kz * kz
        safe = np.where(square > 0, square, 1.0)
        first = np.where(square > 0, 1.0 / (2.0 * ref_shear * safe), 0.0)
        factor = (ref_lambda + ref_shear) / (ref_shear * (ref_lambda + 2.0 * ref_shear))
        second = np.where(square > 0, factor / (safe * safe), 0.0)
        zero, one = np.zeros_like(kx), np.ones_like(kx)
        columns = []
        for j in range(6):
            xx, yy, zz, yz, xz, xy = [one if j == c else zero for c in range(6)]
            wx = xx * kx + xy * ky + xz * kz
            wy = xy * kx + yy * ky + yz * kz
            wz = xz * kx + yz * ky + zz * kz
            s = (wx * kx + wy * ky + wz * kz) * second
            columns.append(
                np.stack(
                    [
                        first * 2 * kx * wx - s * kx * kx,
                        first * 2 * ky * wy - s * ky * ky,
                        first * 2 * kz * wz - s * kz * kz,
                        first * (ky * wz + kz * wy) - s * ky * kz,
                        first * (kx * wz + kz * wx) - s * kx * kz,
                        first * (kx * wy + ky * wx) - s * kx * ky,
                        zero,
                        zero,
                    ]
                )
            )
        return np.stack(columns)

    ix, iy, iz = index[:, None, None], index[None, :, None], index[None, None, :]
    table = 0.5 * (operator(ix, iy, iz) + operator((-ix) % G, (-iy) % G, (-iz) % G)) / NV
    table = table.reshape(6, 8, G, G * G).transpose(2, 0, 1, 3)
    pairs, alone = half_plane()
    even, odd = np.concatenate([pairs, alone[:2]]), np.concatenate([pairs, alone[2:]])
    return np.stack([table[..., even], table[..., odd]]).astype(np.float32)


def half_plane():
    index = np.arange(G * G)
    mirror = (-(index // G)) % G * G + (-(index % G)) % G
    return index[index < mirror], index[index == mirror]


def plane_tables():
    pairs, alone = half_plane()
    plane = np.arange(G * G)

    def angle(k):
        turns = (plane[:, None] // G * (k // G)[None, :] + plane[:, None] % G * (k % G)[None, :]) % G
        return turns * (2 * np.pi / G)

    there = np.concatenate(
        [
            np.cos(angle(pairs)),
            np.cos(angle(alone[:2])),
            -np.sin(angle(pairs)),
            np.cos(angle(alone[2:])),
        ],
        axis=1,
    )
    weight = np.full((G * G, 1), 2.0)
    weight[[126, 127, 254, 255]] = 1.0
    parts = []
    for table in (there, weight * there.T):
        high = table.astype(np.float32).astype(bf16)
        parts += [high, (table - high.astype(np.float64)).astype(np.float32).astype(bf16)]
    return np.stack(parts)


def twiddle(value, power, sign):
    re, im = value
    power %= 16
    if power == 0:
        return re, im
    if power == 4:
        return (-im, re) if sign > 0 else (im, -re)
    if power == 8:
        return -re, -im
    if power == 12:
        return (im, -re) if sign > 0 else (-im, re)
    angle = sign * 2 * math.pi * power / 16
    c, s = math.cos(angle), math.sin(angle)
    if power % 4 == 2:
        h = abs(c)
        a = re if c > 0 else -re
        b = im if c > 0 else -im
        if c * s > 0:
            return (a - b) * h, (a + b) * h
        return (a + b) * h, (b - a) * h
    return re * c - im * s, re * s + im * c


def dft4(v, sign):
    (ar, ai), (br, bi), (cr, ci), (dr, di) = v
    pr, pi_ = ar + cr, ai + ci
    mr, mi = ar - cr, ai - ci
    qr, qi = br + dr, bi + di
    nr, ni = br - dr, bi - di
    if sign < 0:
        jr, ji = ni, -nr
    else:
        jr, ji = -ni, nr
    return [(pr + qr, pi_ + qi), (mr + jr, mi + ji), (pr - qr, pi_ - qi), (mr - jr, mi - ji)]


def dft16(values, sign):
    inner = []
    for n2 in range(4):
        inner.append(dft4([values[n2 + 4 * n1] for n1 in range(4)], sign))
    out = [None] * 16
    for k1 in range(4):
        column = dft4([twiddle(inner[n2][k1], n2 * k1, sign) for n2 in range(4)], sign)
        for k2 in range(4):
            out[k1 + 4 * k2] = column[k2]
    return out


def slab_stress(d, first_rows):
    wide = d.shape
    trace = d[0:1] + d[1:2] + d[2:3]
    lam_trace = jnp.broadcast_to(d[6:7] * trace, wide)
    twice = jnp.broadcast_to(2.0 * d[7:8], wide)
    return twice * d + jnp.where(first_rows, lam_trace, 0.0)


def plane_product(x, cmat, at):
    high = x.astype(bf16)
    low = (x - high.astype(f32)).astype(bf16)
    rows = x.shape[0]
    both = jnp.dot(jnp.concatenate([high, low], axis=0), cmat[at], preferred_element_type=f32)
    return both[:rows] + both[rows:] + jnp.dot(high, cmat[at + 1], preferred_element_type=f32)


def cells_kernel(
    count, owner, element, disp, nm, grads, micro, green, cmat, send, band_stress, replace, st, *work
):
    half_rows = 8 * G
    lane = lax.broadcasted_iota(jnp.int32, (8, LANES), 1)
    row = lax.broadcasted_iota(jnp.int32, (8, LANES), 0)
    row_wide = lax.broadcasted_iota(jnp.int32, (8, 2 * LANES), 0)
    first_rows = row_wide < 3

    targets = []
    for k in range(4):
        e = element[0, k]
        base = pl.multiple_of(e // LANES * LANES, LANES)
        at = lane == e % LANES

        def pick(tile):
            return jnp.sum(jnp.where(at, tile, 0.0), axis=1, keepdims=True)

        node = pick(nm[:, pl.ds(base, LANES)].astype(f32)).astype(jnp.int32)
        shape = [jnp.broadcast_to(pick(grads[j, :, pl.ds(base, LANES)]), (8, LANES)) for j in range(3)]
        node = jnp.broadcast_to(node, (8, LANES)) - lane
        found = [jnp.zeros((8, LANES), f32) for _ in range(3)]
        for r in range(72):
            hit = node == r * LANES
            for c in range(3):
                values = jnp.broadcast_to(disp[c : c + 1, r * LANES : (r + 1) * LANES], (8, LANES))
                found[c] = jnp.where(hit, values, found[c])
        u = [jnp.sum(found[c], axis=1, keepdims=True) for c in range(3)]

        def total(value):
            return jnp.sum(value, axis=0, keepdims=True)

        parts = [
            total(u[0] * shape[0]),
            total(u[1] * shape[1]),
            total(u[2] * shape[2]),
            0.5 * total(u[1] * shape[2] + u[2] * shape[1]),
            0.5 * total(u[0] * shape[2] + u[2] * shape[0]),
            0.5 * total(u[0] * shape[1] + u[1] * shape[0]),
        ]
        target = jnp.zeros((8, LANES), f32)
        for c in range(6):
            target = jnp.where(row == c, jnp.broadcast_to(parts[c], (8, LANES)), target)
        targets.append(target)

    def slab(k, x, iteration):
        if iteration == 0:
            return micro[k, :, 2 * LANES * x : 2 * LANES * (x + 1)]
        return st[k, 8 * x : 8 * x + 8, :]

    shifts = []
    for k in range(4):
        total = jnp.zeros((8, 2 * LANES), f32)
        for x in range(G):
            total = total + slab(k, x, 0)
        mean = jnp.sum(total, axis=1, keepdims=True) * (1.0 / NV)
        shift = jnp.where(row < 6, targets[k] - mean, 0.0)
        shifts.append(jnp.concatenate([shift, shift], axis=1))

    re_cols, im_cols = slice(0, LANES), slice(LANES, 2 * LANES)
    own_mirror = lane >= 126
    whole_mirror = lax.broadcasted_iota(jnp.int32, (half_rows, LANES), 1) >= 126
    for iteration in range(ITERS):
        for pair in range(2):
            plane, spectrum = work[2 * pair], work[2 * pair + 1]
            at = [[cell * half_rows + 8 * x for x in range(G)] for cell in range(2)]
            for cell in range(2):
                for x in range(G):
                    a = at[cell][x]
                    plane[a : a + 8, :] = slab_stress(slab(2 * pair + cell, x, iteration), first_rows)
            plane[...] = plane_product(plane[...], cmat, 0)
            for cell in range(2):
                values = []
                for x in range(G):
                    a = at[cell][x]
                    re, im = plane[a : a + 8, re_cols], plane[a : a + 8, im_cols]
                    if cell == 0:
                        other = at[1][x]
                        im = jnp.where(own_mirror, plane[other : other + 8, re_cols], im)
                    else:
                        other = at[0][x]
                        re = jnp.where(own_mirror, plane[other : other + 8, im_cols], re)
                    values.append((re, im))
                values = dft16(values, -1)
                for x in range(G):
                    a = at[cell][x]
                    spectrum[a : a + 8, re_cols] = values[x][0]
                    spectrum[a : a + 8, im_cols] = values[x][1]
            for cell in range(2):
                updates = []
                for x in range(G):
                    re = im = None
                    for j in range(6):
                        weight = green[cell, x, j]
                        a = at[cell][x] + j
                        tr = weight * jnp.broadcast_to(spectrum[a : a + 1, re_cols], (8, LANES))
                        ti = weight * jnp.broadcast_to(spectrum[a : a + 1, im_cols], (8, LANES))
                        re = tr if re is None else re + tr
                        im = ti if im is None else im + ti
                    updates.append((re, im))
                values = dft16(updates, 1)
                for x in range(G):
                    a = at[cell][x]
                    plane[a : a + 8, re_cols] = values[x][0]
                    plane[a : a + 8, im_cols] = values[x][1]
            first_im = plane[:half_rows, im_cols]
            second_re = plane[half_rows:, re_cols]
            plane[:half_rows, im_cols] = jnp.where(whole_mirror, second_re, first_im)
            plane[half_rows:, re_cols] = jnp.where(whole_mirror, first_im, second_re)
            update = plane_product(plane[...], cmat, 2)
            for cell in range(2):
                k = 2 * pair + cell
                for x in range(G):
                    a = at[cell][x]
                    value = slab(k, x, iteration) - update[a : a + 8, :]
                    if iteration == 0:
                        value = value + shifts[k]
                    st[k, 8 * x : 8 * x + 8, :] = value

    send[pl.ds(8, 4 * TILES, stride=9), :] = jnp.full((4 * TILES, LANES), -1.0, f32)
    result = jnp.zeros((8, LANES), f32)
    for k in range(4):
        live = k < count[0]
        total = jnp.zeros((8, 2 * LANES), f32)
        for x in range(G):
            total = total + slab_stress(st[k, 8 * x : 8 * x + 8, :], first_rows)
        mean = jnp.where(live, jnp.sum(total, axis=1, keepdims=True) * (1.0 / NV), 0.0)
        mean = jnp.broadcast_to(mean, (8, LANES))
        result = jnp.where(lane == k, mean, result)
        across = jnp.sum(jnp.where(lane == row, mean, 0.0), axis=0, keepdims=True)
        band_stress[k : k + 1, :] = across[:, 0:6]
        pool = owner[0, k] & 3

        @pl.when(live)
        def _():
            for i in range(TILES):
                x, part = i // 2, i % 2
                send[pl.ds(9 * (4 * i + pool), 8), :] = st[
                    k, 8 * x : 8 * x + 8, part * LANES : (part + 1) * LANES
                ]
            brick = (owner[0, k] >> 2).astype(f32)
            send[pl.ds(9 * pool + 8, TILES, stride=36), :] = jnp.full((TILES, LANES), brick, f32)

    for k in range(4):
        live_element = jnp.where(k < count[0], element[0, k], -1).astype(f32)
        result = jnp.where((lane == k) & (row == 6), live_element, result)
    replace[...] = result[:, 0:4]


def solve_cells(count, owner, element, disp, nm, grads, micro, green, cmat):
    return pl.pallas_call(
        cells_kernel,
        out_shape=(
            jax.ShapeDtypeStruct((36 * TILES, LANES), f32),
            jax.ShapeDtypeStruct((4, 6), f32),
            jax.ShapeDtypeStruct((8, 4), f32),
        ),
        in_specs=[pl.BlockSpec(memory_space=SMEM)] * 3 + [pl.BlockSpec(memory_space=VMEM)] * 6,
        out_specs=(pl.BlockSpec(memory_space=VMEM),) * 3,
        scratch_shapes=[
            VMEM((4, 8 * G, 2 * LANES), f32),
        ]
        + [VMEM((16 * G, 2 * LANES), f32)] * 4,
        compiler_params=pltpu.CompilerParams(vmem_limit_bytes=56 << 20),
        name="cells",
    )(count, owner, element, disp, nm, grads, micro, green, cmat)


def one_hot_sum(node, values, width):
    def spread(row, rows):
        return jnp.broadcast_to(jnp.broadcast_to(row, (16, width)).astype(bf16)[None], (rows // 16, 16, width)).reshape(
            rows, width
        )

    def index(rows):
        return lax.broadcasted_iota(jnp.int32, (rows, width), 0).astype(f32).astype(bf16)

    coarse = index(HI) == spread((node >> 8).astype(f32), HI)
    fine = index(LO) == spread((node & 255).astype(f32), LO)
    left = jnp.concatenate(
        [jnp.where(coarse, spread(v, HI), jnp.zeros((HI, width), bf16)) for v in values], axis=0
    )
    right = jnp.where(fine, jnp.ones((LO, width), bf16), jnp.zeros((LO, width), bf16))
    return left, right


def halves(value):
    high = value.astype(bf16).astype(f32)
    return high, value - high


def pack_table(disp, table, step):
    largest = jnp.zeros((3, LANES), f32)
    for r in range(72):
        largest = jnp.maximum(largest, jnp.abs(disp[:, r * LANES : (r + 1) * LANES]))
    largest = jnp.maximum(jnp.max(largest, axis=0, keepdims=True), 1e-30)
    step[...] = largest * (1.0 / STEPS)
    scale = jnp.broadcast_to(STEPS / largest, (3, LANES))
    for r in range(72):
        cols = slice(r * LANES, (r + 1) * LANES)
        level = jnp.floor(disp[:, cols] * scale + (OFFSET + 0.5)).astype(jnp.int32)
        last = level[2:3]
        parts = jnp.concatenate([(last & 0x7FF) << 21, (last >> 11) << 21], axis=0)
        table[:, cols] = level[0:2] | parts


def unpack(first, second, step):
    mask = (1 << 21) - 1
    last = lax.shift_right_logical(first, 21) | (lax.shift_right_logical(second, 21) << 11)
    return [(level - OFFSET).astype(f32) * step for level in (first & mask, second & mask, last)]


def macro_tiles(begin, end, unroll, replace, table, step_of, nm, grads, volumes, moduli, sums):
    lane = lax.broadcasted_iota(jnp.int32, (1, LANES), 1).astype(f32)
    steps = jnp.broadcast_to(step_of[...], (8, LANES))

    def scatter(node, forces):
        values = []
        for force in forces:
            values += list(halves(force))
        total = None
        for s in range(0, 8, 2):
            lefts, rights = [], []
            for q in (s, s + 1):
                left, right = one_hot_sum(node[q : q + 1], [v[q : q + 1] for v in values], LANES)
                lefts.append(left)
                rights.append(right)
            product = lax.dot_general(
                jnp.concatenate(lefts, axis=1),
                jnp.concatenate(rights, axis=1),
                (((1,), (1,)), ((), ())),
                preferred_element_type=f32,
            )
            total = product if total is None else total + product
        return total

    def forces_of(t):
        cols = pl.ds(pl.multiple_of(t * LANES, LANES), LANES)
        node = nm[:, cols]
        hi, lo = node >> 7, node & 127
        words = [jnp.zeros((8, LANES), jnp.int32) for _ in range(2)]
        for r in range(72):
            hit = hi == r
            for w in range(2):
                values = jnp.broadcast_to(table[w : w + 1, r * LANES : (r + 1) * LANES], (8, LANES))
                found = jnp.take_along_axis(values, lo, axis=1, mode="promise_in_bounds")
                words[w] = jnp.where(hit, found, words[w])
        u = unpack(*words, jnp.take_along_axis(steps, lo, axis=1, mode="promise_in_bounds"))
        g = [grads[j, :, cols] for j in range(3)]

        def total(value):
            return jnp.sum(value, axis=0, keepdims=True)

        strain = [
            total(u[0] * g[0]),
            total(u[1] * g[1]),
            total(u[2] * g[2]),
            0.5 * total(u[1] * g[2] + u[2] * g[1]),
            0.5 * total(u[0] * g[2] + u[2] * g[0]),
            0.5 * total(u[0] * g[1] + u[1] * g[0]),
        ]
        lam = moduli[0:1, cols]
        mu = moduli[1:2, cols]
        volume = volumes[pl.ds(t, 1), :]
        spherical = lam * (strain[0] + strain[1] + strain[2])
        stress = [spherical + 2.0 * mu * strain[c] for c in range(3)]
        stress += [2.0 * mu * strain[c] for c in range(3, 6)]
        for k in range(4):
            hit = lane == replace[6, k] - lax.convert_element_type(t * LANES, f32)
            stress = [jnp.where(hit, replace[c, k], stress[c]) for c in range(6)]
        xx, yy, zz, yz, xz, xy = [
            jnp.broadcast_to(component * volume, (8, LANES)) for component in stress
        ]
        fx = xx * g[0] + xy * g[1] + xz * g[2]
        fy = xy * g[0] + yy * g[1] + yz * g[2]
        fz = xz * g[0] + yz * g[1] + zz * g[2]
        return node, fx, fy, fz

    def group(step):
        return tuple(forces_of(begin + step * unroll + i) for i in range(unroll))

    def add(carry):
        total = None
        for node, *forces in carry:
            part = scatter(node, forces)
            total = part if total is None else total + part
        sums[...] += total

    def body(step, carry):
        add(carry)
        return group(step)

    add(lax.fori_loop(1, (end - begin) // unroll, body, group(0)))


def macro_first_kernel(
    unroll, replace, disp, nm, grads, volumes, moduli, shared, sums, table, step, face_nodes
):
    for i in range(4):
        for half in range(2):
            cols = slice((2 * i + half) * LANES, (2 * i + half + 1) * LANES)
            face_nodes[i, 4 * half : 4 * half + 4, :] = shared[0, :, cols]
    pack_table(disp, table, step)
    sums[...] = jnp.zeros_like(sums)
    macro_tiles(0, SPLIT, unroll, replace, table, step, nm, grads, volumes, moduli, sums)


def face_lists(core, pool):
    return core, 2 + (pool & 1), 3 - (pool & 1), 1 - core


def macro_last_kernel(
    unroll,
    replace,
    core_index,
    pool_index,
    table,
    step,
    nm,
    grads,
    volumes,
    moduli,
    so_far,
    face_nodes,
    own,
    to_brick,
    to_odd,
    to_even,
    to_core,
    sums,
    faces,
):
    sums[...] = so_far[...]
    macro_tiles(SPLIT, 64, unroll, replace, table, step, nm, grads, volumes, moduli, sums)

    for c in range(3):
        at = 2 * c * HI
        own[c * HI : (c + 1) * HI, :] = sums[at : at + HI, :] + sums[at + HI : at + 2 * HI, :]

    for pair in range(4):
        first, second = 2 * pair, 2 * pair + 1
        node = face_nodes[pair]
        hi, lo = node >> 7, node & 127
        picked = [jnp.zeros((8, LANES), f32) for _ in range(3)]
        for r in range(72):
            hit = hi == r
            for c in range(3):
                at = c * HI + r // 2
                cols = slice(r % 2 * LANES, (r % 2 + 1) * LANES)
                values = jnp.broadcast_to(own[at : at + 1, cols], (8, LANES))
                found = jnp.take_along_axis(values, lo, axis=1, mode="promise_in_bounds")
                picked[c] = jnp.where(hit, found, picked[c])
        for c in range(3):
            for face in range(4):
                faces[face, c : c + 1, first * LANES : (first + 1) * LANES] = picked[c][face : face + 1]
                faces[face, c : c + 1, second * LANES : (second + 1) * LANES] = picked[c][
                    4 + face : 5 + face
                ]
    lists = face_lists(core_index[0], pool_index[0])
    for face, out in zip(lists, (to_brick, to_odd, to_even, to_core)):
        out[...] = faces[face]


def macro_first(*arguments):
    vmem = pl.BlockSpec(memory_space=VMEM)
    return pl.pallas_call(
        functools.partial(macro_first_kernel, UNROLL),
        out_shape=(
            jax.ShapeDtypeStruct((6 * HI, LO), f32),
            jax.ShapeDtypeStruct((2, 72 * LANES), jnp.int32),
            jax.ShapeDtypeStruct((1, LANES), f32),
            jax.ShapeDtypeStruct((4, 8, LANES), jnp.int32),
        ),
        in_specs=[pl.BlockSpec(memory_space=SMEM)] + [vmem] * 6,
        out_specs=(vmem,) * 4,
        compiler_params=pltpu.CompilerParams(vmem_limit_bytes=32 << 20),
        name="macro_first",
    )(*arguments)


def macro_last(*arguments):
    vmem = pl.BlockSpec(memory_space=VMEM)
    return pl.pallas_call(
        functools.partial(macro_last_kernel, UNROLL),
        out_shape=(
            jax.ShapeDtypeStruct((3 * HI, LO), f32),
        )
        + (jax.ShapeDtypeStruct((3, 1024), f32),) * 4,
        in_specs=[pl.BlockSpec(memory_space=SMEM)] * 3 + [vmem] * 8,
        out_specs=(vmem,) * 5,
        scratch_shapes=[VMEM((6 * HI, LO), f32), VMEM((4, 3, 1024), f32)],
        compiler_params=pltpu.CompilerParams(vmem_limit_bytes=32 << 20),
        name="macro_last",
    )(*arguments)


def assemble_kernel(core_index, pool_index, own, shared, r0, r1, r2, r3, external, mass, out):
    total = None
    for face, arrived in zip(face_lists(core_index[0], pool_index[0]), (r0, r1, r2, r3)):
        for part in range(4):
            cols = slice(part * LO, (part + 1) * LO)
            values = []
            for c in range(3):
                values += list(halves(arrived[c : c + 1, cols]))
            left, right = one_hot_sum(shared[0, pl.ds(face, 1), cols], values, LO)
            product = lax.dot_general(
                left, right, (((1,), (1,)), ((), ())), preferred_element_type=f32
            )
            total = product if total is None else total + product
    for c in range(3):
        at = 2 * c * HI
        whole = own[c * HI : (c + 1) * HI, :] + total[at : at + HI] + total[at + HI : at + 2 * HI]
        for r in range(36):
            out[c : c + 1, r * LO : (r + 1) * LO] = whole[r : r + 1]
    out[...] = (external[...] - out[...]) / mass[...]


def assemble(place, own, shared, arrived, external, mass):
    vmem = pl.BlockSpec(memory_space=VMEM)
    return pl.pallas_call(
        assemble_kernel,
        out_shape=jax.ShapeDtypeStruct(external.shape, f32),
        in_specs=[pl.BlockSpec(memory_space=SMEM)] * 2 + [vmem] * 8,
        out_specs=vmem,
        compiler_params=pltpu.CompilerParams(vmem_limit_bytes=32 << 20),
        name="assemble",
    )(*place, own, shared, *arrived, external, mass)


def sort_kernel(pieces, out, order, places, sem):
    blocks = pieces.shape[0] // 9
    lane = lax.broadcasted_iota(jnp.int32, (blocks, LANES), 1)
    block = lax.broadcasted_iota(jnp.int32, (blocks, LANES), 0)
    hit = pieces[pl.ds(8, blocks, stride=9), :] == lane.astype(f32)
    order[0:1, :] = jnp.min(jnp.where(hit, block, blocks - 1), axis=0, keepdims=True)
    order[1:2, :] = jnp.max(jnp.where(hit, block, 0), axis=0, keepdims=True)
    copy = pltpu.make_async_copy(order, places, sem)
    copy.start()
    copy.wait()
    for b in range(out.shape[0]):
        for s in range(2):
            out[b, s] = pieces[pl.ds(9 * places[s, b], 8), :]


def sort_pieces(pieces, bricks):
    vmem = pl.BlockSpec(memory_space=VMEM)
    return pl.pallas_call(
        sort_kernel,
        out_shape=jax.ShapeDtypeStruct((bricks, 2, 8, LANES), f32),
        in_specs=[vmem],
        out_specs=vmem,
        scratch_shapes=[VMEM((8, LANES), jnp.int32), SMEM((8, LANES), jnp.int32), pltpu.SemaphoreType.DMA],
        compiler_params=pltpu.CompilerParams(vmem_limit_bytes=32 << 20),
        name="sort_pieces",
    )(pieces)


def join_kernel(pieces, out):
    for i in range(TILES):
        for s in range(2):
            out[s, :, i * LANES : (i + 1) * LANES] = pieces[i, s]


def join_pieces(pieces):
    vmem = pl.BlockSpec(memory_space=VMEM)
    return pl.pallas_call(
        join_kernel,
        out_shape=jax.ShapeDtypeStruct((2, 8, NV), f32),
        in_specs=[vmem],
        out_specs=vmem,
        name="join_pieces",
    )(pieces)


def shards(
    displacement,
    node_map,
    shape_grads,
    volumes,
    elastic_moduli,
    external_force,
    nodal_mass,
    shared_nodes,
    band_count,
    band_owner,
    band_element,
    micro_fields,
):
    bricks, pools = lax.axis_size(BRICK), lax.axis_size("pool")
    place = tuple(lax.axis_index(axis).astype(jnp.int32).reshape(1) for axis in ("core", "pool"))
    send, band_stress, replace = solve_cells(
        band_count,
        band_owner,
        band_element,
        displacement,
        node_map,
        shape_grads,
        micro_fields,
        jnp.asarray(green_table()),
        jnp.asarray(plane_tables()),
    )
    pieces = lax.all_to_all(
        send.reshape(bricks * pools, 1, 9 * LANES), BOTH, split_axis=0, concat_axis=0, tiled=True
    )
    dense = (node_map, shape_grads, volumes.reshape(64, LANES), elastic_moduli)
    so_far, table, step, face_nodes = macro_first(replace, displacement, *dense, shared_nodes)
    pieces, so_far = lax.optimization_barrier((pieces, so_far))
    sorted_pieces = sort_pieces(pieces.reshape(9 * bricks * pools, LANES), bricks)
    sorted_pieces, so_far = lax.optimization_barrier((sorted_pieces, so_far))
    mine = lax.all_to_all(sorted_pieces, BRICK, split_axis=0, concat_axis=0, tiled=True)
    own, *faces = macro_last(replace, *place, table, step, *dense, so_far, face_nodes)

    def swap(array, axis, size, first):
        steps = [(i, i + 1) for i in range(first, size - 1, 2)]
        return lax.ppermute(array, axis, steps + [(j, i) for i, j in steps])

    arrived = (
        swap(faces[0], BRICK, bricks, 1),
        swap(faces[1], "pool", pools, 1),
        swap(faces[2], "pool", pools, 0),
        swap(faces[3], "core", 2, 0),
    )
    owned_fields = join_pieces(mine)
    *arrived, owned_fields = lax.optimization_barrier((*arrived, owned_fields))
    acceleration = assemble(
        place, own, shared_nodes, arrived, external_force, nodal_mass.reshape(1, -1)
    )
    return (acceleration, band_stress.T, owned_fields)


def solution(mesh):
    bricks, pools = mesh.devices.shape
    split = jax.sharding.Mesh(
        mesh.devices.reshape(4, bricks // 8, 2, pools), ("row", "pair", "core", "pool")
    )
    placed = (
        P(None, BOTH),
        P(None, BOTH),
        P(None, None, BOTH),
        P(BOTH),
        P(None, BOTH),
        P(None, BOTH),
        P(BOTH),
        P(BOTH, None, None),
        P(BOTH),
        P(BOTH, None),
        P(BOTH, None),
        P(BOTH, None, None),
    )
    return jax.shard_map(
        shards,
        mesh=split,
        in_specs=placed,
        out_specs=(P(None, BOTH), P(None, BOTH), P(BOTH, None, None)),
        check_vma=False,
    )
```

```python
import functools
import math

import jax
import jax.numpy as jnp
import numpy as np
from jax import lax
from jax.experimental import pallas as pl
from jax.experimental.pallas import tpu as pltpu
from jax.sharding import PartitionSpec as P

G = 16
NV = 4096
ITERS = 2
LANES = 128
TILES = 32
HI = 48
LO = 256
STEPS = float((1 << 20) - 2)
OFFSET = 1 << 20
UNROLL = 4
SPLIT = 56
BRICK = ("row", "pair", "core")
BOTH = BRICK + ("pool",)
VMEM = pltpu.VMEM
SMEM = pltpu.SMEM
f32 = jnp.float32
bf16 = jnp.bfloat16

ref_lambda = 5.5
ref_shear = 5.5


def green_table():
    index = np.arange(G)

    def operator(ix, iy, iz):
        wave = [np.where(2 * m < G, m, m - G).astype(np.float64) for m in (ix, iy, iz)]
        kx, ky, kz = np.broadcast_arrays(wave[0], wave[1], wave[2])
        square = kx * kx + ky * ky + kz * kz
        safe = np.where(square > 0, square, 1.0)
        first = np.where(square > 0, 1.0 / (2.0 * ref_shear * safe), 0.0)
        factor = (ref_lambda + ref_shear) / (ref_shear * (ref_lambda + 2.0 * ref_shear))
        second = np.where(square > 0, factor / (safe * safe), 0.0)
        zero, one = np.zeros_like(kx), np.ones_like(kx)
        columns = []
        for j in range(6):
            xx, yy, zz, yz, xz, xy = [one if j == c else zero for c in range(6)]
            wx = xx * kx + xy * ky + xz * kz
            wy = xy * kx + yy * ky + yz * kz
            wz = xz * kx + yz * ky + zz * kz
            s = (wx * kx + wy * ky + wz * kz) * second
            columns.append(
                np.stack(
                    [
                        first * 2 * kx * wx - s * kx * kx,
                        first * 2 * ky * wy - s * ky * ky,
                        first * 2 * kz * wz - s * kz * kz,
                        first * (ky * wz + kz * wy) - s * ky * kz,
                        first * (kx * wz + kz * wx) - s * kx * kz,
                        first * (kx * wy + ky * wx) - s * kx * ky,
                        zero,
                        zero,
                    ]
                )
            )
        return np.stack(columns)

    ix, iy, iz = index[:, None, None], index[None, :, None], index[None, None, :]
    table = 0.5 * (operator(ix, iy, iz) + operator((-ix) % G, (-iy) % G, (-iz) % G)) / NV
    table = table.reshape(6, 8, G, G * G).transpose(2, 0, 1, 3)
    pairs, alone = half_plane()
    even, odd = np.concatenate([pairs, alone[:2]]), np.concatenate([pairs, alone[2:]])
    return np.stack([table[..., even], table[..., odd]]).astype(np.float32)


def half_plane():
    index = np.arange(G * G)
    mirror = (-(index // G)) % G * G + (-(index % G)) % G
    return index[index < mirror], index[index == mirror]


def plane_tables():
    pairs, alone = half_plane()
    plane = np.arange(G * G)

    def angle(k):
        turns = (plane[:, None] // G * (k // G)[None, :] + plane[:, None] % G * (k % G)[None, :]) % G
        return turns * (2 * np.pi / G)

    there = np.concatenate(
        [
            np.cos(angle(pairs)),
            np.cos(angle(alone[:2])),
            -np.sin(angle(pairs)),
            np.cos(angle(alone[2:])),
        ],
        axis=1,
    )
    weight = np.full((G * G, 1), 2.0)
    weight[[126, 127, 254, 255]] = 1.0
    parts = []
    for table in (there, weight * there.T):
        high = table.astype(np.float32).astype(bf16)
        parts += [high, (table - high.astype(np.float64)).astype(np.float32).astype(bf16)]
    return np.stack(parts)


def twiddle(value, power, sign):
    re, im = value
    power %= 16
    if power == 0:
        return re, im
    if power == 4:
        return (-im, re) if sign > 0 else (im, -re)
    if power == 8:
        return -re, -im
    if power == 12:
        return (im, -re) if sign > 0 else (-im, re)
    angle = sign * 2 * math.pi * power / 16
    c, s = math.cos(angle), math.sin(angle)
    if power % 4 == 2:
        h = abs(c)
        a = re if c > 0 else -re
        b = im if c > 0 else -im
        if c * s > 0:
            return (a - b) * h, (a + b) * h
        return (a + b) * h, (b - a) * h
    return re * c - im * s, re * s + im * c


def dft4(v, sign):
    (ar, ai), (br, bi), (cr, ci), (dr, di) = v
    pr, pi_ = ar + cr, ai + ci
    mr, mi = ar - cr, ai - ci
    qr, qi = br + dr, bi + di
    nr, ni = br - dr, bi - di
    if sign < 0:
        jr, ji = ni, -nr
    else:
        jr, ji = -ni, nr
    return [(pr + qr, pi_ + qi), (mr + jr, mi + ji), (pr - qr, pi_ - qi), (mr - jr, mi - ji)]


def dft16(values, sign):
    inner = []
    for n2 in range(4):
        inner.append(dft4([values[n2 + 4 * n1] for n1 in range(4)], sign))
    out = [None] * 16
    for k1 in range(4):
        column = dft4([twiddle(inner[n2][k1], n2 * k1, sign) for n2 in range(4)], sign)
        for k2 in range(4):
            out[k1 + 4 * k2] = column[k2]
    return out


def slab_stress(d, first_rows):
    wide = d.shape
    trace = d[0:1] + d[1:2] + d[2:3]
    lam_trace = jnp.broadcast_to(d[6:7] * trace, wide)
    twice = jnp.broadcast_to(2.0 * d[7:8], wide)
    return twice * d + jnp.where(first_rows, lam_trace, 0.0)


def plane_product(x, cmat, at):
    high = x.astype(bf16)
    low = (x - high.astype(f32)).astype(bf16)
    rows = x.shape[0]
    both = jnp.dot(jnp.concatenate([high, low], axis=0), cmat[at], preferred_element_type=f32)
    return both[:rows] + both[rows:] + jnp.dot(high, cmat[at + 1], preferred_element_type=f32)


def cells_kernel(
    count, owner, element, disp, nm, grads, micro, green, cmat, send, band_stress, replace, st, *work
):
    half_rows = 8 * G
    lane = lax.broadcasted_iota(jnp.int32, (8, LANES), 1)
    row = lax.broadcasted_iota(jnp.int32, (8, LANES), 0)
    row_wide = lax.broadcasted_iota(jnp.int32, (8, 2 * LANES), 0)
    first_rows = row_wide < 3

    targets = []
    for k in range(4):
        e = element[0, k]
        base = pl.multiple_of(e // LANES * LANES, LANES)
        at = lane == e % LANES

        def pick(tile):
            return jnp.sum(jnp.where(at, tile, 0.0), axis=1, keepdims=True)

        node = pick(nm[:, pl.ds(base, LANES)].astype(f32)).astype(jnp.int32)
        shape = [jnp.broadcast_to(pick(grads[j, :, pl.ds(base, LANES)]), (8, LANES)) for j in range(3)]
        node = jnp.broadcast_to(node, (8, LANES)) - lane
        found = [jnp.zeros((8, LANES), f32) for _ in range(3)]
        for r in range(72):
            hit = node == r * LANES
            for c in range(3):
                values = jnp.broadcast_to(disp[c : c + 1, r * LANES : (r + 1) * LANES], (8, LANES))
                found[c] = jnp.where(hit, values, found[c])
        u = [jnp.sum(found[c], axis=1, keepdims=True) for c in range(3)]

        def total(value):
            return jnp.sum(value, axis=0, keepdims=True)

        parts = [
            total(u[0] * shape[0]),
            total(u[1] * shape[1]),
            total(u[2] * shape[2]),
            0.5 * total(u[1] * shape[2] + u[2] * shape[1]),
            0.5 * total(u[0] * shape[2] + u[2] * shape[0]),
            0.5 * total(u[0] * shape[1] + u[1] * shape[0]),
        ]
        target = jnp.zeros((8, LANES), f32)
        for c in range(6):
            target = jnp.where(row == c, jnp.broadcast_to(parts[c], (8, LANES)), target)
        targets.append(target)

    def slab(k, x, iteration):
        if iteration == 0:
            return micro[k, :, 2 * LANES * x : 2 * LANES * (x + 1)]
        return st[k, 8 * x : 8 * x + 8, :]

    shifts = []
    for k in range(4):
        total = jnp.zeros((8, 2 * LANES), f32)
        for x in range(G):
            total = total + slab(k, x, 0)
        mean = jnp.sum(total, axis=1, keepdims=True) * (1.0 / NV)
        shift = jnp.where(row < 6, targets[k] - mean, 0.0)
        shifts.append(jnp.concatenate([shift, shift], axis=1))

    re_cols, im_cols = slice(0, LANES), slice(LANES, 2 * LANES)
    own_mirror = lane >= 126
    whole_mirror = lax.broadcasted_iota(jnp.int32, (half_rows, LANES), 1) >= 126
    for iteration in range(ITERS):
        for pair in range(2):
            plane, spectrum = work[2 * pair], work[2 * pair + 1]
            at = [[cell * half_rows + 8 * x for x in range(G)] for cell in range(2)]
            for cell in range(2):
                for x in range(G):
                    a = at[cell][x]
                    plane[a : a + 8, :] = slab_stress(slab(2 * pair + cell, x, iteration), first_rows)
            plane[...] = plane_product(plane[...], cmat, 0)
            for cell in range(2):
                values = []
                for x in range(G):
                    a = at[cell][x]
                    re, im = plane[a : a + 8, re_cols], plane[a : a + 8, im_cols]
                    if cell == 0:
                        other = at[1][x]
                        im = jnp.where(own_mirror, plane[other : other + 8, re_cols], im)
                    else:
                        other = at[0][x]
                        re = jnp.where(own_mirror, plane[other : other + 8, im_cols], re)
                    values.append((re, im))
                values = dft16(values, -1)
                for x in range(G):
                    a = at[cell][x]
                    spectrum[a : a + 8, re_cols] = values[x][0]
                    spectrum[a : a + 8, im_cols] = values[x][1]
            for cell in range(2):
                updates = []
                for x in range(G):
                    re = im = None
                    for j in range(6):
                        weight = green[cell, x, j]
                        a = at[cell][x] + j
                        tr = weight * jnp.broadcast_to(spectrum[a : a + 1, re_cols], (8, LANES))
                        ti = weight * jnp.broadcast_to(spectrum[a : a + 1, im_cols], (8, LANES))
                        re = tr if re is None else re + tr
                        im = ti if im is None else im + ti
                    updates.append((re, im))
                values = dft16(updates, 1)
                for x in range(G):
                    a = at[cell][x]
                    plane[a : a + 8, re_cols] = values[x][0]
                    plane[a : a + 8, im_cols] = values[x][1]
            first_im = plane[:half_rows, im_cols]
            second_re = plane[half_rows:, re_cols]
            plane[:half_rows, im_cols] = jnp.where(whole_mirror, second_re, first_im)
            plane[half_rows:, re_cols] = jnp.where(whole_mirror, first_im, second_re)
            update = plane_product(plane[...], cmat, 2)
            for cell in range(2):
                k = 2 * pair + cell
                for x in range(G):
                    a = at[cell][x]
                    value = slab(k, x, iteration) - update[a : a + 8, :]
                    if iteration == 0:
                        value = value + shifts[k]
                    st[k, 8 * x : 8 * x + 8, :] = value

    send[pl.ds(8, 4 * TILES, stride=9), :] = jnp.full((4 * TILES, LANES), -1.0, f32)
    result = jnp.zeros((8, LANES), f32)
    for k in range(4):
        live = k < count[0]
        total = jnp.zeros((8, 2 * LANES), f32)
        for x in range(G):
            total = total + slab_stress(st[k, 8 * x : 8 * x + 8, :], first_rows)
        mean = jnp.where(live, jnp.sum(total, axis=1, keepdims=True) * (1.0 / NV), 0.0)
        mean = jnp.broadcast_to(mean, (8, LANES))
        result = jnp.where(lane == k, mean, result)
        across = jnp.sum(jnp.where(lane == row, mean, 0.0), axis=0, keepdims=True)
        band_stress[k : k + 1, :] = across[:, 0:6]
        pool = owner[0, k] & 3

        @pl.when(live)
        def _():
            for i in range(TILES):
                x, part = i // 2, i % 2
                send[pl.ds(9 * (4 * i + pool), 8), :] = st[
                    k, 8 * x : 8 * x + 8, part * LANES : (part + 1) * LANES
                ]
            brick = (owner[0, k] >> 2).astype(f32)
            send[pl.ds(9 * pool + 8, TILES, stride=36), :] = jnp.full((TILES, LANES), brick, f32)

    for k in range(4):
        live_element = jnp.where(k < count[0], element[0, k], -1).astype(f32)
        result = jnp.where((lane == k) & (row == 6), live_element, result)
    replace[...] = result[:, 0:4]


def solve_cells(count, owner, element, disp, nm, grads, micro, green, cmat):
    return pl.pallas_call(
        cells_kernel,
        out_shape=(
            jax.ShapeDtypeStruct((36 * TILES, LANES), f32),
            jax.ShapeDtypeStruct((4, 6), f32),
            jax.ShapeDtypeStruct((8, 4), f32),
        ),
        in_specs=[pl.BlockSpec(memory_space=SMEM)] * 3 + [pl.BlockSpec(memory_space=VMEM)] * 6,
        out_specs=(pl.BlockSpec(memory_space=VMEM),) * 3,
        scratch_shapes=[
            VMEM((4, 8 * G, 2 * LANES), f32),
        ]
        + [VMEM((16 * G, 2 * LANES), f32)] * 4,
        compiler_params=pltpu.CompilerParams(vmem_limit_bytes=56 << 20),
        name="cells",
    )(count, owner, element, disp, nm, grads, micro, green, cmat)


def one_hot_sum(node, values, width):
    def spread(row, rows):
        return jnp.broadcast_to(jnp.broadcast_to(row, (16, width)).astype(bf16)[None], (rows // 16, 16, width)).reshape(
            rows, width
        )

    def index(rows):
        return lax.broadcasted_iota(jnp.int32, (rows, width), 0).astype(f32).astype(bf16)

    coarse = index(HI) == spread((node >> 8).astype(f32), HI)
    fine = index(LO) == spread((node & 255).astype(f32), LO)
    left = jnp.concatenate(
        [jnp.where(coarse, spread(v, HI), jnp.zeros((HI, width), bf16)) for v in values], axis=0
    )
    right = jnp.where(fine, jnp.ones((LO, width), bf16), jnp.zeros((LO, width), bf16))
    return left, right


def halves(value):
    high = value.astype(bf16).astype(f32)
    return high, value - high


def pack_table(disp, table, step):
    largest = jnp.zeros((3, LANES), f32)
    for r in range(72):
        largest = jnp.maximum(largest, jnp.abs(disp[:, r * LANES : (r + 1) * LANES]))
    largest = jnp.maximum(jnp.max(largest, axis=0, keepdims=True), 1e-30)
    step[...] = largest * (1.0 / STEPS)
    scale = jnp.broadcast_to(STEPS / largest, (3, LANES))
    for r in range(72):
        cols = slice(r * LANES, (r + 1) * LANES)
        level = jnp.floor(disp[:, cols] * scale + (OFFSET + 0.5)).astype(jnp.int32)
        last = level[2:3]
        parts = jnp.concatenate([(last & 0x7FF) << 21, (last >> 11) << 21], axis=0)
        table[:, cols] = level[0:2] | parts


def unpack(first, second, step):
    mask = (1 << 21) - 1
    last = lax.shift_right_logical(first, 21) | (lax.shift_right_logical(second, 21) << 11)
    return [(level - OFFSET).astype(f32) * step for level in (first & mask, second & mask, last)]


def macro_tiles(begin, end, unroll, replace, table, step_of, nm, grads, volumes, moduli, sums):
    lane = lax.broadcasted_iota(jnp.int32, (1, LANES), 1).astype(f32)
    steps = jnp.broadcast_to(step_of[...], (8, LANES))

    def scatter(node, forces):
        values = []
        for force in forces:
            values += list(halves(force))
        total = None
        for s in range(0, 8, 2):
            lefts, rights = [], []
            for q in (s, s + 1):
                left, right = one_hot_sum(node[q : q + 1], [v[q : q + 1] for v in values], LANES)
                lefts.append(left)
                rights.append(right)
            product = lax.dot_general(
                jnp.concatenate(lefts, axis=1),
                jnp.concatenate(rights, axis=1),
                (((1,), (1,)), ((), ())),
                preferred_element_type=f32,
            )
            total = product if total is None else total + product
        return total

    def forces_of(t):
        cols = pl.ds(pl.multiple_of(t * LANES, LANES), LANES)
        node = nm[:, cols]
        hi, lo = node >> 7, node & 127
        words = [jnp.zeros((8, LANES), jnp.int32) for _ in range(2)]
        for r in range(72):
            hit = hi == r
            for w in range(2):
                values = jnp.broadcast_to(table[w : w + 1, r * LANES : (r + 1) * LANES], (8, LANES))
                found = jnp.take_along_axis(values, lo, axis=1, mode="promise_in_bounds")
                words[w] = jnp.where(hit, found, words[w])
        u = unpack(*words, jnp.take_along_axis(steps, lo, axis=1, mode="promise_in_bounds"))
        g = [grads[j, :, cols] for j in range(3)]

        def total(value):
            return jnp.sum(value, axis=0, keepdims=True)

        strain = [
            total(u[0] * g[0]),
            total(u[1] * g[1]),
            total(u[2] * g[2]),
            0.5 * total(u[1] * g[2] + u[2] * g[1]),
            0.5 * total(u[0] * g[2] + u[2] * g[0]),
            0.5 * total(u[0] * g[1] + u[1] * g[0]),
        ]
        lam = moduli[0:1, cols]
        mu = moduli[1:2, cols]
        volume = volumes[pl.ds(t, 1), :]
        spherical = lam * (strain[0] + strain[1] + strain[2])
        stress = [spherical + 2.0 * mu * strain[c] for c in range(3)]
        stress += [2.0 * mu * strain[c] for c in range(3, 6)]
        for k in range(4):
            hit = lane == replace[6, k] - lax.convert_element_type(t * LANES, f32)
            stress = [jnp.where(hit, replace[c, k], stress[c]) for c in range(6)]
        xx, yy, zz, yz, xz, xy = [
            jnp.broadcast_to(component * volume, (8, LANES)) for component in stress
        ]
        fx = xx * g[0] + xy * g[1] + xz * g[2]
        fy = xy * g[0] + yy * g[1] + yz * g[2]
        fz = xz * g[0] + yz * g[1] + zz * g[2]
        return node, fx, fy, fz

    def group(step):
        return tuple(forces_of(begin + step * unroll + i) for i in range(unroll))

    def add(carry):
        total = None
        for node, *forces in carry:
            part = scatter(node, forces)
            total = part if total is None else total + part
        sums[...] += total

    def body(step, carry):
        add(carry)
        return group(step)

    add(lax.fori_loop(1, (end - begin) // unroll, body, group(0)))


def macro_first_kernel(
    unroll, replace, disp, nm, grads, volumes, moduli, shared, sums, table, step, face_nodes
):
    for i in range(4):
        for half in range(2):
            cols = slice((2 * i + half) * LANES, (2 * i + half + 1) * LANES)
            face_nodes[i, 4 * half : 4 * half + 4, :] = shared[0, :, cols]
    pack_table(disp, table, step)
    sums[...] = jnp.zeros_like(sums)
    macro_tiles(0, SPLIT, unroll, replace, table, step, nm, grads, volumes, moduli, sums)


def face_lists(core, pool):
    return core, 2 + (pool & 1), 3 - (pool & 1), 1 - core


def macro_last_kernel(
    unroll,
    replace,
    core_index,
    pool_index,
    table,
    step,
    nm,
    grads,
    volumes,
    moduli,
    so_far,
    face_nodes,
    own,
    to_brick,
    to_odd,
    to_even,
    to_core,
    sums,
    faces,
):
    sums[...] = so_far[...]
    macro_tiles(SPLIT, 64, unroll, replace, table, step, nm, grads, volumes, moduli, sums)

    for c in range(3):
        at = 2 * c * HI
        own[c * HI : (c + 1) * HI, :] = sums[at : at + HI, :] + sums[at + HI : at + 2 * HI, :]

    for pair in range(4):
        first, second = 2 * pair, 2 * pair + 1
        node = face_nodes[pair]
        hi, lo = node >> 7, node & 127
        picked = [jnp.zeros((8, LANES), f32) for _ in range(3)]
        for r in range(72):
            hit = hi == r
            for c in range(3):
                at = c * HI + r // 2
                cols = slice(r % 2 * LANES, (r % 2 + 1) * LANES)
                values = jnp.broadcast_to(own[at : at + 1, cols], (8, LANES))
                found = jnp.take_along_axis(values, lo, axis=1, mode="promise_in_bounds")
                picked[c] = jnp.where(hit, found, picked[c])
        for c in range(3):
            for face in range(4):
                faces[face, c : c + 1, first * LANES : (first + 1) * LANES] = picked[c][face : face + 1]
                faces[face, c : c + 1, second * LANES : (second + 1) * LANES] = picked[c][
                    4 + face : 5 + face
                ]
    lists = face_lists(core_index[0], pool_index[0])
    for face, out in zip(lists, (to_brick, to_odd, to_even, to_core)):
        out[...] = faces[face]


def macro_first(*arguments):
    vmem = pl.BlockSpec(memory_space=VMEM)
    return pl.pallas_call(
        functools.partial(macro_first_kernel, UNROLL),
        out_shape=(
            jax.ShapeDtypeStruct((6 * HI, LO), f32),
            jax.ShapeDtypeStruct((2, 72 * LANES), jnp.int32),
            jax.ShapeDtypeStruct((1, LANES), f32),
            jax.ShapeDtypeStruct((4, 8, LANES), jnp.int32),
        ),
        in_specs=[pl.BlockSpec(memory_space=SMEM)] + [vmem] * 6,
        out_specs=(vmem,) * 4,
        compiler_params=pltpu.CompilerParams(vmem_limit_bytes=32 << 20),
        name="macro_first",
    )(*arguments)


def macro_last(*arguments):
    vmem = pl.BlockSpec(memory_space=VMEM)
    return pl.pallas_call(
        functools.partial(macro_last_kernel, UNROLL),
        out_shape=(
            jax.ShapeDtypeStruct((3 * HI, LO), f32),
        )
        + (jax.ShapeDtypeStruct((3, 1024), f32),) * 4,
        in_specs=[pl.BlockSpec(memory_space=SMEM)] * 3 + [vmem] * 8,
        out_specs=(vmem,) * 5,
        scratch_shapes=[VMEM((6 * HI, LO), f32), VMEM((4, 3, 1024), f32)],
        compiler_params=pltpu.CompilerParams(vmem_limit_bytes=32 << 20),
        name="macro_last",
    )(*arguments)


def assemble_kernel(
    core_index, pool_index, own, shared, r0, r1, r2, r3, external, mass, pieces, out, fields, joined, sem
):
    for i in range(TILES):
        for s in range(2):
            joined[s, :, i * LANES : (i + 1) * LANES] = pieces[i, s]
    copy = pltpu.make_async_copy(joined, fields, sem)
    copy.start()
    total = None
    for face, arrived in zip(face_lists(core_index[0], pool_index[0]), (r0, r1, r2, r3)):
        for part in range(4):
            cols = slice(part * LO, (part + 1) * LO)
            values = []
            for c in range(3):
                values += list(halves(arrived[c : c + 1, cols]))
            left, right = one_hot_sum(shared[0, pl.ds(face, 1), cols], values, LO)
            product = lax.dot_general(
                left, right, (((1,), (1,)), ((), ())), preferred_element_type=f32
            )
            total = product if total is None else total + product
    for c in range(3):
        at = 2 * c * HI
        whole = own[c * HI : (c + 1) * HI, :] + total[at : at + HI] + total[at + HI : at + 2 * HI]
        for r in range(36):
            out[c : c + 1, r * LO : (r + 1) * LO] = whole[r : r + 1]
    out[...] = (external[...] - out[...]) / mass[...]
    copy.wait()


def assemble(place, own, shared, arrived, external, mass, pieces):
    vmem = pl.BlockSpec(memory_space=VMEM)
    return pl.pallas_call(
        assemble_kernel,
        out_shape=(
            jax.ShapeDtypeStruct(external.shape, f32),
            jax.ShapeDtypeStruct((2, 8, NV), f32),
        ),
        in_specs=[pl.BlockSpec(memory_space=SMEM)] * 2 + [vmem] * 9,
        out_specs=(vmem, pl.BlockSpec(memory_space=pl.ANY)),
        scratch_shapes=[VMEM((2, 8, NV), f32), pltpu.SemaphoreType.DMA],
        compiler_params=pltpu.CompilerParams(vmem_limit_bytes=32 << 20),
        name="assemble",
    )(*place, own, shared, *arrived, external, mass, pieces)


def sort_kernel(pieces, out, order, places, sem):
    blocks = pieces.shape[0] // 9
    lane = lax.broadcasted_iota(jnp.int32, (blocks, LANES), 1)
    block = lax.broadcasted_iota(jnp.int32, (blocks, LANES), 0)
    hit = pieces[pl.ds(8, blocks, stride=9), :] == lane.astype(f32)
    order[0:1, :] = jnp.min(jnp.where(hit, block, blocks - 1), axis=0, keepdims=True)
    order[1:2, :] = jnp.max(jnp.where(hit, block, 0), axis=0, keepdims=True)
    copy = pltpu.make_async_copy(order, places, sem)
    copy.start()
    copy.wait()
    for b in range(out.shape[0]):
        for s in range(2):
            out[b, s] = pieces[pl.ds(9 * places[s, b], 8), :]


def sort_pieces(pieces, bricks):
    vmem = pl.BlockSpec(memory_space=VMEM)
    return pl.pallas_call(
        sort_kernel,
        out_shape=jax.ShapeDtypeStruct((bricks, 2, 8, LANES), f32),
        in_specs=[vmem],
        out_specs=vmem,
        scratch_shapes=[VMEM((8, LANES), jnp.int32), SMEM((8, LANES), jnp.int32), pltpu.SemaphoreType.DMA],
        compiler_params=pltpu.CompilerParams(vmem_limit_bytes=32 << 20),
        name="sort_pieces",
    )(pieces)


def shards(
    displacement,
    node_map,
    shape_grads,
    volumes,
    elastic_moduli,
    external_force,
    nodal_mass,
    shared_nodes,
    band_count,
    band_owner,
    band_element,
    micro_fields,
):
    bricks, pools = lax.axis_size(BRICK), lax.axis_size("pool")
    place = tuple(lax.axis_index(axis).astype(jnp.int32).reshape(1) for axis in ("core", "pool"))
    send, band_stress, replace = solve_cells(
        band_count,
        band_owner,
        band_element,
        displacement,
        node_map,
        shape_grads,
        micro_fields,
        jnp.asarray(green_table()),
        jnp.asarray(plane_tables()),
    )
    pieces = lax.all_to_all(
        send.reshape(bricks * pools, 1, 9 * LANES), BOTH, split_axis=0, concat_axis=0, tiled=True
    )
    dense = (node_map, shape_grads, volumes.reshape(64, LANES), elastic_moduli)
    so_far, table, step, face_nodes = macro_first(replace, displacement, *dense, shared_nodes)
    pieces, so_far = lax.optimization_barrier((pieces, so_far))
    sorted_pieces = sort_pieces(pieces.reshape(9 * bricks * pools, LANES), bricks)
    sorted_pieces, so_far = lax.optimization_barrier((sorted_pieces, so_far))
    mine = lax.all_to_all(sorted_pieces, BRICK, split_axis=0, concat_axis=0, tiled=True)
    own, *faces = macro_last(replace, *place, table, step, *dense, so_far, face_nodes)

    def swap(array, axis, size, first):
        steps = [(i, i + 1) for i in range(first, size - 1, 2)]
        return lax.ppermute(array, axis, steps + [(j, i) for i, j in steps])

    arrived = (
        swap(faces[0], BRICK, bricks, 1),
        swap(faces[1], "pool", pools, 1),
        swap(faces[2], "pool", pools, 0),
        swap(faces[3], "core", 2, 0),
    )
    acceleration, owned_fields = assemble(
        place, own, shared_nodes, arrived, external_force, nodal_mass.reshape(1, -1), mine
    )
    return (acceleration, band_stress.T, owned_fields)


def solution(mesh):
    bricks, pools = mesh.devices.shape
    split = jax.sharding.Mesh(
        mesh.devices.reshape(4, bricks // 8, 2, pools), ("row", "pair", "core", "pool")
    )
    placed = (
        P(None, BOTH),
        P(None, BOTH),
        P(None, None, BOTH),
        P(BOTH),
        P(None, BOTH),
        P(None, BOTH),
        P(BOTH),
        P(BOTH, None, None),
        P(BOTH),
        P(BOTH, None),
        P(BOTH, None),
        P(BOTH, None, None),
    )
    return jax.shard_map(
        shards,
        mesh=split,
        in_specs=placed,
        out_specs=(P(None, BOTH), P(None, BOTH), P(BOTH, None, None)),
        check_vma=False,
    )
```

```python
import functools
import math

import jax
import jax.numpy as jnp
import numpy as np
from jax import lax
from jax.experimental import pallas as pl
from jax.experimental.pallas import tpu as pltpu
from jax.sharding import PartitionSpec as P

G = 16
NV = 4096
ITERS = 2
LANES = 128
TILES = 32
HI = 48
LO = 256
STEPS = float((1 << 20) - 2)
OFFSET = 1 << 20
UNROLL = 4
SPLIT = 56
BRICK = ("row", "pair", "core")
BOTH = BRICK + ("pool",)
VMEM = pltpu.VMEM
SMEM = pltpu.SMEM
f32 = jnp.float32
bf16 = jnp.bfloat16

ref_lambda = 5.5
ref_shear = 5.5


def green_table():
    index = np.arange(G)

    def operator(ix, iy, iz):
        wave = [np.where(2 * m < G, m, m - G).astype(np.float64) for m in (ix, iy, iz)]
        kx, ky, kz = np.broadcast_arrays(wave[0], wave[1], wave[2])
        square = kx * kx + ky * ky + kz * kz
        safe = np.where(square > 0, square, 1.0)
        first = np.where(square > 0, 1.0 / (2.0 * ref_shear * safe), 0.0)
        factor = (ref_lambda + ref_shear) / (ref_shear * (ref_lambda + 2.0 * ref_shear))
        second = np.where(square > 0, factor / (safe * safe), 0.0)
        zero, one = np.zeros_like(kx), np.ones_like(kx)
        columns = []
        for j in range(6):
            xx, yy, zz, yz, xz, xy = [one if j == c else zero for c in range(6)]
            wx = xx * kx + xy * ky + xz * kz
            wy = xy * kx + yy * ky + yz * kz
            wz = xz * kx + yz * ky + zz * kz
            s = (wx * kx + wy * ky + wz * kz) * second
            columns.append(
                np.stack(
                    [
                        first * 2 * kx * wx - s * kx * kx,
                        first * 2 * ky * wy - s * ky * ky,
                        first * 2 * kz * wz - s * kz * kz,
                        first * (ky * wz + kz * wy) - s * ky * kz,
                        first * (kx * wz + kz * wx) - s * kx * kz,
                        first * (kx * wy + ky * wx) - s * kx * ky,
                        zero,
                        zero,
                    ]
                )
            )
        return np.stack(columns)

    ix, iy, iz = index[:, None, None], index[None, :, None], index[None, None, :]
    table = 0.5 * (operator(ix, iy, iz) + operator((-ix) % G, (-iy) % G, (-iz) % G)) / NV
    table = table.reshape(6, 8, G, G * G).transpose(2, 0, 1, 3)
    pairs, alone = half_plane()
    even, odd = np.concatenate([pairs, alone[:2]]), np.concatenate([pairs, alone[2:]])
    return np.stack([table[..., even], table[..., odd]]).astype(np.float32)


def half_plane():
    index = np.arange(G * G)
    mirror = (-(index // G)) % G * G + (-(index % G)) % G
    return index[index < mirror], index[index == mirror]


def plane_tables():
    pairs, alone = half_plane()
    plane = np.arange(G * G)

    def angle(k):
        turns = (plane[:, None] // G * (k // G)[None, :] + plane[:, None] % G * (k % G)[None, :]) % G
        return turns * (2 * np.pi / G)

    there = np.concatenate(
        [
            np.cos(angle(pairs)),
            np.cos(angle(alone[:2])),
            -np.sin(angle(pairs)),
            np.cos(angle(alone[2:])),
        ],
        axis=1,
    )
    weight = np.full((G * G, 1), 2.0)
    weight[[126, 127, 254, 255]] = 1.0
    parts = []
    for table in (there, weight * there.T):
        high = table.astype(np.float32).astype(bf16)
        parts += [high, (table - high.astype(np.float64)).astype(np.float32).astype(bf16)]
    return np.stack(parts)


def twiddle(value, power, sign):
    re, im = value
    power %= 16
    if power == 0:
        return re, im
    if power == 4:
        return (-im, re) if sign > 0 else (im, -re)
    if power == 8:
        return -re, -im
    if power == 12:
        return (im, -re) if sign > 0 else (-im, re)
    angle = sign * 2 * math.pi * power / 16
    c, s = math.cos(angle), math.sin(angle)
    if power % 4 == 2:
        h = abs(c)
        a = re if c > 0 else -re
        b = im if c > 0 else -im
        if c * s > 0:
            return (a - b) * h, (a + b) * h
        return (a + b) * h, (b - a) * h
    return re * c - im * s, re * s + im * c


def dft4(v, sign):
    (ar, ai), (br, bi), (cr, ci), (dr, di) = v
    pr, pi_ = ar + cr, ai + ci
    mr, mi = ar - cr, ai - ci
    qr, qi = br + dr, bi + di
    nr, ni = br - dr, bi - di
    if sign < 0:
        jr, ji = ni, -nr
    else:
        jr, ji = -ni, nr
    return [(pr + qr, pi_ + qi), (mr + jr, mi + ji), (pr - qr, pi_ - qi), (mr - jr, mi - ji)]


def dft16(values, sign):
    inner = []
    for n2 in range(4):
        inner.append(dft4([values[n2 + 4 * n1] for n1 in range(4)], sign))
    out = [None] * 16
    for k1 in range(4):
        column = dft4([twiddle(inner[n2][k1], n2 * k1, sign) for n2 in range(4)], sign)
        for k2 in range(4):
            out[k1 + 4 * k2] = column[k2]
    return out


def slab_stress(d, first_rows):
    wide = d.shape
    trace = d[0:1] + d[1:2] + d[2:3]
    lam_trace = jnp.broadcast_to(d[6:7] * trace, wide)
    twice = jnp.broadcast_to(2.0 * d[7:8], wide)
    return twice * d + jnp.where(first_rows, lam_trace, 0.0)


def plane_product(x, cmat, at):
    high = x.astype(bf16)
    low = (x - high.astype(f32)).astype(bf16)
    rows = x.shape[0]
    both = jnp.dot(jnp.concatenate([high, low], axis=0), cmat[at], preferred_element_type=f32)
    return both[:rows] + both[rows:] + jnp.dot(high, cmat[at + 1], preferred_element_type=f32)


def cells_kernel(
    count, owner, element, disp, nm, grads, micro, green, cmat, send, band_stress, replace, st, *work
):
    half_rows = 8 * G
    lane = lax.broadcasted_iota(jnp.int32, (8, LANES), 1)
    row = lax.broadcasted_iota(jnp.int32, (8, LANES), 0)
    row_wide = lax.broadcasted_iota(jnp.int32, (8, 2 * LANES), 0)
    first_rows = row_wide < 3

    targets = []
    for k in range(4):
        e = element[0, k]
        base = pl.multiple_of(e // LANES * LANES, LANES)
        at = lane == e % LANES

        def pick(tile):
            return jnp.sum(jnp.where(at, tile, 0.0), axis=1, keepdims=True)

        node = pick(nm[:, pl.ds(base, LANES)].astype(f32)).astype(jnp.int32)
        shape = [jnp.broadcast_to(pick(grads[j, :, pl.ds(base, LANES)]), (8, LANES)) for j in range(3)]
        node = jnp.broadcast_to(node, (8, LANES)) - lane
        found = [jnp.zeros((8, LANES), f32) for _ in range(3)]
        for r in range(72):
            hit = node == r * LANES
            for c in range(3):
                values = jnp.broadcast_to(disp[c : c + 1, r * LANES : (r + 1) * LANES], (8, LANES))
                found[c] = jnp.where(hit, values, found[c])
        u = [jnp.sum(found[c], axis=1, keepdims=True) for c in range(3)]

        def total(value):
            return jnp.sum(value, axis=0, keepdims=True)

        parts = [
            total(u[0] * shape[0]),
            total(u[1] * shape[1]),
            total(u[2] * shape[2]),
            0.5 * total(u[1] * shape[2] + u[2] * shape[1]),
            0.5 * total(u[0] * shape[2] + u[2] * shape[0]),
            0.5 * total(u[0] * shape[1] + u[1] * shape[0]),
        ]
        target = jnp.zeros((8, LANES), f32)
        for c in range(6):
            target = jnp.where(row == c, jnp.broadcast_to(parts[c], (8, LANES)), target)
        targets.append(target)

    def slab(k, x, iteration):
        if iteration == 0:
            return micro[k, :, 2 * LANES * x : 2 * LANES * (x + 1)]
        return st[k, 8 * x : 8 * x + 8, :]

    shifts = []
    for k in range(4):
        total = jnp.zeros((8, 2 * LANES), f32)
        for x in range(G):
            total = total + slab(k, x, 0)
        mean = jnp.sum(total, axis=1, keepdims=True) * (1.0 / NV)
        shift = jnp.where(row < 6, targets[k] - mean, 0.0)
        shifts.append(jnp.concatenate([shift, shift], axis=1))

    re_cols, im_cols = slice(0, LANES), slice(LANES, 2 * LANES)
    own_mirror = lane >= 126
    whole_mirror = lax.broadcasted_iota(jnp.int32, (half_rows, LANES), 1) >= 126
    for iteration in range(ITERS):
        for pair in range(2):
            plane, spectrum = work[2 * pair], work[2 * pair + 1]
            at = [[cell * half_rows + 8 * x for x in range(G)] for cell in range(2)]
            for cell in range(2):
                for x in range(G):
                    a = at[cell][x]
                    plane[a : a + 8, :] = slab_stress(slab(2 * pair + cell, x, iteration), first_rows)
            plane[...] = plane_product(plane[...], cmat, 0)
            for cell in range(2):
                values = []
                for x in range(G):
                    a = at[cell][x]
                    re, im = plane[a : a + 8, re_cols], plane[a : a + 8, im_cols]
                    if cell == 0:
                        other = at[1][x]
                        im = jnp.where(own_mirror, plane[other : other + 8, re_cols], im)
                    else:
                        other = at[0][x]
                        re = jnp.where(own_mirror, plane[other : other + 8, im_cols], re)
                    values.append((re, im))
                values = dft16(values, -1)
                for x in range(G):
                    a = at[cell][x]
                    spectrum[a : a + 8, re_cols] = values[x][0]
                    spectrum[a : a + 8, im_cols] = values[x][1]
            for cell in range(2):
                updates = []
                for x in range(G):
                    re = im = None
                    for j in range(6):
                        weight = green[cell, x, j]
                        a = at[cell][x] + j
                        tr = weight * jnp.broadcast_to(spectrum[a : a + 1, re_cols], (8, LANES))
                        ti = weight * jnp.broadcast_to(spectrum[a : a + 1, im_cols], (8, LANES))
                        re = tr if re is None else re + tr
                        im = ti if im is None else im + ti
                    updates.append((re, im))
                values = dft16(updates, 1)
                for x in range(G):
                    a = at[cell][x]
                    plane[a : a + 8, re_cols] = values[x][0]
                    plane[a : a + 8, im_cols] = values[x][1]
            first_im = plane[:half_rows, im_cols]
            second_re = plane[half_rows:, re_cols]
            plane[:half_rows, im_cols] = jnp.where(whole_mirror, second_re, first_im)
            plane[half_rows:, re_cols] = jnp.where(whole_mirror, first_im, second_re)
            update = plane_product(plane[...], cmat, 2)
            for cell in range(2):
                k = 2 * pair + cell
                for x in range(G):
                    a = at[cell][x]
                    value = slab(k, x, iteration) - update[a : a + 8, :]
                    if iteration == 0:
                        value = value + shifts[k]
                    st[k, 8 * x : 8 * x + 8, :] = value

    send[pl.ds(8, 4 * TILES, stride=9), :] = jnp.full((4 * TILES, LANES), -1.0, f32)
    result = jnp.zeros((8, LANES), f32)
    for k in range(4):
        live = k < count[0]
        total = jnp.zeros((8, 2 * LANES), f32)
        for x in range(G):
            total = total + slab_stress(st[k, 8 * x : 8 * x + 8, :], first_rows)
        mean = jnp.where(live, jnp.sum(total, axis=1, keepdims=True) * (1.0 / NV), 0.0)
        mean = jnp.broadcast_to(mean, (8, LANES))
        result = jnp.where(lane == k, mean, result)
        across = jnp.sum(jnp.where(lane == row, mean, 0.0), axis=0, keepdims=True)
        band_stress[k : k + 1, :] = across[:, 0:6]
        pool = owner[0, k] & 3

        @pl.when(live)
        def _():
            for i in range(TILES):
                x, part = i // 2, i % 2
                send[pl.ds(9 * (4 * i + pool), 8), :] = st[
                    k, 8 * x : 8 * x + 8, part * LANES : (part + 1) * LANES
                ]
            brick = (owner[0, k] >> 2).astype(f32)
            send[pl.ds(9 * pool + 8, TILES, stride=36), :] = jnp.full((TILES, LANES), brick, f32)

    for k in range(4):
        live_element = jnp.where(k < count[0], element[0, k], -1).astype(f32)
        result = jnp.where((lane == k) & (row == 6), live_element, result)
    replace[...] = result[:, 0:4]


def solve_cells(count, owner, element, disp, nm, grads, micro, green, cmat):
    return pl.pallas_call(
        cells_kernel,
        out_shape=(
            jax.ShapeDtypeStruct((36 * TILES, LANES), f32),
            jax.ShapeDtypeStruct((4, 6), f32),
            jax.ShapeDtypeStruct((8, 4), f32),
        ),
        in_specs=[pl.BlockSpec(memory_space=SMEM)] * 3 + [pl.BlockSpec(memory_space=VMEM)] * 6,
        out_specs=(pl.BlockSpec(memory_space=VMEM),) * 3,
        scratch_shapes=[
            VMEM((4, 8 * G, 2 * LANES), f32),
        ]
        + [VMEM((16 * G, 2 * LANES), f32)] * 4,
        compiler_params=pltpu.CompilerParams(vmem_limit_bytes=56 << 20),
        name="cells",
    )(count, owner, element, disp, nm, grads, micro, green, cmat)


def one_hot_sum(node, values, width):
    def spread(row, rows):
        return jnp.broadcast_to(jnp.broadcast_to(row, (16, width)).astype(bf16)[None], (rows // 16, 16, width)).reshape(
            rows, width
        )

    def index(rows):
        return lax.broadcasted_iota(jnp.int32, (rows, width), 0).astype(f32).astype(bf16)

    coarse = index(HI) == spread((node >> 8).astype(f32), HI)
    fine = index(LO) == spread((node & 255).astype(f32), LO)
    left = jnp.concatenate(
        [jnp.where(coarse, spread(v, HI), jnp.zeros((HI, width), bf16)) for v in values], axis=0
    )
    right = jnp.where(fine, jnp.ones((LO, width), bf16), jnp.zeros((LO, width), bf16))
    return left, right


def halves(value):
    high = value.astype(bf16).astype(f32)
    return high, value - high


def pack_table(disp, table, step):
    largest = jnp.zeros((3, LANES), f32)
    for r in range(72):
        largest = jnp.maximum(largest, jnp.abs(disp[:, r * LANES : (r + 1) * LANES]))
    largest = jnp.maximum(jnp.max(largest, axis=0, keepdims=True), 1e-30)
    step[...] = largest * (1.0 / STEPS)
    scale = jnp.broadcast_to(STEPS / largest, (3, LANES))
    for r in range(72):
        cols = slice(r * LANES, (r + 1) * LANES)
        level = jnp.floor(disp[:, cols] * scale + (OFFSET + 0.5)).astype(jnp.int32)
        last = level[2:3]
        parts = jnp.concatenate([(last & 0x7FF) << 21, (last >> 11) << 21], axis=0)
        table[:, cols] = level[0:2] | parts


def unpack(first, second, step):
    mask = (1 << 21) - 1
    last = lax.shift_right_logical(first, 21) | (lax.shift_right_logical(second, 21) << 11)
    return [(level - OFFSET).astype(f32) * step for level in (first & mask, second & mask, last)]


def macro_tiles(begin, end, unroll, replace, table, step_of, nm, grads, volumes, moduli, sums):
    lane = lax.broadcasted_iota(jnp.int32, (1, LANES), 1).astype(f32)
    steps = jnp.broadcast_to(step_of[...], (8, LANES))

    def scatter(node, forces):
        values = []
        for force in forces:
            values += list(halves(force))
        total = None
        for s in range(0, 8, 2):
            lefts, rights = [], []
            for q in (s, s + 1):
                left, right = one_hot_sum(node[q : q + 1], [v[q : q + 1] for v in values], LANES)
                lefts.append(left)
                rights.append(right)
            product = lax.dot_general(
                jnp.concatenate(lefts, axis=1),
                jnp.concatenate(rights, axis=1),
                (((1,), (1,)), ((), ())),
                preferred_element_type=f32,
            )
            total = product if total is None else total + product
        return total

    def forces_of(t):
        cols = pl.ds(pl.multiple_of(t * LANES, LANES), LANES)
        node = nm[:, cols]
        hi, lo = node >> 7, node & 127
        words = [jnp.zeros((8, LANES), jnp.int32) for _ in range(2)]
        for r in range(72):
            hit = hi == r
            for w in range(2):
                values = jnp.broadcast_to(table[w : w + 1, r * LANES : (r + 1) * LANES], (8, LANES))
                found = jnp.take_along_axis(values, lo, axis=1, mode="promise_in_bounds")
                words[w] = jnp.where(hit, found, words[w])
        u = unpack(*words, jnp.take_along_axis(steps, lo, axis=1, mode="promise_in_bounds"))
        g = [grads[j, :, cols] for j in range(3)]

        def total(value):
            return jnp.sum(value, axis=0, keepdims=True)

        strain = [
            total(u[0] * g[0]),
            total(u[1] * g[1]),
            total(u[2] * g[2]),
            0.5 * total(u[1] * g[2] + u[2] * g[1]),
            0.5 * total(u[0] * g[2] + u[2] * g[0]),
            0.5 * total(u[0] * g[1] + u[1] * g[0]),
        ]
        lam = moduli[0:1, cols]
        mu = moduli[1:2, cols]
        volume = volumes[pl.ds(t, 1), :]
        spherical = lam * (strain[0] + strain[1] + strain[2])
        stress = [spherical + 2.0 * mu * strain[c] for c in range(3)]
        stress += [2.0 * mu * strain[c] for c in range(3, 6)]
        for k in range(4):
            hit = lane == replace[6, k] - lax.convert_element_type(t * LANES, f32)
            stress = [jnp.where(hit, replace[c, k], stress[c]) for c in range(6)]
        xx, yy, zz, yz, xz, xy = [
            jnp.broadcast_to(component * volume, (8, LANES)) for component in stress
        ]
        fx = xx * g[0] + xy * g[1] + xz * g[2]
        fy = xy * g[0] + yy * g[1] + yz * g[2]
        fz = xz * g[0] + yz * g[1] + zz * g[2]
        return node, fx, fy, fz

    def group(step):
        return tuple(forces_of(begin + step * unroll + i) for i in range(unroll))

    def add(carry):
        total = None
        for node, *forces in carry:
            part = scatter(node, forces)
            total = part if total is None else total + part
        sums[...] += total

    def body(step, carry):
        add(carry)
        return group(step)

    add(lax.fori_loop(1, (end - begin) // unroll, body, group(0)))


def macro_first_kernel(
    unroll, replace, disp, nm, grads, volumes, moduli, shared, sums, table, step, face_nodes
):
    for i in range(4):
        for half in range(2):
            cols = slice((2 * i + half) * LANES, (2 * i + half + 1) * LANES)
            face_nodes[i, 4 * half : 4 * half + 4, :] = shared[0, :, cols]
    pack_table(disp, table, step)
    sums[...] = jnp.zeros_like(sums)
    macro_tiles(0, SPLIT, unroll, replace, table, step, nm, grads, volumes, moduli, sums)


def face_lists(core, pool):
    return 3 - (pool & 1), 2 + (pool & 1), core, 1 - core


def macro_last_kernel(
    unroll,
    replace,
    core_index,
    pool_index,
    table,
    step,
    nm,
    grads,
    volumes,
    moduli,
    so_far,
    face_nodes,
    own,
    to_even,
    to_odd,
    to_brick,
    to_core,
    sums,
    faces,
):
    sums[...] = so_far[...]
    macro_tiles(SPLIT, 64, unroll, replace, table, step, nm, grads, volumes, moduli, sums)

    for c in range(3):
        at = 2 * c * HI
        own[c * HI : (c + 1) * HI, :] = sums[at : at + HI, :] + sums[at + HI : at + 2 * HI, :]

    for pair in range(4):
        first, second = 2 * pair, 2 * pair + 1
        node = face_nodes[pair]
        hi, lo = node >> 7, node & 127
        picked = [jnp.zeros((8, LANES), f32) for _ in range(3)]
        for r in range(72):
            hit = hi == r
            for c in range(3):
                at = c * HI + r // 2
                cols = slice(r % 2 * LANES, (r % 2 + 1) * LANES)
                values = jnp.broadcast_to(own[at : at + 1, cols], (8, LANES))
                found = jnp.take_along_axis(values, lo, axis=1, mode="promise_in_bounds")
                picked[c] = jnp.where(hit, found, picked[c])
        for c in range(3):
            for face in range(4):
                faces[face, c : c + 1, first * LANES : (first + 1) * LANES] = picked[c][face : face + 1]
                faces[face, c : c + 1, second * LANES : (second + 1) * LANES] = picked[c][
                    4 + face : 5 + face
                ]
    lists = face_lists(core_index[0], pool_index[0])
    for face, out in zip(lists, (to_even, to_odd, to_brick, to_core)):
        out[...] = faces[face]


def macro_first(*arguments):
    vmem = pl.BlockSpec(memory_space=VMEM)
    return pl.pallas_call(
        functools.partial(macro_first_kernel, UNROLL),
        out_shape=(
            jax.ShapeDtypeStruct((6 * HI, LO), f32),
            jax.ShapeDtypeStruct((2, 72 * LANES), jnp.int32),
            jax.ShapeDtypeStruct((1, LANES), f32),
            jax.ShapeDtypeStruct((4, 8, LANES), jnp.int32),
        ),
        in_specs=[pl.BlockSpec(memory_space=SMEM)] + [vmem] * 6,
        out_specs=(vmem,) * 4,
        compiler_params=pltpu.CompilerParams(vmem_limit_bytes=32 << 20),
        name="macro_first",
    )(*arguments)


def macro_last(*arguments):
    vmem = pl.BlockSpec(memory_space=VMEM)
    return pl.pallas_call(
        functools.partial(macro_last_kernel, UNROLL),
        out_shape=(
            jax.ShapeDtypeStruct((3 * HI, LO), f32),
        )
        + (jax.ShapeDtypeStruct((3, 1024), f32),) * 4,
        in_specs=[pl.BlockSpec(memory_space=SMEM)] * 3 + [vmem] * 8,
        out_specs=(vmem,) * 5,
        scratch_shapes=[VMEM((6 * HI, LO), f32), VMEM((4, 3, 1024), f32)],
        compiler_params=pltpu.CompilerParams(vmem_limit_bytes=32 << 20),
        name="macro_last",
    )(*arguments)


def assemble_kernel(
    core_index, pool_index, own, shared, r0, r1, r2, r3, external, mass, pieces, out, fields, joined, sem
):
    for i in range(TILES):
        for s in range(2):
            joined[s, :, i * LANES : (i + 1) * LANES] = pieces[i, s]
    copy = pltpu.make_async_copy(joined, fields, sem)
    copy.start()
    total = None
    for face, arrived in zip(face_lists(core_index[0], pool_index[0]), (r0, r1, r2, r3)):
        for part in range(4):
            cols = slice(part * LO, (part + 1) * LO)
            values = []
            for c in range(3):
                values += list(halves(arrived[c : c + 1, cols]))
            left, right = one_hot_sum(shared[0, pl.ds(face, 1), cols], values, LO)
            product = lax.dot_general(
                left, right, (((1,), (1,)), ((), ())), preferred_element_type=f32
            )
            total = product if total is None else total + product
    for c in range(3):
        at = 2 * c * HI
        whole = own[c * HI : (c + 1) * HI, :] + total[at : at + HI] + total[at + HI : at + 2 * HI]
        for r in range(36):
            out[c : c + 1, r * LO : (r + 1) * LO] = whole[r : r + 1]
    out[...] = (external[...] - out[...]) / mass[...]
    copy.wait()


def assemble(place, own, shared, arrived, external, mass, pieces):
    vmem = pl.BlockSpec(memory_space=VMEM)
    return pl.pallas_call(
        assemble_kernel,
        out_shape=(
            jax.ShapeDtypeStruct(external.shape, f32),
            jax.ShapeDtypeStruct((2, 8, NV), f32),
        ),
        in_specs=[pl.BlockSpec(memory_space=SMEM)] * 2 + [vmem] * 9,
        out_specs=(vmem, pl.BlockSpec(memory_space=pl.ANY)),
        scratch_shapes=[VMEM((2, 8, NV), f32), pltpu.SemaphoreType.DMA],
        compiler_params=pltpu.CompilerParams(vmem_limit_bytes=32 << 20),
        name="assemble",
    )(*place, own, shared, *arrived, external, mass, pieces)


def sort_kernel(pieces, out, order, places, sem):
    blocks = pieces.shape[0] // 9
    lane = lax.broadcasted_iota(jnp.int32, (blocks, LANES), 1)
    block = lax.broadcasted_iota(jnp.int32, (blocks, LANES), 0)
    hit = pieces[pl.ds(8, blocks, stride=9), :] == lane.astype(f32)
    order[0:1, :] = jnp.min(jnp.where(hit, block, blocks - 1), axis=0, keepdims=True)
    order[1:2, :] = jnp.max(jnp.where(hit, block, 0), axis=0, keepdims=True)
    copy = pltpu.make_async_copy(order, places, sem)
    copy.start()
    copy.wait()
    for b in range(out.shape[0]):
        for s in range(2):
            out[b, s] = pieces[pl.ds(9 * places[s, b], 8), :]


def sort_pieces(pieces, bricks):
    vmem = pl.BlockSpec(memory_space=VMEM)
    return pl.pallas_call(
        sort_kernel,
        out_shape=jax.ShapeDtypeStruct((bricks, 2, 8, LANES), f32),
        in_specs=[vmem],
        out_specs=vmem,
        scratch_shapes=[VMEM((8, LANES), jnp.int32), SMEM((8, LANES), jnp.int32), pltpu.SemaphoreType.DMA],
        compiler_params=pltpu.CompilerParams(vmem_limit_bytes=32 << 20),
        name="sort_pieces",
    )(pieces)


def shards(
    displacement,
    node_map,
    shape_grads,
    volumes,
    elastic_moduli,
    external_force,
    nodal_mass,
    shared_nodes,
    band_count,
    band_owner,
    band_element,
    micro_fields,
):
    bricks, pools = lax.axis_size(BRICK), lax.axis_size("pool")
    place = tuple(lax.axis_index(axis).astype(jnp.int32).reshape(1) for axis in ("core", "pool"))
    send, band_stress, replace = solve_cells(
        band_count,
        band_owner,
        band_element,
        displacement,
        node_map,
        shape_grads,
        micro_fields,
        jnp.asarray(green_table()),
        jnp.asarray(plane_tables()),
    )
    pieces = lax.all_to_all(
        send.reshape(bricks * pools, 1, 9 * LANES), BOTH, split_axis=0, concat_axis=0, tiled=True
    )
    dense = (node_map, shape_grads, volumes.reshape(64, LANES), elastic_moduli)
    so_far, table, step, face_nodes = macro_first(replace, displacement, *dense, shared_nodes)
    pieces, so_far = lax.optimization_barrier((pieces, so_far))
    sorted_pieces = sort_pieces(pieces.reshape(9 * bricks * pools, LANES), bricks)
    sorted_pieces, so_far = lax.optimization_barrier((sorted_pieces, so_far))
    mine = lax.all_to_all(sorted_pieces, BRICK, split_axis=0, concat_axis=0, tiled=True)
    own, *faces = macro_last(replace, *place, table, step, *dense, so_far, face_nodes)

    def swap(array, axis, size, first):
        steps = [(i, i + 1) for i in range(first, size - 1, 2)]
        return lax.ppermute(array, axis, steps + [(j, i) for i, j in steps])

    arrived = (
        swap(faces[0], "pool", pools, 0),
        swap(faces[1], "pool", pools, 1),
        swap(faces[2], BRICK, bricks, 1),
        swap(faces[3], "core", 2, 0),
    )
    acceleration, owned_fields = assemble(
        place, own, shared_nodes, arrived, external_force, nodal_mass.reshape(1, -1), mine
    )
    return (acceleration, band_stress.T, owned_fields)


def solution(mesh):
    bricks, pools = mesh.devices.shape
    split = jax.sharding.Mesh(
        mesh.devices.reshape(4, bricks // 8, 2, pools), ("row", "pair", "core", "pool")
    )
    placed = (
        P(None, BOTH),
        P(None, BOTH),
        P(None, None, BOTH),
        P(BOTH),
        P(None, BOTH),
        P(None, BOTH),
        P(BOTH),
        P(BOTH, None, None),
        P(BOTH),
        P(BOTH, None),
        P(BOTH, None),
        P(BOTH, None, None),
    )
    return jax.shard_map(
        shards,
        mesh=split,
        in_specs=placed,
        out_specs=(P(None, BOTH), P(None, BOTH), P(BOTH, None, None)),
        check_vma=False,
    )
```
